512 devices in a mesh: stn: 64 (over z, x_hi, core), tm: 8 (over x_lo, y).
Axes of the slice: x: 4 (x_hi: 2, x_lo: 2; x = x_hi * 2 + x_lo), y: 4, z: 16, core: 2. Of those that a mesh axis runs over, the one named last changes fastest.
Arguments:
- samples: bfloat16 [2, 512, 491520], P(None, 'stn', 'tm'), may hold values from -6 to 6
- taps: bfloat16 [16, 4096], replicated, may hold values from -1.5 to 1.5
- scales: int32 [512, 2048], P('stn'), may hold values from 1 to 8
Outputs:
- visibilities: bfloat16 [2048, 512, 512], P(('stn', 'tm'))
The draws below stay inside these ranges and needn't reach their ends.
Inputs may be any that keep to these rules, and one draw needn't show every extreme that they name: scales are whole numbers.
All inputs are finite; a program needn't handle non-finite values.
Results may differ from the reference program's by a relative error of at most 0.0041.
Values may be sent and summed in bfloat16 or wider, within the bound.
No kernel may reach another device: no remote copies, remote signals or barrier semaphores. Data moves between devices by JAX's collectives and lax.ppermute only.
A program may use at most 128 MiB of HBM per device.

```python
import math
import jax
import jax.numpy as jnp
from jax import lax

STN_DEV = 4
FFTLEN = 4096
TAPS = 16
INPUTS = 512
FRAMES = 120
SAMPLES = 491520
BAND = 2048
N_STN = 64


def plant(array, rng, smallest, high):
    longest = array.shape.index(max(array.shape))
    spots = []
    for shift in (0, 1):
        where = [jax.random.randint(jax.random.fold_in(rng, axis), (), 0, length) for axis, length in enumerate(array.shape)]
        where[longest] = (where[longest] + shift) % array.shape[longest]
        spots.append(tuple(where))
    return array.at[spots[0]].set(smallest).at[spots[1]].set(high)


def block_levels(key, extent, split, low, largest):
    gain = 1.0
    for dim, blocks in split:
        draws = jax.random.uniform(jax.random.fold_in(jax.random.fold_in(key, 6), dim), (blocks,), jnp.float32, low / len(split), largest / len(split))
        gain = gain * jnp.repeat(jnp.exp(draws), extent[dim] // blocks).reshape((-1,) + (1,) * (len(extent) - 1 - dim))
    return gain


def scatter_about(own_key, shape, deviation, bound, pieces=(), kind=jnp.bfloat16):
    values = deviation * jax.random.normal(own_key, shape, jnp.float32)
    if pieces:
        values = values * block_levels(own_key, shape, pieces, -0.22, 0.18)
    return jnp.clip(values, -bound, bound).astype(kind)


def setup_inputs(seed: int = 0) -> dict:
    splits = jax.random.split(jax.random.key(seed), 4)
    return {
        "samples": scatter_about(splits[0], (2, INPUTS, SAMPLES), 1.0, 6.0, ((1, 64), (2, 8))),
        "taps": scatter_about(splits[1], (TAPS, FFTLEN), TAPS ** -0.5, 1.5),
        "scales": plant(jax.random.randint(splits[2], (INPUTS, BAND), 1, 9), jax.random.fold_in(splits[2], 1), 1, 8).astype(jnp.int32),
    }


def cos_sin(row_index, col_index, modulus):
    product = row_index[:, None] * col_index[None, :] % modulus
    angles = product.astype(jnp.float32) * (2.0 * math.pi / modulus)
    return (jnp.cos(angles), jnp.sin(angles))

def factor_length(length):
    outer_size = 1
    for divisor in range(1, math.isqrt(length) + 1):
        if length % divisor == 0:
            outer_size = divisor
    return outer_size

def band_transform(real_rows, imag_rows, band_size):
    length = real_rows.shape[1]
    outer_size = factor_length(length)
    inner_size = length // outer_size
    highest = lax.Precision.HIGHEST
    first_real = real_rows.reshape(-1, outer_size, inner_size)
    first_imag = imag_rows.reshape(-1, outer_size, inner_size)
    outer_index = jnp.arange(outer_size, dtype=jnp.int32)
    inner_index = jnp.arange(inner_size, dtype=jnp.int32)
    cos_outer, sin_outer = cos_sin(outer_index, outer_index, outer_size)
    mixed_real = jnp.einsum('rnq,nk->rkq', first_real, cos_outer, precision=highest, preferred_element_type=jnp.float32)
    mixed_real = mixed_real + jnp.einsum('rnq,nk->rkq', first_imag, sin_outer, precision=highest, preferred_element_type=jnp.float32)
    mixed_imag = jnp.einsum('rnq,nk->rkq', first_imag, cos_outer, precision=highest, preferred_element_type=jnp.float32)
    mixed_imag = mixed_imag - jnp.einsum('rnq,nk->rkq', first_real, sin_outer, precision=highest, preferred_element_type=jnp.float32)
    cos_twist, sin_twist = cos_sin(outer_index, inner_index, length)
    twisted_real = mixed_real * cos_twist + mixed_imag * sin_twist
    twisted_imag = mixed_imag * cos_twist - mixed_real * sin_twist
    offset = (length - band_size) // 2
    low_col = offset // outer_size
    high_col = -(-(offset + band_size) // outer_size)
    kept = high_col - low_col
    cos_inner, sin_inner = cos_sin(inner_index, inner_index, inner_size)
    cos_inner = cos_inner[:, low_col:high_col]
    sin_inner = sin_inner[:, low_col:high_col]
    final_real = jnp.einsum('rkq,qm->rmk', twisted_real, cos_inner, precision=highest, preferred_element_type=jnp.float32)
    final_real = final_real + jnp.einsum('rkq,qm->rmk', twisted_imag, sin_inner, precision=highest, preferred_element_type=jnp.float32)
    final_imag = jnp.einsum('rkq,qm->rmk', twisted_imag, cos_inner, precision=highest, preferred_element_type=jnp.float32)
    final_imag = final_imag - jnp.einsum('rkq,qm->rmk', twisted_real, sin_inner, precision=highest, preferred_element_type=jnp.float32)
    start = offset - low_col * outer_size
    rescale = 1.0 / math.sqrt(length)
    final_real = final_real.reshape(-1, kept * outer_size)[:, start:start + band_size] * rescale
    final_imag = final_imag.reshape(-1, kept * outer_size)[:, start:start + band_size] * rescale
    return (final_real, final_imag)

def reference(samples, taps, scales):
    history = TAPS - 1
    group_size = 2 * STN_DEV
    tap_values = taps.astype(jnp.float32)

    def one_group(group_index):
        first_input = (group_index * group_size).astype(jnp.int32)
        voltages = lax.dynamic_slice_in_dim(samples, first_input, group_size, 1)
        voltages = voltages.reshape(2, group_size, FRAMES, FFTLEN)
        padded = jnp.concatenate([jnp.zeros((2, group_size, history, FFTLEN), samples.dtype), voltages], axis=2)
        filtered = jnp.zeros((2, group_size, FRAMES, FFTLEN), jnp.float32)
        for tap_index in range(TAPS):
            filtered = filtered + tap_values[tap_index] * padded[:, :, tap_index:tap_index + FRAMES].astype(jnp.float32)
        spec_real, spec_imag = band_transform(filtered[0].reshape(group_size * FRAMES, FFTLEN), filtered[1].reshape(group_size * FRAMES, FFTLEN), BAND)
        factor = lax.dynamic_slice_in_dim(scales, first_input, group_size, 0).astype(jnp.float32) * 16.0
        factor = factor[:, None, :]
        quant_real = jnp.clip(spec_real.reshape(group_size, FRAMES, BAND) * factor, -127.0, 127.0).astype(jnp.bfloat16)
        quant_imag = jnp.clip(spec_imag.reshape(group_size, FRAMES, BAND) * factor, -127.0, 127.0).astype(jnp.bfloat16)
        stacked = jnp.concatenate([quant_real, quant_imag], axis=1)
        return jnp.transpose(stacked, (2, 0, 1))
    quantized = lax.map(one_group, jnp.arange(N_STN, dtype=jnp.int32))
    quantized = jnp.transpose(quantized, (1, 0, 2, 3)).reshape(BAND, INPUTS, 2 * FRAMES)
    positions = jnp.arange(INPUTS, dtype=jnp.int32)
    lower_mask = positions[:, None] >= positions[None, :]
    normalizer = 1.0 / (2.0 * FRAMES * FFTLEN)

    def one_channel(channel):
        joined = lax.dynamic_index_in_dim(quantized, channel, 0, keepdims=False)
        swapped = jnp.concatenate([joined[:, FRAMES:], -joined[:, :FRAMES]], axis=1)
        real_out = jnp.dot(joined, joined.T, preferred_element_type=jnp.float32)
        imag_out = jnp.dot(swapped, joined.T, preferred_element_type=jnp.float32)
        return (jnp.where(lower_mask, real_out, imag_out) * normalizer).astype(jnp.bfloat16)
    return lax.map(one_channel, jnp.arange(BAND, dtype=jnp.int32))
```

```python
import functools
import math

import jax
import jax.numpy as jnp
import numpy as np
from jax import lax
from jax.experimental import pallas as pl
from jax.experimental.pallas import tpu as pltpu
from jax.sharding import PartitionSpec as P

LANES = 128
RADIX = 16
FINE = 256
KEPT = 128
SLOT = 16
VMEM_LIMIT = 56 * 2**20


def second_table():
    fine = np.arange(FINE)
    outputs = np.arange(KEPT) + (FINE - KEPT) // 2
    angle = 2.0 * np.pi * ((outputs[:, None] * fine[None, :]) % FINE) / FINE
    cosine, sine = np.cos(angle), np.sin(angle)
    return np.block([[cosine, sine], [-sine, cosine]])


def twist_table():
    angle = 2.0 * np.pi * (np.arange(RADIX)[:, None] * np.arange(FINE)[None, :]) / (RADIX * FINE)
    return np.stack([np.cos(angle), -np.sin(angle)]).astype(np.float32)


def add(a, b):
    return (a[0] + b[0], a[1] + b[1])


def sub(a, b):
    return (a[0] - b[0], a[1] - b[1])


def turn(a):
    return (a[1], -a[0])


def four(a, b, c, d):
    even, odd = add(a, c), sub(a, c)
    both, rest = add(b, d), turn(sub(b, d))
    return (add(even, both), add(odd, rest), sub(even, both), sub(odd, rest))


def times_root(a, power):
    if power == 0:
        return a
    if power == 4:
        return turn(a)
    half = math.sqrt(0.5)
    if power == 2:
        return ((a[0] + a[1]) * half, (a[1] - a[0]) * half)
    if power == 6:
        return ((a[1] - a[0]) * half, -(a[0] + a[1]) * half)
    cosine, sine = math.cos(2 * math.pi * power / 16), math.sin(2 * math.pi * power / 16)
    return (a[0] * cosine + a[1] * sine, a[1] * cosine - a[0] * sine)


def sixteen(points):
    columns = [four(points[b], points[4 + b], points[8 + b], points[12 + b]) for b in range(4)]
    out = [None] * 16
    for low in range(4):
        mixed = four(*[times_root(columns[b][low], b * low) for b in range(4)])
        for high in range(4):
            out[low + 4 * high] = mixed[high]
    return out


def channelize_kernel(
    frames, own_ref, halo_ref, taps_ref, twist_ref, table_ref, factor_ref, out_ref, filt, rows, words
):
    length = RADIX * FINE
    tap_count = taps_ref.shape[0]
    history = tap_count - 1

    def filter_chunk(chunk, _):
        taps = [
            jnp.broadcast_to(taps_ref[pl.ds(p, 1), pl.ds(pl.multiple_of(chunk * LANES, LANES), LANES)], (8, LANES))
            for p in range(tap_count)
        ]
        for comp in range(2):
            sums = [None] * frames
            for v in range(history + frames):
                ref, u = (halo_ref, v) if v < history else (own_ref, v - history)
                at = pl.multiple_of(u * length + chunk * LANES, LANES)
                block = ref[comp, :, pl.ds(at, LANES)].astype(jnp.float32)
                for f in range(max(0, v - history), min(frames, v + 1)):
                    term = taps[v - f] * block
                    sums[f] = term if sums[f] is None else sums[f] + term
            for f in range(frames):
                filt[comp, chunk, f] = sums[f]
        return 0

    lax.fori_loop(0, length // LANES, filter_chunk, 0)

    rows[...] = jnp.zeros_like(rows)

    def first_transform(f, _):
        for half in range(2):
            points = [(filt[0, 2 * n + half, f], filt[1, 2 * n + half, f]) for n in range(RADIX)]
            mixed = sixteen(points)
            for k1 in range(RADIX):
                real, imag = mixed[k1]
                if k1:
                    cosine = twist_ref[0, pl.ds(k1, 1), pl.ds(half * LANES, LANES)]
                    sine = twist_ref[1, pl.ds(k1, 1), pl.ds(half * LANES, LANES)]
                    real, imag = real * cosine - imag * sine, imag * cosine + real * sine
                start = (k1 // 4) * (8 * 4 * SLOT) + (k1 % 4) * SLOT + f
                rows[half, pl.ds(start, 8, stride=4 * SLOT), :] = real
                rows[2 + half, pl.ds(start, 8, stride=4 * SLOT), :] = imag
        return 0

    lax.fori_loop(0, frames, first_transform, 0)

    low_lanes = lax.broadcasted_iota(jnp.int32, (KEPT, LANES), 1) < LANES // 2

    def second_transform(group, _):
        span = pl.ds(pl.multiple_of(group * 256, 256), 256)
        block = jnp.concatenate([rows[q, span, :] for q in range(4)], axis=1)
        high = block.astype(jnp.bfloat16)
        low = (block - high.astype(jnp.float32)).astype(jnp.bfloat16)
        contract = (((1,), (1,)), ((), ()))
        both = lax.dot_general(table_ref[...], high, contract, preferred_element_type=jnp.float32)
        rest = lax.dot_general(table_ref[: 2 * KEPT], low, contract, preferred_element_type=jnp.float32)
        total = both[: 2 * KEPT] + both[2 * KEPT :] + rest
        for pair in range(2):
            real = total[:KEPT, pair * LANES : (pair + 1) * LANES]
            imag = total[KEPT:, pair * LANES : (pair + 1) * LANES]
            first = jnp.where(low_lanes, real, pltpu.roll(imag, LANES // 2, 1))
            second = jnp.where(low_lanes, pltpu.roll(real, LANES // 2, 1), imag)
            at = group * 4 + pair * 2
            words[pl.ds(at, KEPT, stride=32), :] = first
            words[pl.ds(at + 1, KEPT, stride=32), :] = second
        return 0

    lax.fori_loop(0, rows.shape[1] // 256, second_transform, 0)

    def requantize(step, _):
        span = pl.ds(pl.multiple_of(step * 256, 256), 256)
        values = words[span, :] * factor_ref[span, :].astype(jnp.float32)
        out_ref[span, :] = jnp.clip(values, -127.0, 127.0).astype(jnp.bfloat16)
        return 0

    lax.fori_loop(0, words.shape[0] // 256, requantize, 0)


def channelize(own, halo, taps, factor):
    inputs, frames = own.shape[1], own.shape[2] // taps.shape[1]
    table = second_table()
    high = table.astype(jnp.bfloat16)
    low = (table - high.astype(np.float64)).astype(jnp.bfloat16)
    vmem = pl.BlockSpec(memory_space=pltpu.VMEM)
    messages = KEPT * 4 * inputs
    return pl.pallas_call(
        functools.partial(channelize_kernel, frames),
        out_shape=jax.ShapeDtypeStruct((messages, LANES), jnp.bfloat16),
        in_specs=[vmem] * 6,
        out_specs=vmem,
        scratch_shapes=[
            pltpu.VMEM((2, RADIX * FINE // LANES, frames, inputs, LANES), jnp.float32),
            pltpu.VMEM((4, 4 * inputs * 4 * SLOT, LANES), jnp.float32),
            pltpu.VMEM((messages, LANES), jnp.float32),
        ],
        compiler_params=pltpu.CompilerParams(vmem_limit_bytes=VMEM_LIMIT),
        name="channelize",
    )(own, halo, taps.astype(jnp.float32), twist_table(), jnp.concatenate([high, low]), factor)


def correlate_kernel(normalizer, words_ref, out_ref, joined, swapped):
    channel = pl.program_id(0)
    size = joined.shape[0]
    lane = lax.broadcasted_iota(jnp.int32, (size, LANES), 1)

    @pl.when(channel == 0)
    def _():
        sign = jnp.where(lane < LANES // 2, 1.0, -1.0)
        for t in range(8):
            block = words_ref[:, t].astype(jnp.float32).reshape(size, LANES)
            joined[:, t * LANES : (t + 1) * LANES] = block.astype(jnp.bfloat16)
            other = pltpu.roll(block, LANES // 2, 1) * sign
            swapped[:, t * LANES : (t + 1) * LANES] = other.astype(jnp.bfloat16)

    ours = (lane // SLOT) % 4 == channel
    chosen = jnp.concatenate([ours] * 8, axis=1)
    zero = jnp.zeros((), jnp.bfloat16)
    real_left = jnp.where(chosen, joined[...], zero)
    imag_left = jnp.where(chosen, swapped[...], zero)
    half = size // 2

    def product(left, right):
        return lax.dot_general(
            left, right, (((1,), (1,)), ((), ())), preferred_element_type=jnp.float32
        )

    first, second = joined[:half], joined[half:]
    lower = lax.broadcasted_iota(jnp.int32, (half, half), 0) >= lax.broadcasted_iota(
        jnp.int32, (half, half), 1
    )

    def finish(values):
        return (values * normalizer).astype(jnp.bfloat16)

    out_ref[0, :half, :half] = finish(
        jnp.where(lower, product(real_left[:half], first), product(imag_left[:half], first))
    )
    out_ref[0, half:, :half] = finish(product(real_left[half:], first))
    out_ref[0, :half, half:] = finish(product(imag_left[:half], second))
    out_ref[0, half:, half:] = finish(
        jnp.where(lower, product(real_left[half:], second), product(imag_left[half:], second))
    )


def correlate(words, normalizer):
    stations, _, inputs, _ = words.shape
    size = stations * inputs
    return pl.pallas_call(
        functools.partial(correlate_kernel, normalizer),
        grid=(4,),
        out_shape=jax.ShapeDtypeStruct((4, size, size), jnp.bfloat16),
        in_specs=[pl.BlockSpec(words.shape, lambda c: (0, 0, 0, 0))],
        out_specs=pl.BlockSpec((1, size, size), lambda c: (c, 0, 0)),
        scratch_shapes=[
            pltpu.VMEM((size, 8 * LANES), jnp.bfloat16),
            pltpu.VMEM((size, 8 * LANES), jnp.bfloat16),
        ],
        compiler_params=pltpu.CompilerParams(vmem_limit_bytes=VMEM_LIMIT),
        name="correlate",
    )(words)


def message_factor(scales, rescale):
    inputs, band = scales.shape
    factor = (scales.astype(jnp.float32) * rescale).astype(jnp.bfloat16)
    factor = jnp.transpose(factor.reshape(inputs, band // 4, 4), (1, 0, 2))
    factor = jnp.broadcast_to(factor[:, :, None, :, None], (band // 4, inputs, 2, 4, SLOT))
    return factor.reshape(band // 4 * inputs, 8 * SLOT)


def body(samples, taps, scales):
    length = taps.shape[1]
    inputs = samples.shape[1]
    frames = samples.shape[2] // length
    stations, times = lax.axis_size("stn"), lax.axis_size("tm")
    halo = lax.ppermute(samples, "tm", [(i, i + 1) for i in range(times - 1)])
    factor = message_factor(scales, 16.0 / math.sqrt(length))
    words = channelize(samples, halo, taps, factor)
    words = words.reshape(stations * times, inputs, LANES)
    words = lax.all_to_all(words, ("stn", "tm"), split_axis=0, concat_axis=0, tiled=True)
    words = words.reshape(stations, times, inputs, LANES)
    return correlate(words, 1.0 / (2.0 * frames * times * length))


def solution(mesh):
    placed = (P(None, "stn", "tm"), P(), P("stn", None))
    return jax.shard_map(
        body, mesh=mesh, in_specs=placed, out_specs=P(("stn", "tm"), None, None), check_vma=False
    )
```

```python
import functools
import math

import jax
import jax.numpy as jnp
import numpy as np
from jax import lax
from jax.experimental import pallas as pl
from jax.experimental.pallas import tpu as pltpu
from jax.sharding import PartitionSpec as P

LANES = 128
RADIX = 16
FINE = 256
KEPT = 128
SLOT = 16
PAD = 1
VMEM_LIMIT = 56 * 2**20


def second_table():
    fine = np.arange(FINE)
    outputs = np.arange(KEPT) + (FINE - KEPT) // 2
    angle = 2.0 * np.pi * ((outputs[:, None] * fine[None, :]) % FINE) / FINE
    cosine, sine = np.cos(angle), np.sin(angle)
    return np.block([[cosine, sine], [-sine, cosine]]).T


def twist_table():
    angle = 2.0 * np.pi * (np.arange(RADIX)[:, None] * np.arange(FINE)[None, :]) / (RADIX * FINE)
    return np.stack([np.cos(angle), -np.sin(angle)]).astype(np.float32)


def add(a, b):
    return (a[0] + b[0], a[1] + b[1])


def sub(a, b):
    return (a[0] - b[0], a[1] - b[1])


def turn(a):
    return (a[1], -a[0])


def four(a, b, c, d):
    even, odd = add(a, c), sub(a, c)
    both, rest = add(b, d), turn(sub(b, d))
    return (add(even, both), add(odd, rest), sub(even, both), sub(odd, rest))


def times_root(a, power):
    if power == 0:
        return a
    if power == 4:
        return turn(a)
    half = math.sqrt(0.5)
    if power == 2:
        return ((a[0] + a[1]) * half, (a[1] - a[0]) * half)
    if power == 6:
        return ((a[1] - a[0]) * half, -(a[0] + a[1]) * half)
    cosine, sine = math.cos(2 * math.pi * power / 16), math.sin(2 * math.pi * power / 16)
    return (a[0] * cosine + a[1] * sine, a[1] * cosine - a[0] * sine)


def sixteen(points):
    columns = [four(points[b], points[4 + b], points[8 + b], points[12 + b]) for b in range(4)]
    out = [None] * 16
    for low in range(4):
        mixed = four(*[times_root(columns[b][low], b * low) for b in range(4)])
        for high in range(4):
            out[low + 4 * high] = mixed[high]
    return out


def deal_kernel(in_ref, out_ref, rows):
    inputs, count = out_ref.shape[0], out_ref.shape[1]
    stride = rows.shape[0] // inputs
    for j in range(count):
        block = in_ref[0, :, j * LANES : (j + 1) * LANES].astype(jnp.float32)
        rows[pl.ds(j, inputs, stride=stride), :] = block
    for i in range(inputs):
        out_ref[i] = rows[i * stride : i * stride + count, :].astype(jnp.bfloat16)


def deal(samples):
    components, inputs, length = samples.shape
    count = 480
    steps = length // LANES // count
    return pl.pallas_call(
        deal_kernel,
        grid=(components, steps),
        out_shape=jax.ShapeDtypeStruct((inputs, components * length // LANES, LANES), samples.dtype),
        in_specs=[pl.BlockSpec((1, inputs, count * LANES), lambda c, j: (c, 0, j))],
        out_specs=pl.BlockSpec((inputs, count, LANES), lambda c, j: (0, c * steps + j, 0)),
        scratch_shapes=[pltpu.VMEM((inputs * (count + 8), LANES), jnp.float32)],
        compiler_params=pltpu.CompilerParams(vmem_limit_bytes=VMEM_LIMIT),
        name="deal",
    )(samples)


def channelize_kernel(
    frames, in_ref, taps_ref, twist_ref, table_ref, factor_ref, out_ref, wide, filt, rows, words
):
    chunks = RADIX * FINE // LANES
    tap_count = taps_ref.shape[0]
    history = tap_count - 1
    times, block_rows = in_ref.shape[0], in_ref.shape[1]
    stride = wide.shape[0] // (times + 1)

    wide[:block_rows] = jnp.zeros((block_rows, LANES), jnp.float32)
    for t in range(times):
        wide[(t + 1) * stride : (t + 1) * stride + block_rows] = in_ref[t].astype(jnp.float32)

    def filter_chunk(chunk, _):
        lanes = pl.ds(pl.multiple_of(chunk * LANES, LANES), LANES)
        weights = taps_ref[:, lanes].astype(jnp.float32)
        taps = [jnp.broadcast_to(weights[p : p + 1], (times, LANES)) for p in range(tap_count)]
        for comp in range(2):
            sums = [None] * frames
            for v in range(history + frames):
                before, u = (0, v) if v < history else (1, v - history)
                start = before * stride + (comp * frames + u) * chunks + chunk
                block = wide[pl.ds(start, times, stride=stride), :]
                for f in range(max(0, v - history), min(frames, v + 1)):
                    term = taps[v - f] * block
                    sums[f] = term if sums[f] is None else sums[f] + term
            for f in range(frames):
                filt[comp, chunk, f] = sums[f]
        return 0

    lax.fori_loop(0, chunks, filter_chunk, 0)

    for q in range(4):
        rows[q, pl.ds(frames, RADIX * times, stride=SLOT), :] = jnp.zeros((RADIX * times, LANES), jnp.float32)

    def first_transform(f, _):
        for half in range(2):
            points = [(filt[0, 2 * n + half, f], filt[1, 2 * n + half, f]) for n in range(RADIX)]
            mixed = sixteen(points)
            for k1 in range(RADIX):
                real, imag = mixed[k1]
                if k1:
                    cosine = twist_ref[0, pl.ds(k1, 1), pl.ds(half * LANES, LANES)]
                    sine = twist_ref[1, pl.ds(k1, 1), pl.ds(half * LANES, LANES)]
                    real, imag = real * cosine - imag * sine, imag * cosine + real * sine
                start = k1 * times * SLOT + f
                rows[half, pl.ds(start, times, stride=SLOT), :] = real
                rows[2 + half, pl.ds(start, times, stride=SLOT), :] = imag
        return 0

    lax.fori_loop(0, frames, first_transform, 0)

    def second_transform(group, _):
        span = pl.ds(pl.multiple_of(group * 512, 512), 512)
        block = jnp.concatenate([rows[q, span, :] for q in range(4)], axis=1)
        high = block.astype(jnp.bfloat16)
        low = (block - high.astype(jnp.float32)).astype(jnp.bfloat16)
        both = jnp.dot(high, table_ref[...], preferred_element_type=jnp.float32)
        rest = jnp.dot(low, table_ref[:, : 2 * KEPT], preferred_element_type=jnp.float32)
        total = both[:, : 2 * KEPT] + both[:, 2 * KEPT :] + rest
        for channel in range(4):
            scale = factor_ref[pl.ds(group * 4 + channel, 1), :]
            part = total[channel * LANES : (channel + 1) * LANES]
            real = jnp.clip(part[:, :KEPT] * scale, -127.0, 127.0)
            imag = jnp.clip(part[:, KEPT:] * scale, -127.0, 127.0)
            for side in range(2):
                cut = slice(side * 64, side * 64 + 64)
                word = jnp.concatenate([real[cut], imag[cut]], axis=0).T
                words[pl.ds(group * 8 + channel * 2 + side, KEPT, stride=32), :] = word
        return 0

    lax.fori_loop(0, rows.shape[1] // 512, second_transform, 0)

    def narrow(step, _):
        span = pl.ds(pl.multiple_of(step * 1024, 1024), 1024)
        out_ref[span, :] = words[span, :].astype(jnp.bfloat16)
        return 0

    lax.fori_loop(0, words.shape[0] // 1024, narrow, 0)


def channelize(dealt, taps, factor):
    times, block_rows, _ = dealt.shape
    chunks = RADIX * FINE // LANES
    frames = block_rows // (2 * chunks)
    table = second_table()
    high = table.astype(jnp.bfloat16)
    low = (table - high.astype(np.float64)).astype(jnp.bfloat16)
    vmem = pl.BlockSpec(memory_space=pltpu.VMEM)
    messages = KEPT * RADIX * 2
    return pl.pallas_call(
        functools.partial(channelize_kernel, frames),
        out_shape=jax.ShapeDtypeStruct((messages, LANES), jnp.bfloat16),
        in_specs=[vmem] * 5,
        out_specs=vmem,
        scratch_shapes=[
            pltpu.VMEM(((times + 1) * (block_rows + PAD), LANES), jnp.float32),
            pltpu.VMEM((2, chunks, frames, times, LANES), jnp.float32),
            pltpu.VMEM((4, RADIX * times * SLOT, LANES), jnp.float32),
            pltpu.VMEM((messages, LANES), jnp.float32),
        ],
        compiler_params=pltpu.CompilerParams(vmem_limit_bytes=VMEM_LIMIT),
        name="channelize",
    )(dealt, taps, twist_table(), jnp.concatenate([high, low], axis=1), factor)


def correlate_kernel(normalizer, words_ref, out_ref, wide):
    channel = pl.program_id(0)
    size = words_ref.shape[0] // 8
    half = size // 2

    @pl.when(channel == 0)
    def _():
        wide[...] = words_ref[...].astype(jnp.float32)

    sign = jnp.where(lax.broadcasted_iota(jnp.int32, (size, LANES), 1) < LANES // 2, 1.0, -1.0)
    blocks = [wide[pl.ds(2 * channel + q, size, stride=8), :] for q in range(2)]
    joined = jnp.concatenate(blocks, axis=1).astype(jnp.bfloat16)
    swapped = [pltpu.roll(block, LANES // 2, 1) * sign for block in blocks]
    swapped = jnp.concatenate(swapped, axis=1).astype(jnp.bfloat16)

    def product(left, right):
        return lax.dot_general(
            left, right, (((1,), (1,)), ((), ())), preferred_element_type=jnp.float32
        )

    first, second = joined[:half], joined[half:]
    lower = lax.broadcasted_iota(jnp.int32, (half, half), 0) >= lax.broadcasted_iota(
        jnp.int32, (half, half), 1
    )

    def finish(values):
        return (values * normalizer).astype(jnp.bfloat16)

    out_ref[0, :half, :half] = finish(
        jnp.where(lower, product(first, first), product(swapped[:half], first))
    )
    out_ref[0, half:, :half] = finish(product(second, first))
    out_ref[0, :half, half:] = finish(product(swapped[:half], second))
    out_ref[0, half:, half:] = finish(
        jnp.where(lower, product(second, second), product(swapped[half:], second))
    )


def correlate(words, normalizer):
    rows, _ = words.shape
    size = rows // 8
    return pl.pallas_call(
        functools.partial(correlate_kernel, normalizer),
        grid=(4,),
        out_shape=jax.ShapeDtypeStruct((4, size, size), jnp.bfloat16),
        in_specs=[pl.BlockSpec(words.shape, lambda c: (0, 0))],
        out_specs=pl.BlockSpec((1, size, size), lambda c: (c, 0, 0)),
        scratch_shapes=[pltpu.VMEM((rows, LANES), jnp.float32)],
        compiler_params=pltpu.CompilerParams(vmem_limit_bytes=VMEM_LIMIT),
        name="correlate",
    )(words)


def band_factor(scales, rescale):
    return (scales.astype(jnp.float32) * rescale).reshape(KEPT, RADIX).T


def body(samples, taps, scales):
    length = taps.shape[1]
    inputs = samples.shape[1]
    frames = samples.shape[2] // length
    stations, times = lax.axis_size("stn"), lax.axis_size("tm")
    mine = lax.dynamic_index_in_dim(scales, lax.axis_index("tm"), 0, keepdims=False)
    factor = band_factor(mine, 16.0 / math.sqrt(length))
    dealt = lax.all_to_all(deal(samples), "tm", split_axis=0, concat_axis=0, tiled=True)
    words = channelize(dealt, taps, factor)
    words = words.reshape(stations * times, 8, LANES)
    words = lax.all_to_all(words, ("stn", "tm"), split_axis=0, concat_axis=0, tiled=True)
    words = words.reshape(stations * times * 8, LANES)
    return correlate(words, 1.0 / (2.0 * frames * times * length))


def solution(mesh):
    placed = (P(None, "stn", "tm"), P(), P("stn", None))
    return jax.shard_map(
        body, mesh=mesh, in_specs=placed, out_specs=P(("stn", "tm"), None, None), check_vma=False
    )
```

```python
import functools
import math

import jax
import jax.numpy as jnp
import numpy as np
from jax import lax
from jax.experimental import pallas as pl
from jax.experimental.pallas import tpu as pltpu
from jax.sharding import PartitionSpec as P

LANES = 128
RADIX = 16
FINE = 256
KEPT = 128
SLOT = 16
VMEM_LIMIT = 28 * 2**20


def second_table():
    fine = np.arange(FINE)
    outputs = np.arange(KEPT) + (FINE - KEPT) // 2
    angle = 2.0 * np.pi * ((outputs[:, None] * fine[None, :]) % FINE) / FINE
    cosine, sine = np.cos(angle), np.sin(angle)
    return np.block([[cosine, sine], [-sine, cosine]]).T


def twist_table():
    angle = 2.0 * np.pi * (np.arange(RADIX)[:, None] * np.arange(FINE)[None, :]) / (RADIX * FINE)
    return np.stack([np.cos(angle), -np.sin(angle)]).astype(np.float32)


def add(a, b):
    return (a[0] + b[0], a[1] + b[1])


def sub(a, b):
    return (a[0] - b[0], a[1] - b[1])


def turn(a):
    return (a[1], -a[0])


def four(a, b, c, d):
    even, odd = add(a, c), sub(a, c)
    both, rest = add(b, d), turn(sub(b, d))
    return (add(even, both), add(odd, rest), sub(even, both), sub(odd, rest))


def times_root(a, power):
    if power == 0:
        return a
    if power == 4:
        return turn(a)
    half = math.sqrt(0.5)
    if power == 2:
        return ((a[0] + a[1]) * half, (a[1] - a[0]) * half)
    if power == 6:
        return ((a[1] - a[0]) * half, -(a[0] + a[1]) * half)
    cosine, sine = math.cos(2 * math.pi * power / 16), math.sin(2 * math.pi * power / 16)
    return (a[0] * cosine + a[1] * sine, a[1] * cosine - a[0] * sine)


def sixteen(points):
    columns = [four(points[b], points[4 + b], points[8 + b], points[12 + b]) for b in range(4)]
    out = [None] * 16
    for low in range(4):
        mixed = four(*[times_root(columns[b][low], b * low) for b in range(4)])
        for high in range(4):
            out[low + 4 * high] = mixed[high]
    return out


def analyze(plan, sources, taps_ref, keep_ref, twist_ref, table_ref, factor_ref, filt, rows, store):
    tap_count, length = taps_ref.shape
    chunks = length // LANES
    inputs = factor_ref.shape[1]
    slots = 8

    def filter_chunk(chunk, _):
        lanes = pl.ds(pl.multiple_of(chunk * LANES, LANES), LANES)
        weights = taps_ref[:, lanes].astype(jnp.float32)
        taps = [jnp.broadcast_to(weights[p : p + 1], (inputs, LANES)) for p in range(tap_count)]
        keep = keep_ref[...]
        window, first_later = sources
        for comp in range(2):
            sums = {f: [None, None] for f in plan}
            for v in range(min(plan), max(plan) + tap_count):
                users = [f for f in plan if f <= v < f + tap_count]
                if not users:
                    continue
                ref, u = window[v]
                at = pl.multiple_of(u * length + chunk * LANES, LANES)
                block = ref[comp, :, pl.ds(at, LANES)].astype(jnp.float32)
                later = int(v >= first_later)
                for f in users:
                    term = taps[v - f] * block
                    held = sums[f][later]
                    sums[f][later] = term if held is None else held + term
            for slot, f in enumerate(plan):
                early, late = sums[f]
                filt[comp, chunk, slot] = early if late is None else early * keep + late
        return 0

    lax.fori_loop(0, chunks, filter_chunk, 0)

    def first_transform(slot, _):
        for half in range(2):
            points = [(filt[0, 2 * n + half, slot], filt[1, 2 * n + half, slot]) for n in range(RADIX)]
            mixed = sixteen(points)
            for k1 in range(RADIX):
                real, imag = mixed[k1]
                if k1:
                    cosine = twist_ref[0, pl.ds(k1, 1), pl.ds(half * LANES, LANES)]
                    sine = twist_ref[1, pl.ds(k1, 1), pl.ds(half * LANES, LANES)]
                    real, imag = real * cosine - imag * sine, imag * cosine + real * sine
                at = pl.ds(pl.multiple_of((k1 * slots + slot) * inputs, inputs), inputs)
                rows[half, at, :] = real
                rows[2 + half, at, :] = imag
        return 0

    lax.fori_loop(0, len(plan), first_transform, 0)
    for slot in range(len(plan), slots):
        for q in range(4):
            for k1 in range(RADIX):
                at = (k1 * slots + slot) * inputs
                rows[q, at : at + inputs, :] = jnp.zeros((inputs, LANES), jnp.float32)

    many = 4
    count = many * slots * inputs

    def second_transform(group, _):
        span = pl.ds(pl.multiple_of(group * count, count), count)
        block = jnp.concatenate([rows[q, span, :] for q in range(4)], axis=1)
        high = block.astype(jnp.bfloat16)
        low = (block - high.astype(jnp.float32)).astype(jnp.bfloat16)
        both = jnp.dot(high, table_ref[...], preferred_element_type=jnp.float32)
        rest = jnp.dot(low, table_ref[:, : 2 * KEPT], preferred_element_type=jnp.float32)
        total = both[:, : 2 * KEPT] + both[:, 2 * KEPT :] + rest
        scale = factor_ref[pl.ds(group * many, many)][:, None]
        for comp in range(2):
            part = total[:, comp * KEPT : (comp + 1) * KEPT].reshape(many, slots, inputs, KEPT)
            part = jnp.clip(part * scale, -127.0, 127.0)
            store[comp, span, :] = part.reshape(count, KEPT)
        return 0

    lax.fori_loop(0, RADIX // many, second_transform, 0)


def window_of(own_ref, before, after, frames):
    window = [(ref, u) for ref, count in before for u in range(count)]
    window += [(own_ref, u) for u in range(frames)]
    first_later = len(window)
    window += [(ref, u) for ref, count in after for u in range(count)]
    return window, first_later


def middle_kernel(
    frames, near, far, own_ref, before_ref, after_ref, taps_ref, keep_ref, twist_ref, table_ref, factor_ref,
    out_ref, filt, rows,
):
    window, first_later = window_of(own_ref, [(None, far[0]), (before_ref, near[0])], [(after_ref, near[1])], frames)
    plan = middle_frames(near, far)
    analyze(plan, (window, first_later), taps_ref, keep_ref, twist_ref, table_ref, factor_ref, filt, rows, out_ref)


def middle_frames(near, far):
    return list(range(far[0], far[0] + near[0] + near[1]))


def outer_kernel(
    frames, near, far, own_ref, before_ref, after_ref, farther_before_ref, farther_after_ref, taps_ref, keep_ref,
    twist_ref, table_ref, factor_ref, middle_ref, out_ref, filt, rows, edge, words,
):
    window, first_later = window_of(
        own_ref,
        [(farther_before_ref, far[0]), (before_ref, near[0])],
        [(after_ref, near[1]), (farther_after_ref, far[1])],
        frames,
    )
    middle = middle_frames(near, far)
    plan = [f for f in range(frames) if f not in middle]
    analyze(plan, (window, first_later), taps_ref, keep_ref, twist_ref, table_ref, factor_ref, filt, rows, edge)
    inputs = factor_ref.shape[1]

    def arrange(high, _):
        for i in range(inputs):
            parts = []
            for comp in range(2):
                for channel in range(4):
                    at = pl.ds((high * 4 + channel) * 8 * inputs + i, 8, stride=inputs)
                    parts += [middle_ref[comp, at, :], edge[comp, at, :]]
            words[pl.ds(high * inputs + i, KEPT, stride=4 * inputs), :] = jnp.concatenate(parts, axis=0).T
        return 0

    lax.fori_loop(0, RADIX // 4, arrange, 0)

    def narrow(step, _):
        span = pl.ds(pl.multiple_of(step * 1024, 1024), 1024)
        out_ref[span, :] = words[span, :].astype(jnp.bfloat16)
        return 0

    lax.fori_loop(0, words.shape[0] // 1024, narrow, 0)


def tables():
    table = second_table()
    high = table.astype(jnp.bfloat16)
    low = (table - high.astype(np.float64)).astype(jnp.bfloat16)
    return twist_table(), jnp.concatenate([high, low], axis=1)


def scratch(inputs):
    return [
        pltpu.VMEM((2, RADIX * FINE // LANES, 8, inputs, LANES), jnp.float32),
        pltpu.VMEM((4, RADIX * 8 * inputs, LANES), jnp.float32),
    ]


def middle_frames_call(own, before, after, taps, keep, factor, frames, near, far):
    inputs = own.shape[1]
    vmem = pl.BlockSpec(memory_space=pltpu.VMEM)
    return pl.pallas_call(
        functools.partial(middle_kernel, frames, near, far),
        out_shape=jax.ShapeDtypeStruct((2, RADIX * 8 * inputs, KEPT), jnp.float32),
        in_specs=[vmem] * 8,
        out_specs=vmem,
        scratch_shapes=scratch(inputs),
        compiler_params=pltpu.CompilerParams(vmem_limit_bytes=VMEM_LIMIT),
        cost_estimate=pl.CostEstimate(flops=4 * 10**9, bytes_accessed=5 * 2**20, transcendentals=0),
        name="middle_frames",
    )(own, before, after, taps, keep, *tables(), factor)


def outer_frames_call(own, near_blocks, far_blocks, taps, keep, factor, middle, frames, near, far):
    inputs = own.shape[1]
    vmem = pl.BlockSpec(memory_space=pltpu.VMEM)
    messages = KEPT * 4 * inputs
    return pl.pallas_call(
        functools.partial(outer_kernel, frames, near, far),
        out_shape=jax.ShapeDtypeStruct((messages, LANES), jnp.bfloat16),
        in_specs=[vmem] * 11,
        out_specs=vmem,
        scratch_shapes=scratch(inputs)
        + [pltpu.VMEM((2, RADIX * 8 * inputs, KEPT), jnp.float32), pltpu.VMEM((messages, LANES), jnp.float32)],
        compiler_params=pltpu.CompilerParams(vmem_limit_bytes=VMEM_LIMIT),
        name="outer_frames",
    )(own, *near_blocks, *far_blocks, taps, keep, *tables(), factor, middle)


def correlate_kernel(normalizer, words_ref, out_ref, joined, swapped):
    channel = pl.program_id(0)
    stations, times, inputs, _ = words_ref.shape
    size = stations * inputs
    half = size // 2

    @pl.when(channel == 0)
    def _():
        some = 8
        lane = lax.broadcasted_iota(jnp.int32, (some * inputs, LANES), 1)
        sign = jnp.where(lane < LANES // 2, 1.0, -1.0)

        def trade(block, _):
            span = pl.ds(pl.multiple_of(block * some * inputs, some * inputs), some * inputs)
            for q in range(times // 4):
                held = [
                    words_ref[pl.ds(block * some, some), 4 * q + r].astype(jnp.float32).reshape(some * inputs, LANES)
                    for r in range(4)
                ]
                for bit in (1, 2):
                    shift = bit * SLOT
                    left = (lane // shift) % 2 == 0
                    for r in range(4):
                        if not r & bit:
                            x, y = held[r], held[r | bit]
                            held[r] = jnp.where(left, x, pltpu.roll(y, shift, 1))
                            held[r | bit] = jnp.where(left, pltpu.roll(x, LANES - shift, 1), y)
                for c in range(4):
                    lanes = pl.ds(q * LANES, LANES)
                    joined[c, span, lanes] = held[c].astype(jnp.bfloat16)
                    other = pltpu.roll(held[c], LANES // 2, 1) * sign
                    swapped[c, span, lanes] = other.astype(jnp.bfloat16)
            return 0

        lax.fori_loop(0, stations // some, trade, 0)

    def product(left, right):
        return lax.dot_general(
            left, right, (((1,), (1,)), ((), ())), preferred_element_type=jnp.float32
        )

    first, second = joined[channel, :half], joined[channel, half:]
    first_other, second_other = swapped[channel, :half], swapped[channel, half:]
    lower = lax.broadcasted_iota(jnp.int32, (half, half), 0) >= lax.broadcasted_iota(
        jnp.int32, (half, half), 1
    )

    def finish(values):
        return (values * normalizer).astype(jnp.bfloat16)

    out_ref[0, :half, :half] = finish(jnp.where(lower, product(first, first), product(first_other, first)))
    out_ref[0, half:, :half] = finish(product(second, first))
    out_ref[0, :half, half:] = finish(product(first_other, second))
    out_ref[0, half:, half:] = finish(
        jnp.where(lower, product(second, second), product(second_other, second))
    )


def correlate(words, normalizer):
    stations, times, inputs, _ = words.shape
    size = stations * inputs
    return pl.pallas_call(
        functools.partial(correlate_kernel, normalizer),
        grid=(4,),
        out_shape=jax.ShapeDtypeStruct((4, size, size), jnp.bfloat16),
        in_specs=[pl.BlockSpec(words.shape, lambda c: (0, 0, 0, 0))],
        out_specs=pl.BlockSpec((1, size, size), lambda c: (c, 0, 0)),
        scratch_shapes=[pltpu.VMEM((4, size, times * 2 * SLOT), jnp.bfloat16)] * 2,
        compiler_params=pltpu.CompilerParams(vmem_limit_bytes=VMEM_LIMIT),
        name="correlate",
    )(words)


def band_factor(scales, rescale):
    factor = (scales.astype(jnp.float32) * rescale).reshape(-1, KEPT, RADIX)
    return jnp.transpose(factor, (2, 0, 1))


def body(samples, taps, scales):
    length = taps.shape[1]
    inputs = samples.shape[1]
    frames = samples.shape[2] // length
    stations, times = lax.axis_size("stn"), lax.axis_size("tm")
    near, far = (4, 4), (4, 3)
    cut = frames - near[0]
    onward = [(i, i + 1) for i in range(times - 1)]
    backward = [(i, (i - 1) % times) for i in range(times)]

    def blocks(start, stop):
        return samples[:, :, start * length : stop * length]

    near_blocks = (
        lax.ppermute(blocks(cut, frames), "tm", onward),
        lax.ppermute(blocks(0, near[1]), "tm", backward),
    )
    far_blocks = (
        lax.ppermute(blocks(cut - far[0], cut), "tm", onward),
        lax.ppermute(blocks(near[1], near[1] + far[1]), "tm", backward),
    )
    keep = jnp.where(lax.axis_index("tm") == times - 1, 0.0, 1.0)
    keep = jnp.broadcast_to(keep.astype(jnp.float32), (inputs, LANES))
    factor = band_factor(scales, 16.0 / math.sqrt(length))
    middle = middle_frames_call(samples, *near_blocks, taps, keep, factor, frames, near, far)
    words = outer_frames_call(samples, near_blocks, far_blocks, taps, keep, factor, middle, frames, near, far)
    words = words.reshape(stations * times, inputs, LANES)
    words = lax.all_to_all(words, ("stn", "tm"), split_axis=0, concat_axis=0, tiled=True)
    words = words.reshape(stations, times, inputs, LANES)
    return correlate(words, 1.0 / (2.0 * frames * times * length))


def solution(mesh):
    placed = (P(None, "stn", "tm"), P(), P("stn", None))
    return jax.shard_map(
        body, mesh=mesh, in_specs=placed, out_specs=P(("stn", "tm"), None, None), check_vma=False
    )
```

```python
import functools
import math

import jax
import jax.numpy as jnp
import numpy as np
from jax import lax
from jax.experimental import pallas as pl
from jax.experimental.pallas import tpu as pltpu
from jax.sharding import PartitionSpec as P

LANES = 128
RADIX = 16
FINE = 256
KEPT = 128
SLOT = 16
VMEM_LIMIT = 28 * 2**20


def second_table():
    fine = np.arange(FINE)
    outputs = np.arange(KEPT) + (FINE - KEPT) // 2
    angle = 2.0 * np.pi * ((outputs[:, None] * fine[None, :]) % FINE) / FINE
    cosine, sine = np.cos(angle), np.sin(angle)
    return np.block([[cosine, sine], [-sine, cosine]]).T


def twist_table():
    angle = 2.0 * np.pi * (np.arange(RADIX)[:, None] * np.arange(FINE)[None, :]) / (RADIX * FINE)
    return np.stack([np.cos(angle), -np.sin(angle)]).astype(np.float32)


def add(a, b):
    return (a[0] + b[0], a[1] + b[1])


def sub(a, b):
    return (a[0] - b[0], a[1] - b[1])


def turn(a):
    return (a[1], -a[0])


def four(a, b, c, d):
    even, odd = add(a, c), sub(a, c)
    both, rest = add(b, d), turn(sub(b, d))
    return (add(even, both), add(odd, rest), sub(even, both), sub(odd, rest))


def times_root(a, power):
    if power == 0:
        return a
    if power == 4:
        return turn(a)
    half = math.sqrt(0.5)
    if power == 2:
        return ((a[0] + a[1]) * half, (a[1] - a[0]) * half)
    if power == 6:
        return ((a[1] - a[0]) * half, -(a[0] + a[1]) * half)
    cosine, sine = math.cos(2 * math.pi * power / 16), math.sin(2 * math.pi * power / 16)
    return (a[0] * cosine + a[1] * sine, a[1] * cosine - a[0] * sine)


def sixteen(points):
    columns = [four(points[b], points[4 + b], points[8 + b], points[12 + b]) for b in range(4)]
    out = [None] * 16
    for low in range(4):
        mixed = four(*[times_root(columns[b][low], b * low) for b in range(4)])
        for high in range(4):
            out[low + 4 * high] = mixed[high]
    return out


def filter_blocks(plan, fresh, sources, taps_ref, keep_ref, out_ref, begun_ref=None):
    tap_count, length = taps_ref.shape
    inputs = keep_ref.shape[0]
    window, first_later = sources

    def filter_chunk(chunk, _):
        lanes = pl.ds(pl.multiple_of(chunk * LANES, LANES), LANES)
        weights = taps_ref[:, lanes]
        taps = [jnp.broadcast_to(weights[p : p + 1], (inputs, LANES)) for p in range(tap_count)]
        keep = keep_ref[...]
        for comp in range(2):
            sums = {f: [None, None] for f in plan}
            if begun_ref is not None:
                sums = {f: [None, begun_ref[comp, chunk, slot]] for slot, f in enumerate(plan)}
            for v in fresh:
                users = [f for f in plan if f <= v < f + tap_count]
                if not users:
                    continue
                ref, u = window[v]
                at = pl.multiple_of(u * length + chunk * LANES, LANES)
                block = ref[comp, :, pl.ds(at, LANES)].astype(jnp.float32)
                for f in users:
                    later = int(begun_ref is not None or v >= first_later or f < first_later - tap_count + 1)
                    term = taps[v - f] * block
                    held = sums[f][later]
                    sums[f][later] = term if held is None else held + term
            for slot, f in enumerate(plan):
                early, late = sums[f]
                if early is not None:
                    early = early * keep
                    late = early if late is None else late + early
                out_ref[comp, chunk, slot] = late
        return 0

    lax.fori_loop(0, length // LANES, filter_chunk, 0)


def transform(count_used, twist_ref, table_ref, factor_ref, filt, rows, store):
    inputs = factor_ref.shape[1]
    slots = 8

    def first_transform(slot, _):
        for half in range(2):
            points = [(filt[0, 2 * n + half, slot], filt[1, 2 * n + half, slot]) for n in range(RADIX)]
            mixed = sixteen(points)
            for k1 in range(RADIX):
                real, imag = mixed[k1]
                if k1:
                    cosine = twist_ref[0, pl.ds(k1, 1), pl.ds(half * LANES, LANES)]
                    sine = twist_ref[1, pl.ds(k1, 1), pl.ds(half * LANES, LANES)]
                    real, imag = real * cosine - imag * sine, imag * cosine + real * sine
                at = pl.ds(pl.multiple_of((k1 * slots + slot) * inputs, inputs), inputs)
                rows[half, at, :] = real
                rows[2 + half, at, :] = imag
        return 0

    lax.fori_loop(0, count_used, first_transform, 0, unroll=True)
    for slot in range(count_used, slots):
        for q in range(4):
            for k1 in range(RADIX):
                at = (k1 * slots + slot) * inputs
                rows[q, at : at + inputs, :] = jnp.zeros((inputs, LANES), jnp.float32)

    block = jnp.concatenate([rows[q] for q in range(4)], axis=1)
    high = block.astype(jnp.bfloat16)
    low = (block - high.astype(jnp.float32)).astype(jnp.bfloat16)
    both = jnp.dot(high, table_ref[...], preferred_element_type=jnp.float32)
    rest = jnp.dot(low, table_ref[:, : 2 * KEPT], preferred_element_type=jnp.float32)
    total = both[:, : 2 * KEPT] + both[:, 2 * KEPT :] + rest
    scale = factor_ref[...][:, None]
    for comp in range(2):
        part = total[:, comp * KEPT : (comp + 1) * KEPT].reshape(RADIX, slots, inputs, KEPT)
        store[comp] = jnp.clip(part * scale, -127.0, 127.0).reshape(-1, KEPT)


def split_frames(frames, near, far):
    middle = range(far[0], far[0] + near[0] + near[1])
    return list(middle), [f for f in range(frames) if f not in middle]


def window_of(frames, near, far, refs):
    far_before, before, own, after, far_after = refs
    counts = (far[0], near[0], frames, near[1], far[1])
    window = [(ref, u) for ref, count in zip(refs, counts) for u in range(count)]
    return window, far[0] + near[0] + frames


def given(window):
    return [v for v, (ref, _) in enumerate(window) if ref is not None]


def own_kernel(
    frames, near, far, rescale, own_ref, taps_ref, keep_ref, scales_ref, order_ref, twist_ref,
    middle_ref, outer_ref, factor_ref, wide_taps_ref, same_twist_ref,
):
    inputs = scales_ref.shape[0]
    blocks = scales_ref.shape[1] // LANES
    part = LANES // blocks
    values = scales_ref[...].astype(jnp.float32) * rescale
    stacked = jnp.concatenate([values[:, b * LANES : (b + 1) * LANES] for b in range(blocks)], axis=0)
    stacked = jnp.dot(stacked.astype(jnp.bfloat16), order_ref[...], preferred_element_type=jnp.float32)
    held = [stacked[b * inputs : (b + 1) * inputs] for b in range(blocks)]
    lane = lax.broadcasted_iota(jnp.int32, (inputs, LANES), 1)
    bit = 1
    while bit < blocks:
        shift = bit * part
        left = (lane // shift) % 2 == 0
        for b in range(blocks):
            if not b & bit:
                x, y = held[b], held[b | bit]
                held[b] = jnp.where(left, x, pltpu.roll(y, shift, 1))
                held[b | bit] = jnp.where(left, pltpu.roll(x, LANES - shift, 1), y)
        bit *= 2
    for k1 in range(blocks):
        factor_ref[k1] = held[k1]
    wide_taps_ref[...] = taps_ref[...].astype(jnp.float32)
    same_twist_ref[...] = twist_ref[...]

    sources = window_of(frames, near, far, (None, None, own_ref, None, None))
    for plan, out_ref in zip(split_frames(frames, near, far), (middle_ref, outer_ref)):
        filter_blocks(plan, given(sources[0]), sources, wide_taps_ref, keep_ref, out_ref)


def middle_kernel(
    frames, near, far, before_ref, after_ref, taps_ref, keep_ref, twist_ref, table_ref, factor_ref, begun_ref,
    outer_begun_ref, out_ref, outer_ref, filt, rows,
):
    sources = window_of(frames, near, far, (None, before_ref, None, after_ref, None))
    middle, outer = split_frames(frames, near, far)
    fresh = given(sources[0])
    filter_blocks(middle, fresh, sources, taps_ref, keep_ref, filt, begun_ref)
    transform(len(middle), twist_ref, table_ref, factor_ref, filt, rows, out_ref)
    filter_blocks(outer, fresh, sources, taps_ref, keep_ref, outer_ref, outer_begun_ref)


def outer_kernel(
    frames, near, far, before_ref, after_ref, taps_ref, keep_ref, twist_ref, table_ref, factor_ref, middle_ref,
    begun_ref, out_ref, filt, rows, edge, words,
):
    sources = window_of(frames, near, far, (before_ref, None, None, None, after_ref))
    _, plan = split_frames(frames, near, far)
    filter_blocks(plan, given(sources[0]), sources, taps_ref, keep_ref, filt, begun_ref)
    transform(len(plan), twist_ref, table_ref, factor_ref, filt, rows, edge)
    inputs = factor_ref.shape[1]

    def arrange(high, _):
        for i in range(inputs):
            parts = []
            for comp in range(2):
                for channel in range(4):
                    at = pl.ds((high * 4 + channel) * 8 * inputs + i, 8, stride=inputs)
                    parts += [middle_ref[comp, at, :], edge[comp, at, :]]
            words[pl.ds(high * inputs + i, KEPT, stride=4 * inputs), :] = jnp.concatenate(parts, axis=0).T
        return 0

    lax.fori_loop(0, RADIX // 4, arrange, 0, unroll=True)

    def narrow(step, _):
        span = pl.ds(pl.multiple_of(step * 1024, 1024), 1024)
        out_ref[span, :] = words[span, :].astype(jnp.bfloat16)
        return 0

    lax.fori_loop(0, words.shape[0] // 1024, narrow, 0, unroll=True)


def split_table():
    table = second_table()
    high = table.astype(jnp.bfloat16)
    low = (table - high.astype(np.float64)).astype(jnp.bfloat16)
    return jnp.concatenate([high, low], axis=1)


def scratch(inputs):
    return [
        pltpu.VMEM((2, RADIX * FINE // LANES, 8, inputs, LANES), jnp.float32),
        pltpu.VMEM((4, RADIX * 8 * inputs, LANES), jnp.float32),
    ]


VMEM = pl.BlockSpec(memory_space=pltpu.VMEM)


def sums_shape(count, chunks, inputs):
    return jax.ShapeDtypeStruct((2, chunks, count, inputs, LANES), jnp.float32)


def lane_order():
    part = LANES // RADIX
    order = np.zeros((LANES, LANES))
    for m in range(part):
        for k1 in range(RADIX):
            order[m * RADIX + k1, k1 * part + m] = 1.0
    return order.astype(jnp.bfloat16)


def own_blocks_call(own, taps, keep, scales, rescale, frames, near, far):
    inputs = own.shape[1]
    chunks = taps.shape[1] // LANES
    twist = twist_table()
    middle, outer = split_frames(frames, near, far)
    return pl.pallas_call(
        functools.partial(own_kernel, frames, near, far, rescale),
        out_shape=(
            sums_shape(len(middle), chunks, inputs),
            sums_shape(len(outer), chunks, inputs),
            jax.ShapeDtypeStruct((RADIX, inputs, KEPT), jnp.float32),
            jax.ShapeDtypeStruct(taps.shape, jnp.float32),
            jax.ShapeDtypeStruct(twist.shape, jnp.float32),
        ),
        in_specs=[VMEM] * 6,
        out_specs=(VMEM,) * 5,
        compiler_params=pltpu.CompilerParams(vmem_limit_bytes=VMEM_LIMIT),
        cost_estimate=pl.CostEstimate(flops=3 * 10**9, bytes_accessed=6 * 2**20, transcendentals=0),
        name="own_blocks",
    )(own, taps, keep, scales, lane_order(), twist)


def middle_frames_call(near_blocks, taps, keep, twist, table, factor, begun, outer_begun, frames, near, far):
    inputs = near_blocks[0].shape[1]
    return pl.pallas_call(
        functools.partial(middle_kernel, frames, near, far),
        out_shape=(
            jax.ShapeDtypeStruct((2, RADIX * 8 * inputs, KEPT), jnp.float32),
            jax.ShapeDtypeStruct(outer_begun.shape, jnp.float32),
        ),
        in_specs=[VMEM] * 9,
        out_specs=(VMEM, VMEM),
        scratch_shapes=scratch(inputs),
        compiler_params=pltpu.CompilerParams(vmem_limit_bytes=VMEM_LIMIT),
        cost_estimate=pl.CostEstimate(flops=3 * 10**9, bytes_accessed=5 * 2**20, transcendentals=0),
        name="middle_frames",
    )(*near_blocks, taps, keep, twist, table, factor, begun, outer_begun)


def outer_frames_call(far_blocks, taps, keep, twist, table, factor, middle, begun, frames, near, far):
    inputs = far_blocks[0].shape[1]
    messages = KEPT * 4 * inputs
    return pl.pallas_call(
        functools.partial(outer_kernel, frames, near, far),
        out_shape=jax.ShapeDtypeStruct((messages, LANES), jnp.bfloat16),
        in_specs=[VMEM] * 9,
        out_specs=VMEM,
        scratch_shapes=scratch(inputs)
        + [pltpu.VMEM((2, RADIX * 8 * inputs, KEPT), jnp.float32), pltpu.VMEM((messages, LANES), jnp.float32)],
        compiler_params=pltpu.CompilerParams(vmem_limit_bytes=VMEM_LIMIT),
        name="outer_frames",
    )(*far_blocks, taps, keep, twist, table, factor, middle, begun)


def cut_kernel(spans, in_ref, *outs):
    for (start, stop), out in zip(spans, outs):
        out[...] = in_ref[:, :, start:stop]


def cut_spans(samples, spans):
    return pl.pallas_call(
        functools.partial(cut_kernel, spans),
        out_shape=[jax.ShapeDtypeStruct(samples.shape[:2] + (b - a,), samples.dtype) for a, b in spans],
        in_specs=[VMEM],
        out_specs=[VMEM] * len(spans),
        compiler_params=pltpu.CompilerParams(vmem_limit_bytes=VMEM_LIMIT),
        name="cut",
    )(samples)


def correlate_kernel(normalizer, words_ref, out_ref, joined, swapped):
    channel = pl.program_id(0)
    stations, times, inputs, _ = words_ref.shape
    size = stations * inputs
    half = size // 2

    @pl.when(channel == 0)
    def _():
        some = stations
        lane = lax.broadcasted_iota(jnp.int32, (some * inputs, LANES), 1)
        sign = jnp.where(lane < LANES // 2, 1.0, -1.0)

        def trade(block, _):
            span = pl.ds(pl.multiple_of(block * some * inputs, some * inputs), some * inputs)
            for q in range(times // 4):
                held = [
                    words_ref[pl.ds(block * some, some), 4 * q + r].astype(jnp.float32).reshape(some * inputs, LANES)
                    for r in range(4)
                ]
                for bit in (1, 2):
                    shift = bit * SLOT
                    left = (lane // shift) % 2 == 0
                    for r in range(4):
                        if not r & bit:
                            x, y = held[r], held[r | bit]
                            held[r] = jnp.where(left, x, pltpu.roll(y, shift, 1))
                            held[r | bit] = jnp.where(left, pltpu.roll(x, LANES - shift, 1), y)
                for c in range(4):
                    lanes = pl.ds(q * LANES, LANES)
                    joined[c, span, lanes] = held[c].astype(jnp.bfloat16)
                    other = pltpu.roll(held[c], LANES // 2, 1) * sign
                    swapped[c, span, lanes] = other.astype(jnp.bfloat16)
            return 0

        lax.fori_loop(0, stations // some, trade, 0)

    def product(left, right):
        return lax.dot_general(
            left, right, (((1,), (1,)), ((), ())), preferred_element_type=jnp.float32
        )

    first, second = joined[channel, :half], joined[channel, half:]
    first_other, second_other = swapped[channel, :half], swapped[channel, half:]
    lower = lax.broadcasted_iota(jnp.int32, (half, half), 0) >= lax.broadcasted_iota(
        jnp.int32, (half, half), 1
    )

    def finish(values):
        return (values * normalizer).astype(jnp.bfloat16)

    out_ref[0, :half, :half] = finish(jnp.where(lower, product(first, first), product(first_other, first)))
    out_ref[0, half:, :half] = finish(product(second, first))
    out_ref[0, :half, half:] = finish(product(first_other, second))
    out_ref[0, half:, half:] = finish(
        jnp.where(lower, product(second, second), product(second_other, second))
    )


def correlate(words, normalizer):
    stations, times, inputs, _ = words.shape
    size = stations * inputs
    return pl.pallas_call(
        functools.partial(correlate_kernel, normalizer),
        grid=(4,),
        out_shape=jax.ShapeDtypeStruct((4, size, size), jnp.bfloat16),
        in_specs=[pl.BlockSpec(words.shape, lambda c: (0, 0, 0, 0))],
        out_specs=pl.BlockSpec((1, size, size), lambda c: (c, 0, 0)),
        scratch_shapes=[pltpu.VMEM((4, size, times * 2 * SLOT), jnp.bfloat16)] * 2,
        compiler_params=pltpu.CompilerParams(vmem_limit_bytes=VMEM_LIMIT),
        name="correlate",
    )(words)


def body(samples, taps, scales):
    length = taps.shape[1]
    inputs = samples.shape[1]
    frames = samples.shape[2] // length
    stations, times = lax.axis_size("stn"), lax.axis_size("tm")
    near, far = (4, 4), (4, 3)
    cut = frames - near[0]
    onward = [(i, i + 1) for i in range(times - 1)]
    backward = [(i, (i - 1) % times) for i in range(times)]

    spans = [
        (cut, frames),
        (0, near[1]),
        (cut - far[0], cut),
        (near[1], near[1] + far[1]),
    ]
    blocks = cut_spans(samples, [(a * length, b * length) for a, b in spans])
    before, after, far_before, far_after = [
        lax.ppermute(block, "tm", route) for block, route in zip(blocks, (onward, backward) * 2)
    ]
    keep = jnp.where(lax.axis_index("tm") == times - 1, 0.0, 1.0)
    keep = jnp.broadcast_to(keep.astype(jnp.float32), (inputs, LANES))
    table = split_table()
    rescale = 16.0 / math.sqrt(length)
    begun, outer_begun, factor, wide_taps, twist = own_blocks_call(
        samples, taps, keep, scales, rescale, frames, near, far
    )
    middle, outer_begun = middle_frames_call(
        (before, after), wide_taps, keep, twist, table, factor, begun, outer_begun, frames, near, far
    )
    words = outer_frames_call(
        (far_before, far_after), wide_taps, keep, twist, table, factor, middle, outer_begun, frames, near, far
    )
    words = words.reshape(stations * times, inputs, LANES)
    words = lax.all_to_all(words, ("stn", "tm"), split_axis=0, concat_axis=0, tiled=True)
    words = words.reshape(stations, times, inputs, LANES)
    return correlate(words, 1.0 / (2.0 * frames * times * length))


def solution(mesh):
    placed = (P(None, "stn", "tm"), P(), P("stn", None))
    return jax.shard_map(
        body, mesh=mesh, in_specs=placed, out_specs=P(("stn", "tm"), None, None), check_vma=False
    )
```

```python
import functools
import math

import jax
import jax.numpy as jnp
import numpy as np
from jax import lax
from jax.experimental import pallas as pl
from jax.experimental.pallas import tpu as pltpu
from jax.sharding import PartitionSpec as P

LANES = 128
RADIX = 16
FINE = 256
KEPT = 128
SLOT = 16
VMEM_LIMIT = 28 * 2**20
WHOLE_VMEM = 62 * 2**20


def second_table():
    fine = np.arange(FINE)
    outputs = np.arange(KEPT) + (FINE - KEPT) // 2
    angle = 2.0 * np.pi * ((outputs[:, None] * fine[None, :]) % FINE) / FINE
    cosine, sine = np.cos(angle), np.sin(angle)
    return np.block([[cosine, sine], [-sine, cosine]]).T


def twist_table():
    angle = 2.0 * np.pi * (np.arange(RADIX)[:, None] * np.arange(FINE)[None, :]) / (RADIX * FINE)
    return np.stack([np.cos(angle), -np.sin(angle)]).astype(np.float32)


def add(a, b):
    return (a[0] + b[0], a[1] + b[1])


def sub(a, b):
    return (a[0] - b[0], a[1] - b[1])


def turn(a):
    return (a[1], -a[0])


def four(a, b, c, d):
    even, odd = add(a, c), sub(a, c)
    both, rest = add(b, d), turn(sub(b, d))
    return (add(even, both), add(odd, rest), sub(even, both), sub(odd, rest))


def times_root(a, power):
    if power == 0:
        return a
    if power == 4:
        return turn(a)
    half = math.sqrt(0.5)
    if power == 2:
        return ((a[0] + a[1]) * half, (a[1] - a[0]) * half)
    if power == 6:
        return ((a[1] - a[0]) * half, -(a[0] + a[1]) * half)
    cosine, sine = math.cos(2 * math.pi * power / 16), math.sin(2 * math.pi * power / 16)
    return (a[0] * cosine + a[1] * sine, a[1] * cosine - a[0] * sine)


def sixteen(points):
    columns = [four(points[b], points[4 + b], points[8 + b], points[12 + b]) for b in range(4)]
    out = [None] * 16
    for low in range(4):
        mixed = four(*[times_root(columns[b][low], b * low) for b in range(4)])
        for high in range(4):
            out[low + 4 * high] = mixed[high]
    return out


def filter_blocks(plan, fresh, sources, taps_ref, keep_ref, out_ref, begun_ref=None):
    tap_count, length = taps_ref.shape
    inputs = keep_ref.shape[0]
    window, first_later = sources

    def filter_chunk(chunk, _):
        lanes = pl.ds(pl.multiple_of(chunk * LANES, LANES), LANES)
        weights = taps_ref[:, lanes]
        taps = [jnp.broadcast_to(weights[p : p + 1], (inputs, LANES)) for p in range(tap_count)]
        keep = keep_ref[...]
        for comp in range(2):
            sums = {f: [None, None] for f in plan}
            if begun_ref is not None:
                sums = {f: [None, begun_ref[comp, chunk, slot]] for slot, f in enumerate(plan)}
            for v in fresh:
                users = [f for f in plan if f <= v < f + tap_count]
                if not users:
                    continue
                ref, u = window[v]
                at = pl.multiple_of(u * length + chunk * LANES, LANES)
                block = ref[comp, :, pl.ds(at, LANES)].astype(jnp.float32)
                for f in users:
                    later = int(begun_ref is not None or v >= first_later or f < first_later - tap_count + 1)
                    term = taps[v - f] * block
                    held = sums[f][later]
                    sums[f][later] = term if held is None else held + term
            for slot, f in enumerate(plan):
                early, late = sums[f]
                if early is not None:
                    early = early * keep
                    late = early if late is None else late + early
                out_ref[comp, chunk, slot] = late
        return 0

    lax.fori_loop(0, length // LANES, filter_chunk, 0)


def transform(count_used, twist_ref, table_ref, factor_ref, filt, rows, store):
    inputs = factor_ref.shape[1]
    slots = 8

    def first_transform(slot, _):
        for half in range(2):
            points = [(filt[0, 2 * n + half, slot], filt[1, 2 * n + half, slot]) for n in range(RADIX)]
            mixed = sixteen(points)
            for k1 in range(RADIX):
                real, imag = mixed[k1]
                if k1:
                    cosine = twist_ref[0, pl.ds(k1, 1), pl.ds(half * LANES, LANES)]
                    sine = twist_ref[1, pl.ds(k1, 1), pl.ds(half * LANES, LANES)]
                    real, imag = real * cosine - imag * sine, imag * cosine + real * sine
                at = pl.ds(pl.multiple_of((k1 * slots + slot) * inputs, inputs), inputs)
                rows[half, at, :] = real
                rows[2 + half, at, :] = imag
        return 0

    lax.fori_loop(0, count_used, first_transform, 0, unroll=True)
    for slot in range(count_used, slots):
        for q in range(4):
            for k1 in range(RADIX):
                at = (k1 * slots + slot) * inputs
                rows[q, at : at + inputs, :] = jnp.zeros((inputs, LANES), jnp.float32)

    block = jnp.concatenate([rows[q] for q in range(4)], axis=1)
    high = block.astype(jnp.bfloat16)
    low = (block - high.astype(jnp.float32)).astype(jnp.bfloat16)
    both = jnp.dot(high, table_ref[...], preferred_element_type=jnp.float32)
    rest = jnp.dot(low, table_ref[:, : 2 * KEPT], preferred_element_type=jnp.float32)
    total = both[:, : 2 * KEPT] + both[:, 2 * KEPT :] + rest
    scale = factor_ref[...][:, None]
    for comp in range(2):
        part = total[:, comp * KEPT : (comp + 1) * KEPT].reshape(RADIX, slots, inputs, KEPT)
        store[comp] = jnp.clip(part * scale, -127.0, 127.0).reshape(-1, KEPT)


def split_frames(frames, near, far):
    middle = range(far[0], far[0] + near[0] + near[1])
    return list(middle), [f for f in range(frames) if f not in middle]


def window_of(frames, near, far, refs):
    far_before, before, own, after, far_after = refs
    counts = (far[0], near[0], frames, near[1], far[1])
    window = [(ref, u) for ref, count in zip(refs, counts) for u in range(count)]
    return window, far[0] + near[0] + frames


def given(window):
    return [v for v, (ref, _) in enumerate(window) if ref is not None]


def own_kernel(
    frames, near, far, rescale, own_ref, taps_ref, keep_ref, scales_ref, order_ref, twist_ref,
    middle_ref, outer_ref, factor_ref, wide_taps_ref, same_twist_ref,
):
    inputs = scales_ref.shape[0]
    blocks = scales_ref.shape[1] // LANES
    part = LANES // blocks
    values = scales_ref[...].astype(jnp.float32) * rescale
    stacked = jnp.concatenate([values[:, b * LANES : (b + 1) * LANES] for b in range(blocks)], axis=0)
    stacked = jnp.dot(stacked.astype(jnp.bfloat16), order_ref[...], preferred_element_type=jnp.float32)
    held = [stacked[b * inputs : (b + 1) * inputs] for b in range(blocks)]
    lane = lax.broadcasted_iota(jnp.int32, (inputs, LANES), 1)
    bit = 1
    while bit < blocks:
        shift = bit * part
        left = (lane // shift) % 2 == 0
        for b in range(blocks):
            if not b & bit:
                x, y = held[b], held[b | bit]
                held[b] = jnp.where(left, x, pltpu.roll(y, shift, 1))
                held[b | bit] = jnp.where(left, pltpu.roll(x, LANES - shift, 1), y)
        bit *= 2
    for k1 in range(blocks):
        factor_ref[k1] = held[k1]
    wide_taps_ref[...] = taps_ref[...].astype(jnp.float32)
    same_twist_ref[...] = twist_ref[...]

    sources = window_of(frames, near, far, (None, None, own_ref, None, None))
    for plan, out_ref in zip(split_frames(frames, near, far), (middle_ref, outer_ref)):
        filter_blocks(plan, given(sources[0]), sources, wide_taps_ref, keep_ref, out_ref)


def middle_kernel(
    frames, near, far, before_ref, after_ref, taps_ref, keep_ref, twist_ref, table_ref, factor_ref, begun_ref,
    outer_begun_ref, out_ref, outer_ref, filt, rows,
):
    sources = window_of(frames, near, far, (None, before_ref, None, after_ref, None))
    middle, outer = split_frames(frames, near, far)
    fresh = given(sources[0])
    filter_blocks(middle, fresh, sources, taps_ref, keep_ref, filt, begun_ref)
    transform(len(middle), twist_ref, table_ref, factor_ref, filt, rows, out_ref)
    filter_blocks(outer, fresh, sources, taps_ref, keep_ref, outer_ref, outer_begun_ref)


def outer_kernel(
    frames, near, far, before_ref, after_ref, taps_ref, keep_ref, twist_ref, table_ref, factor_ref, middle_ref,
    begun_ref, out_ref, filt, rows, edge, words,
):
    sources = window_of(frames, near, far, (before_ref, None, None, None, after_ref))
    _, plan = split_frames(frames, near, far)
    filter_blocks(plan, given(sources[0]), sources, taps_ref, keep_ref, filt, begun_ref)
    transform(len(plan), twist_ref, table_ref, factor_ref, filt, rows, edge)
    inputs = factor_ref.shape[1]

    def arrange(high, _):
        for i in range(inputs):
            parts = []
            for comp in range(2):
                for channel in range(4):
                    at = pl.ds((high * 4 + channel) * 8 * inputs + i, 8, stride=inputs)
                    parts += [middle_ref[comp, at, :], edge[comp, at, :]]
            words[pl.ds(high * inputs + i, KEPT, stride=4 * inputs), :] = jnp.concatenate(parts, axis=0).T
        return 0

    lax.fori_loop(0, RADIX // 4, arrange, 0, unroll=True)

    def narrow(step, _):
        span = pl.ds(pl.multiple_of(step * 1024, 1024), 1024)
        out_ref[span, :] = words[span, :].astype(jnp.bfloat16)
        return 0

    lax.fori_loop(0, words.shape[0] // 1024, narrow, 0, unroll=True)


def split_table():
    table = second_table()
    high = table.astype(jnp.bfloat16)
    low = (table - high.astype(np.float64)).astype(jnp.bfloat16)
    return jnp.concatenate([high, low], axis=1)


def scratch(inputs):
    return [
        pltpu.VMEM((2, RADIX * FINE // LANES, 8, inputs, LANES), jnp.float32),
        pltpu.VMEM((4, RADIX * 8 * inputs, LANES), jnp.float32),
    ]


VMEM = pl.BlockSpec(memory_space=pltpu.VMEM)


def sums_shape(count, chunks, inputs):
    return jax.ShapeDtypeStruct((2, chunks, count, inputs, LANES), jnp.float32)


def lane_order():
    part = LANES // RADIX
    order = np.zeros((LANES, LANES))
    for m in range(part):
        for k1 in range(RADIX):
            order[m * RADIX + k1, k1 * part + m] = 1.0
    return order.astype(jnp.bfloat16)


def own_blocks_call(own, taps, keep, scales, rescale, frames, near, far):
    inputs = own.shape[1]
    chunks = taps.shape[1] // LANES
    twist = twist_table()
    middle, outer = split_frames(frames, near, far)
    return pl.pallas_call(
        functools.partial(own_kernel, frames, near, far, rescale),
        out_shape=(
            sums_shape(len(middle), chunks, inputs),
            sums_shape(len(outer), chunks, inputs),
            jax.ShapeDtypeStruct((RADIX, inputs, KEPT), jnp.float32),
            jax.ShapeDtypeStruct(taps.shape, jnp.float32),
            jax.ShapeDtypeStruct(twist.shape, jnp.float32),
        ),
        in_specs=[VMEM] * 6,
        out_specs=(VMEM,) * 5,
        compiler_params=pltpu.CompilerParams(vmem_limit_bytes=VMEM_LIMIT),
        cost_estimate=pl.CostEstimate(flops=3 * 10**9, bytes_accessed=6 * 2**20, transcendentals=0),
        name="own_blocks",
    )(own, taps, keep, scales, lane_order(), twist)


def middle_frames_call(near_blocks, taps, keep, twist, table, factor, begun, outer_begun, frames, near, far):
    inputs = near_blocks[0].shape[1]
    return pl.pallas_call(
        functools.partial(middle_kernel, frames, near, far),
        out_shape=(
            jax.ShapeDtypeStruct((2, RADIX * 8 * inputs, KEPT), jnp.float32),
            jax.ShapeDtypeStruct(outer_begun.shape, jnp.float32),
        ),
        in_specs=[VMEM] * 9,
        out_specs=(VMEM, VMEM),
        scratch_shapes=scratch(inputs),
        compiler_params=pltpu.CompilerParams(vmem_limit_bytes=VMEM_LIMIT),
        cost_estimate=pl.CostEstimate(flops=3 * 10**9, bytes_accessed=5 * 2**20, transcendentals=0),
        name="middle_frames",
    )(*near_blocks, taps, keep, twist, table, factor, begun, outer_begun)


def outer_frames_call(far_blocks, taps, keep, twist, table, factor, middle, begun, frames, near, far):
    inputs = far_blocks[0].shape[1]
    messages = KEPT * 4 * inputs
    return pl.pallas_call(
        functools.partial(outer_kernel, frames, near, far),
        out_shape=jax.ShapeDtypeStruct((messages, LANES), jnp.bfloat16),
        in_specs=[VMEM] * 9,
        out_specs=VMEM,
        scratch_shapes=scratch(inputs)
        + [pltpu.VMEM((2, RADIX * 8 * inputs, KEPT), jnp.float32), pltpu.VMEM((messages, LANES), jnp.float32)],
        compiler_params=pltpu.CompilerParams(vmem_limit_bytes=VMEM_LIMIT),
        name="outer_frames",
    )(*far_blocks, taps, keep, twist, table, factor, middle, begun)


def cut_kernel(spans, in_ref, *refs):
    outs, sems = refs[:-1], refs[-1]
    copies = [
        pltpu.make_async_copy(in_ref.at[:, :, start:stop], out, sems.at[i])
        for i, ((start, stop), out) in enumerate(zip(spans, outs))
    ]
    for copy in copies:
        copy.start()
    for copy in copies:
        copy.wait()


def cut_spans(samples, spans):
    return pl.pallas_call(
        functools.partial(cut_kernel, spans),
        out_shape=[jax.ShapeDtypeStruct(samples.shape[:2] + (b - a,), samples.dtype) for a, b in spans],
        in_specs=[pl.BlockSpec(memory_space=pltpu.HBM)],
        out_specs=[VMEM] * len(spans),
        scratch_shapes=[pltpu.SemaphoreType.DMA((len(spans),))],
        compiler_params=pltpu.CompilerParams(vmem_limit_bytes=WHOLE_VMEM),
        name="cut",
    )(samples)


def correlate_kernel(normalizer, words_ref, out_ref, joined, swapped, result, sems):
    stations, times, inputs, _ = words_ref.shape
    size = stations * inputs
    half = size // 2

    some = stations
    lane = lax.broadcasted_iota(jnp.int32, (some * inputs, LANES), 1)
    sign = jnp.where(lane < LANES // 2, 1.0, -1.0)

    def trade(block, _):
        span = pl.ds(pl.multiple_of(block * some * inputs, some * inputs), some * inputs)
        for q in range(times // 4):
            held = [
                words_ref[pl.ds(block * some, some), 4 * q + r].astype(jnp.float32).reshape(some * inputs, LANES)
                for r in range(4)
            ]
            for bit in (1, 2):
                shift = bit * SLOT
                left = (lane // shift) % 2 == 0
                for r in range(4):
                    if not r & bit:
                        x, y = held[r], held[r | bit]
                        held[r] = jnp.where(left, x, pltpu.roll(y, shift, 1))
                        held[r | bit] = jnp.where(left, pltpu.roll(x, LANES - shift, 1), y)
            for c in range(4):
                lanes = pl.ds(q * LANES, LANES)
                joined[c, span, lanes] = held[c].astype(jnp.bfloat16)
                other = pltpu.roll(held[c], LANES // 2, 1) * sign
                swapped[c, span, lanes] = other.astype(jnp.bfloat16)
        return 0

    lax.fori_loop(0, stations // some, trade, 0)

    def product(left, right):
        return lax.dot_general(
            left, right, (((1,), (1,)), ((), ())), preferred_element_type=jnp.float32
        )

    def finish(values):
        return (values * normalizer).astype(jnp.bfloat16)

    lower = lax.broadcasted_iota(jnp.int32, (half, half), 0) >= lax.broadcasted_iota(
        jnp.int32, (half, half), 1
    )
    copies = []
    for channel in range(4):
        first, second = joined[channel, :half], joined[channel, half:]
        first_other, second_other = swapped[channel, :half], swapped[channel, half:]
        result[channel, :half, :half] = finish(jnp.where(lower, product(first, first), product(first_other, first)))
        result[channel, half:, :half] = finish(product(second, first))
        result[channel, :half, half:] = finish(product(first_other, second))
        result[channel, half:, half:] = finish(
            jnp.where(lower, product(second, second), product(second_other, second))
        )
        copies.append(pltpu.make_async_copy(result.at[channel], out_ref.at[channel], sems.at[channel]))
        copies[-1].start()
    for copy in copies:
        copy.wait()


def correlate(words, normalizer):
    stations, times, inputs, _ = words.shape
    size = stations * inputs
    return pl.pallas_call(
        functools.partial(correlate_kernel, normalizer),
        out_shape=jax.ShapeDtypeStruct((4, size, size), jnp.bfloat16),
        in_specs=[VMEM],
        out_specs=pl.BlockSpec(memory_space=pltpu.HBM),
        scratch_shapes=[pltpu.VMEM((4, size, times * 2 * SLOT), jnp.bfloat16)] * 2
        + [pltpu.VMEM((4, size, size), jnp.bfloat16), pltpu.SemaphoreType.DMA((4,))],
        compiler_params=pltpu.CompilerParams(vmem_limit_bytes=VMEM_LIMIT),
        name="correlate",
    )(words)


def body(samples, taps, scales):
    length = taps.shape[1]
    inputs = samples.shape[1]
    frames = samples.shape[2] // length
    stations, times = lax.axis_size("stn"), lax.axis_size("tm")
    near, far = (4, 4), (4, 3)
    cut = frames - near[0]
    onward = [(i, i + 1) for i in range(times - 1)]
    backward = [(i, (i - 1) % times) for i in range(times)]

    spans = [
        (cut, frames),
        (0, near[1]),
        (cut - far[0], cut),
        (near[1], near[1] + far[1]),
    ]
    spans = [(a * length, b * length) for a, b in spans]
    blocks = cut_spans(samples, spans[:2]) + cut_spans(samples, spans[2:])
    before, after, far_before, far_after = [
        lax.ppermute(block, "tm", route) for block, route in zip(blocks, (onward, backward) * 2)
    ]
    keep = jnp.where(lax.axis_index("tm") == times - 1, 0.0, 1.0)
    keep = jnp.broadcast_to(keep.astype(jnp.float32), (inputs, LANES))
    table = split_table()
    rescale = 16.0 / math.sqrt(length)
    begun, outer_begun, factor, wide_taps, twist = own_blocks_call(
        samples, taps, keep, scales, rescale, frames, near, far
    )
    middle, outer_begun = middle_frames_call(
        (before, after), wide_taps, keep, twist, table, factor, begun, outer_begun, frames, near, far
    )
    words = outer_frames_call(
        (far_before, far_after), wide_taps, keep, twist, table, factor, middle, outer_begun, frames, near, far
    )
    words = words.reshape(stations * times, inputs, LANES)
    words = lax.all_to_all(words, ("stn", "tm"), split_axis=0, concat_axis=0, tiled=True)
    words = words.reshape(stations, times, inputs, LANES)
    return correlate(words, 1.0 / (2.0 * frames * times * length))


def solution(mesh):
    placed = (P(None, "stn", "tm"), P(), P("stn", None))
    return jax.shard_map(
        body, mesh=mesh, in_specs=placed, out_specs=P(("stn", "tm"), None, None), check_vma=False
    )
```

```python
import functools
import math

import jax
import jax.numpy as jnp
import numpy as np
from jax import lax
from jax.experimental import pallas as pl
from jax.experimental.pallas import tpu as pltpu
from jax.sharding import PartitionSpec as P

LANES = 128
RADIX = 16
FINE = 256
KEPT = 128
SLOT = 16
VMEM_LIMIT = 28 * 2**20


def second_table():
    fine = np.arange(FINE)
    outputs = np.arange(KEPT) + (FINE - KEPT) // 2
    angle = 2.0 * np.pi * ((outputs[:, None] * fine[None, :]) % FINE) / FINE
    cosine, sine = np.cos(angle), np.sin(angle)
    return np.block([[cosine, sine], [-sine, cosine]]).T


def twist_table():
    angle = 2.0 * np.pi * (np.arange(RADIX)[:, None] * np.arange(FINE)[None, :]) / (RADIX * FINE)
    return np.stack([np.cos(angle), -np.sin(angle)]).astype(np.float32)


def add(a, b):
    return (a[0] + b[0], a[1] + b[1])


def sub(a, b):
    return (a[0] - b[0], a[1] - b[1])


def turn(a):
    return (a[1], -a[0])


def four(a, b, c, d):
    even, odd = add(a, c), sub(a, c)
    both, rest = add(b, d), turn(sub(b, d))
    return (add(even, both), add(odd, rest), sub(even, both), sub(odd, rest))


def times_root(a, power):
    if power == 0:
        return a
    if power == 4:
        return turn(a)
    half = math.sqrt(0.5)
    if power == 2:
        return ((a[0] + a[1]) * half, (a[1] - a[0]) * half)
    if power == 6:
        return ((a[1] - a[0]) * half, -(a[0] + a[1]) * half)
    cosine, sine = math.cos(2 * math.pi * power / 16), math.sin(2 * math.pi * power / 16)
    return (a[0] * cosine + a[1] * sine, a[1] * cosine - a[0] * sine)


def sixteen(points):
    columns = [four(points[b], points[4 + b], points[8 + b], points[12 + b]) for b in range(4)]
    out = [None] * 16
    for low in range(4):
        mixed = four(*[times_root(columns[b][low], b * low) for b in range(4)])
        for high in range(4):
            out[low + 4 * high] = mixed[high]
    return out


def filter_blocks(plan, fresh, sources, taps_ref, keep_ref, out_ref, begun_ref=None):
    tap_count, length = taps_ref.shape
    inputs = keep_ref.shape[0]
    window, first_later = sources

    def filter_chunk(chunk, _):
        lanes = pl.ds(pl.multiple_of(chunk * LANES, LANES), LANES)
        weights = taps_ref[:, lanes]
        taps = [jnp.broadcast_to(weights[p : p + 1], (inputs, LANES)) for p in range(tap_count)]
        keep = keep_ref[...]
        for comp in range(2):
            sums = {f: [None, None] for f in plan}
            if begun_ref is not None:
                sums = {f: [None, begun_ref[comp, chunk, slot]] for slot, f in enumerate(plan)}
            for v in fresh:
                users = [f for f in plan if f <= v < f + tap_count]
                if not users:
                    continue
                ref, u = window[v]
                at = pl.multiple_of(u * length + chunk * LANES, LANES)
                block = ref[comp, :, pl.ds(at, LANES)].astype(jnp.float32)
                for f in users:
                    later = int(begun_ref is not None or v >= first_later or f < first_later - tap_count + 1)
                    term = taps[v - f] * block
                    held = sums[f][later]
                    sums[f][later] = term if held is None else held + term
            for slot, f in enumerate(plan):
                early, late = sums[f]
                if early is not None:
                    early = early * keep
                    late = early if late is None else late + early
                out_ref[comp, chunk, slot] = late
        return 0

    lax.fori_loop(0, length // LANES, filter_chunk, 0)


def transform(used, slots, twist_ref, table_ref, factor_ref, filt, rows, store):
    inputs = factor_ref.shape[1]

    def first_transform(slot, _):
        for half in range(2):
            points = [(filt[0, 2 * n + half, slot], filt[1, 2 * n + half, slot]) for n in range(RADIX)]
            mixed = sixteen(points)
            for k1 in range(RADIX):
                real, imag = mixed[k1]
                if k1:
                    cosine = twist_ref[0, pl.ds(k1, 1), pl.ds(half * LANES, LANES)]
                    sine = twist_ref[1, pl.ds(k1, 1), pl.ds(half * LANES, LANES)]
                    real, imag = real * cosine - imag * sine, imag * cosine + real * sine
                at = pl.ds(pl.multiple_of((k1 * slots + slot) * inputs, inputs), inputs)
                rows[half, at, :] = real
                rows[2 + half, at, :] = imag
        return 0

    lax.fori_loop(0, used, first_transform, 0, unroll=True)
    for slot in range(used, slots):
        for q in range(4):
            for k1 in range(RADIX):
                at = (k1 * slots + slot) * inputs
                rows[q, at : at + inputs, :] = jnp.zeros((inputs, LANES), jnp.float32)

    some = 8
    count = some * slots * inputs
    for first in range(0, RADIX, some):
        span = slice(first * slots * inputs, first * slots * inputs + count)
        block = jnp.concatenate([rows[q, span, :] for q in range(4)], axis=1)
        high = block.astype(jnp.bfloat16)
        low = (block - high.astype(jnp.float32)).astype(jnp.bfloat16)
        both = jnp.dot(high, table_ref[...], preferred_element_type=jnp.float32)
        rest = jnp.dot(low, table_ref[:, : 2 * KEPT], preferred_element_type=jnp.float32)
        total = both[:, : 2 * KEPT] + both[:, 2 * KEPT :] + rest
        scale = factor_ref[first : first + some][:, None]
        for comp in range(2):
            part = total[:, comp * KEPT : (comp + 1) * KEPT].reshape(some, slots, inputs, KEPT)
            part = jnp.clip(part * scale, -127.0, 127.0)
            store(comp, slice(first, first + some), part.reshape(some, slots * inputs, KEPT))


def split_frames(frames, near, far):
    middle = range(far[0], far[0] + near[0] + near[1])
    return list(middle), [f for f in range(frames) if f not in middle]


def window_of(frames, near, far, refs):
    counts = (far[0], near[0], near[1], frames - near[0] - near[1], near[0], near[1], far[1])
    window = [(ref, u) for ref, count in zip(refs, counts) for u in range(count)]
    return window, far[0] + near[0] + frames


def given(window):
    return [v for v, (ref, _) in enumerate(window) if ref is not None]


def own_kernel(
    frames, near, far, rescale, early_ref, between_ref, late_ref, taps_ref, keep_ref, scales_ref, order_ref, twist_ref,
    middle_ref, outer_ref, factor_ref, wide_taps_ref, same_twist_ref, early_far_ref, late_far_ref,
):
    inputs = scales_ref.shape[0]
    blocks = scales_ref.shape[1] // LANES
    part = LANES // blocks
    values = scales_ref[...].astype(jnp.float32) * rescale
    stacked = jnp.concatenate([values[:, b * LANES : (b + 1) * LANES] for b in range(blocks)], axis=0)
    stacked = jnp.dot(stacked.astype(jnp.bfloat16), order_ref[...], preferred_element_type=jnp.float32)
    held = [stacked[b * inputs : (b + 1) * inputs] for b in range(blocks)]
    lane = lax.broadcasted_iota(jnp.int32, (inputs, LANES), 1)
    bit = 1
    while bit < blocks:
        shift = bit * part
        left = (lane // shift) % 2 == 0
        for b in range(blocks):
            if not b & bit:
                x, y = held[b], held[b | bit]
                held[b] = jnp.where(left, x, pltpu.roll(y, shift, 1))
                held[b | bit] = jnp.where(left, pltpu.roll(x, LANES - shift, 1), y)
        bit *= 2
    for k1 in range(blocks):
        factor_ref[k1] = held[k1]
    wide_taps_ref[...] = taps_ref[...].astype(jnp.float32)
    same_twist_ref[...] = twist_ref[...]
    cut = early_far_ref.shape[2]
    early_far_ref[...] = between_ref[:, :, :cut]
    late_far_ref[...] = between_ref[:, :, cut:]

    own = (early_ref, between_ref, late_ref)
    sources = window_of(frames, near, far, (None, None, *own, None, None))
    for plan, out_ref in zip(split_frames(frames, near, far), (middle_ref, outer_ref)):
        filter_blocks(plan, given(sources[0]), sources, wide_taps_ref, keep_ref, out_ref)


def middle_kernel(
    frames, near, far, before_ref, after_ref, taps_ref, keep_ref, twist_ref, table_ref, factor_ref, begun_ref,
    outer_begun_ref, out_ref, edge_ref, outer_ref, filt, rows,
):
    sources = window_of(frames, near, far, (None, before_ref) + (None,) * 3 + (after_ref, None))
    middle, outer = split_frames(frames, near, far)
    fresh = given(sources[0])
    inputs = factor_ref.shape[1]

    def store(comp, some, part):
        out_ref[comp, some] = part[:, : 8 * inputs]
        edge_ref[comp, some] = part[:, 8 * inputs :]

    filter_blocks(middle, fresh, sources, taps_ref, keep_ref, filt, begun_ref)
    transform(len(middle), len(middle), twist_ref, table_ref, factor_ref, filt, rows, store)
    filter_blocks(outer, fresh, sources, taps_ref, keep_ref, outer_ref, outer_begun_ref)


def outer_kernel(
    frames, near, far, before_ref, after_ref, taps_ref, keep_ref, twist_ref, table_ref, factor_ref, middle_ref,
    edge_ref, begun_ref, out_ref, filt, rows, edge, words,
):
    sources = window_of(frames, near, far, (before_ref,) + (None,) * 5 + (after_ref,))
    middle, plan = split_frames(frames, near, far)
    inputs = factor_ref.shape[1]
    taken = (len(middle) - 8) * inputs
    edge[:, :, :taken] = edge_ref[...]

    def store(comp, some, part):
        edge[comp, some, taken:] = part

    filter_blocks(plan, given(sources[0]), sources, taps_ref, keep_ref, filt, begun_ref)
    transform(len(plan), SLOT - len(middle), twist_ref, table_ref, factor_ref, filt, rows, store)

    for high in range(RADIX // 4):
        for i in range(inputs):
            parts = []
            for comp in range(2):
                for channel in range(4):
                    for half in (middle_ref, edge):
                        parts.append(half[comp, high * 4 + channel, pl.ds(i, 8, stride=inputs), :])
            words[pl.ds(high * inputs + i, KEPT, stride=4 * inputs), :] = jnp.concatenate(parts, axis=0).T

    def narrow(step, _):
        span = pl.ds(pl.multiple_of(step * 1024, 1024), 1024)
        out_ref[span, :] = words[span, :].astype(jnp.bfloat16)
        return 0

    lax.fori_loop(0, words.shape[0] // 1024, narrow, 0, unroll=True)


def split_table():
    table = second_table()
    high = table.astype(jnp.bfloat16)
    low = (table - high.astype(np.float64)).astype(jnp.bfloat16)
    return jnp.concatenate([high, low], axis=1)


def scratch(inputs, slots):
    return [
        pltpu.VMEM((2, RADIX * FINE // LANES, slots, inputs, LANES), jnp.float32),
        pltpu.VMEM((4, RADIX * slots * inputs, LANES), jnp.float32),
    ]


VMEM = pl.BlockSpec(memory_space=pltpu.VMEM)


def sums_shape(count, chunks, inputs):
    return jax.ShapeDtypeStruct((2, chunks, count, inputs, LANES), jnp.float32)


def lane_order():
    part = LANES // RADIX
    order = np.zeros((LANES, LANES))
    for m in range(part):
        for k1 in range(RADIX):
            order[m * RADIX + k1, k1 * part + m] = 1.0
    return order.astype(jnp.bfloat16)


def own_blocks_call(pieces, taps, keep, scales, rescale, frames, near, far):
    inputs = pieces[0].shape[1]
    chunks = taps.shape[1] // LANES
    twist = twist_table()
    middle, outer = split_frames(frames, near, far)
    return pl.pallas_call(
        functools.partial(own_kernel, frames, near, far, rescale),
        out_shape=(
            sums_shape(len(middle), chunks, inputs),
            sums_shape(len(outer), chunks, inputs),
            jax.ShapeDtypeStruct((RADIX, inputs, KEPT), jnp.float32),
            jax.ShapeDtypeStruct(taps.shape, jnp.float32),
            jax.ShapeDtypeStruct(twist.shape, jnp.float32),
            jax.ShapeDtypeStruct((2, inputs, far[1] * taps.shape[1]), pieces[0].dtype),
            jax.ShapeDtypeStruct((2, inputs, far[0] * taps.shape[1]), pieces[0].dtype),
        ),
        in_specs=[VMEM] * 8,
        out_specs=(VMEM,) * 7,
        compiler_params=pltpu.CompilerParams(vmem_limit_bytes=VMEM_LIMIT),
        cost_estimate=pl.CostEstimate(flops=3 * 10**9, bytes_accessed=6 * 2**20, transcendentals=0),
        name="own_blocks",
    )(*pieces, taps, keep, scales, lane_order(), twist)


def middle_frames_call(near_blocks, taps, keep, twist, table, factor, begun, outer_begun, frames, near, far):
    inputs = near_blocks[0].shape[1]
    count = near[0] + near[1]
    return pl.pallas_call(
        functools.partial(middle_kernel, frames, near, far),
        out_shape=(
            jax.ShapeDtypeStruct((2, RADIX, 8 * inputs, KEPT), jnp.float32),
            jax.ShapeDtypeStruct((2, RADIX, (count - 8) * inputs, KEPT), jnp.float32),
            jax.ShapeDtypeStruct(outer_begun.shape, jnp.float32),
        ),
        in_specs=[VMEM] * 9,
        out_specs=(VMEM,) * 3,
        scratch_shapes=scratch(inputs, count),
        compiler_params=pltpu.CompilerParams(vmem_limit_bytes=VMEM_LIMIT),
        cost_estimate=pl.CostEstimate(flops=3 * 10**9, bytes_accessed=5 * 2**20, transcendentals=0),
        name="middle_frames",
    )(*near_blocks, taps, keep, twist, table, factor, begun, outer_begun)


def outer_frames_call(far_blocks, taps, keep, twist, table, factor, middle, edge, begun, frames, near, far):
    inputs = far_blocks[0].shape[1]
    messages = KEPT * 4 * inputs
    return pl.pallas_call(
        functools.partial(outer_kernel, frames, near, far),
        out_shape=jax.ShapeDtypeStruct((messages, LANES), jnp.bfloat16),
        in_specs=[VMEM] * 10,
        out_specs=VMEM,
        scratch_shapes=scratch(inputs, SLOT - near[0] - near[1])
        + [pltpu.VMEM((2, RADIX, 8 * inputs, KEPT), jnp.float32), pltpu.VMEM((messages, LANES), jnp.float32)],
        compiler_params=pltpu.CompilerParams(vmem_limit_bytes=VMEM_LIMIT),
        name="outer_frames",
    )(*far_blocks, taps, keep, twist, table, factor, middle, edge, begun)


def correlate_kernel(normalizer, words_ref, out_ref, joined, swapped, result, sems):
    stations, times, inputs, _ = words_ref.shape
    size = stations * inputs
    half = size // 2

    lane = lax.broadcasted_iota(jnp.int32, (size, LANES), 1)
    sign = jnp.where(lane < LANES // 2, 1.0, -1.0).astype(jnp.bfloat16)

    for q in range(times // 4):
        held = [words_ref[:, 4 * q + r].astype(jnp.float32).reshape(size, LANES).astype(jnp.bfloat16) for r in range(4)]
        for bit in (1, 2):
            shift = bit * SLOT
            left = (lane // shift) % 2 == 0
            for r in range(4):
                if not r & bit:
                    x, y = held[r], held[r | bit]
                    held[r] = jnp.where(left, x, pltpu.roll(y, shift, 1))
                    held[r | bit] = jnp.where(left, pltpu.roll(x, LANES - shift, 1), y)
        for c in range(4):
            lanes = slice(q * LANES, (q + 1) * LANES)
            joined[c, :, lanes] = held[c]
            swapped[c, :, lanes] = pltpu.roll(held[c], LANES // 2, 1) * sign

    def product(left, right):
        return lax.dot_general(
            left, right, (((1,), (1,)), ((), ())), preferred_element_type=jnp.float32
        )

    def finish(values):
        return (values * normalizer).astype(jnp.bfloat16)

    lower = lax.broadcasted_iota(jnp.int32, (half, half), 0) >= lax.broadcasted_iota(
        jnp.int32, (half, half), 1
    )
    copies = []
    for channel in range(4):
        first, second = joined[channel, :half], joined[channel, half:]
        first_other, second_other = swapped[channel, :half], swapped[channel, half:]
        result[channel, :half, :half] = finish(jnp.where(lower, product(first, first), product(first_other, first)))
        result[channel, half:, :half] = finish(product(second, first))
        result[channel, :half, half:] = finish(product(first_other, second))
        result[channel, half:, half:] = finish(
            jnp.where(lower, product(second, second), product(second_other, second))
        )
        copies.append(pltpu.make_async_copy(result.at[channel], out_ref.at[channel], sems.at[channel]))
        copies[-1].start()
    for copy in copies:
        copy.wait()


def correlate(words, normalizer):
    stations, times, inputs, _ = words.shape
    size = stations * inputs
    return pl.pallas_call(
        functools.partial(correlate_kernel, normalizer),
        out_shape=jax.ShapeDtypeStruct((4, size, size), jnp.bfloat16),
        in_specs=[VMEM],
        out_specs=pl.BlockSpec(memory_space=pltpu.HBM),
        scratch_shapes=[pltpu.VMEM((4, size, times * 2 * SLOT), jnp.bfloat16)] * 2
        + [pltpu.VMEM((4, size, size), jnp.bfloat16), pltpu.SemaphoreType.DMA((4,))],
        compiler_params=pltpu.CompilerParams(vmem_limit_bytes=VMEM_LIMIT),
        name="correlate",
    )(words)


def body(samples, taps, scales):
    length = taps.shape[1]
    inputs = samples.shape[1]
    frames = samples.shape[2] // length
    stations, times = lax.axis_size("stn"), lax.axis_size("tm")
    near, far = (5, 5), (2, 3)
    onward = [(i, i + 1) for i in range(times - 1)]
    backward = [(i, (i - 1) % times) for i in range(times)]

    def third(whole, which):
        span = frames // 3 * length
        return lax.slice_in_dim(whole, which * span, (which + 1) * span, axis=2)

    late = third(samples, 2)
    before = lax.ppermute(late, "tm", onward)
    later, late = lax.optimization_barrier((samples, late))
    early = third(later, 0)
    after = lax.ppermute(early, "tm", backward)
    latest, early = lax.optimization_barrier((later, early))
    pieces = (early, third(latest, 1), late)
    keep = jnp.where(lax.axis_index("tm") == times - 1, 0.0, 1.0)
    keep = jnp.broadcast_to(keep.astype(jnp.float32), (inputs, LANES))
    table = split_table()
    rescale = 16.0 / math.sqrt(length)
    begun, outer_begun, factor, wide_taps, twist, early_far, late_far = own_blocks_call(
        pieces, taps, keep, scales, rescale, frames, near, far
    )
    far_after = lax.ppermute(early_far, "tm", backward)
    far_before = lax.ppermute(late_far, "tm", onward)
    middle, edge, outer_begun = middle_frames_call(
        (before, after), wide_taps, keep, twist, table, factor, begun, outer_begun, frames, near, far
    )
    words = outer_frames_call(
        (far_before, far_after), wide_taps, keep, twist, table, factor, middle, edge, outer_begun, frames, near, far
    )
    words = words.reshape(stations * times, inputs, LANES)
    words = lax.all_to_all(words, ("stn", "tm"), split_axis=0, concat_axis=0, tiled=True)
    words = words.reshape(stations, times, inputs, LANES)
    return correlate(words, 1.0 / (2.0 * frames * times * length))


def solution(mesh):
    placed = (P(None, "stn", "tm"), P(), P("stn", None))
    return jax.shard_map(
        body, mesh=mesh, in_specs=placed, out_specs=P(("stn", "tm"), None, None), check_vma=False
    )
```

```python
import functools
import math

import jax
import jax.numpy as jnp
import numpy as np
from jax import lax
from jax.experimental import pallas as pl
from jax.experimental.pallas import tpu as pltpu
from jax.sharding import PartitionSpec as P

LANES = 128
RADIX = 16
FINE = 256
KEPT = 128
SLOT = 16
VMEM_LIMIT = 28 * 2**20


def second_table():
    fine = np.arange(FINE)
    outputs = np.arange(KEPT) + (FINE - KEPT) // 2
    angle = 2.0 * np.pi * ((outputs[:, None] * fine[None, :]) % FINE) / FINE
    cosine, sine = np.cos(angle), np.sin(angle)
    return np.block([[cosine, sine], [-sine, cosine]]).T


def twist_table():
    angle = 2.0 * np.pi * (np.arange(RADIX)[:, None] * np.arange(FINE)[None, :]) / (RADIX * FINE)
    return np.stack([np.cos(angle), -np.sin(angle)]).astype(np.float32)


def add(a, b):
    return (a[0] + b[0], a[1] + b[1])


def sub(a, b):
    return (a[0] - b[0], a[1] - b[1])


def turn(a):
    return (a[1], -a[0])


def four(a, b, c, d):
    even, odd = add(a, c), sub(a, c)
    both, rest = add(b, d), turn(sub(b, d))
    return (add(even, both), add(odd, rest), sub(even, both), sub(odd, rest))


def times_root(a, power):
    if power == 0:
        return a
    if power == 4:
        return turn(a)
    half = math.sqrt(0.5)
    if power == 2:
        return ((a[0] + a[1]) * half, (a[1] - a[0]) * half)
    if power == 6:
        return ((a[1] - a[0]) * half, -(a[0] + a[1]) * half)
    cosine, sine = math.cos(2 * math.pi * power / 16), math.sin(2 * math.pi * power / 16)
    return (a[0] * cosine + a[1] * sine, a[1] * cosine - a[0] * sine)


def sixteen(points):
    columns = [four(points[b], points[4 + b], points[8 + b], points[12 + b]) for b in range(4)]
    out = [None] * 16
    for low in range(4):
        mixed = four(*[times_root(columns[b][low], b * low) for b in range(4)])
        for high in range(4):
            out[low + 4 * high] = mixed[high]
    return out


def filter_blocks(plan, fresh, sources, taps_ref, keep_ref, out_ref, begun_ref=None):
    tap_count, length = taps_ref.shape
    inputs = keep_ref.shape[0]
    window, first_later = sources

    def filter_chunk(chunk, _):
        lanes = pl.ds(pl.multiple_of(chunk * LANES, LANES), LANES)
        weights = taps_ref[:, lanes]
        taps = [jnp.broadcast_to(weights[p : p + 1], (inputs, LANES)) for p in range(tap_count)]
        keep = keep_ref[...]
        for comp in range(2):
            sums = {f: [None, None] for f in plan}
            if begun_ref is not None:
                sums = {f: [None, begun_ref[comp, chunk, slot]] for slot, f in enumerate(plan)}
            for v in fresh:
                users = [f for f in plan if f <= v < f + tap_count]
                if not users:
                    continue
                ref, u = window[v]
                at = pl.multiple_of(u * length + chunk * LANES, LANES)
                block = ref[comp, :, pl.ds(at, LANES)].astype(jnp.float32)
                for f in users:
                    later = int(begun_ref is not None or v >= first_later or f < first_later - tap_count + 1)
                    term = taps[v - f] * block
                    held = sums[f][later]
                    sums[f][later] = term if held is None else held + term
            for slot, f in enumerate(plan):
                early, late = sums[f]
                if early is not None:
                    early = early * keep
                    late = early if late is None else late + early
                out_ref[comp, chunk, slot] = late
        return 0

    lax.fori_loop(0, length // LANES, filter_chunk, 0, unroll=4)


def transform(used, slots, twist_ref, table_ref, factor_ref, filt, rows, store):
    inputs = factor_ref.shape[1]

    def first_transform(slot, _):
        for half in range(2):
            points = [(filt[0, 2 * n + half, slot], filt[1, 2 * n + half, slot]) for n in range(RADIX)]
            mixed = sixteen(points)
            for k1 in range(RADIX):
                real, imag = mixed[k1]
                if k1:
                    cosine = twist_ref[0, pl.ds(k1, 1), pl.ds(half * LANES, LANES)]
                    sine = twist_ref[1, pl.ds(k1, 1), pl.ds(half * LANES, LANES)]
                    real, imag = real * cosine - imag * sine, imag * cosine + real * sine
                at = pl.ds(pl.multiple_of((k1 * slots + slot) * inputs, inputs), inputs)
                rows[half, at, :] = real
                rows[2 + half, at, :] = imag
        return 0

    lax.fori_loop(0, used, first_transform, 0, unroll=True)
    for slot in range(used, slots):
        for q in range(4):
            for k1 in range(RADIX):
                at = (k1 * slots + slot) * inputs
                rows[q, at : at + inputs, :] = jnp.zeros((inputs, LANES), jnp.float32)

    some = 8
    count = some * slots * inputs
    for first in range(0, RADIX, some):
        span = slice(first * slots * inputs, first * slots * inputs + count)
        block = jnp.concatenate([rows[q, span, :] for q in range(4)], axis=1)
        high = block.astype(jnp.bfloat16)
        low = (block - high.astype(jnp.float32)).astype(jnp.bfloat16)
        both = jnp.dot(high, table_ref[...], preferred_element_type=jnp.float32)
        rest = jnp.dot(low, table_ref[:, : 2 * KEPT], preferred_element_type=jnp.float32)
        total = both[:, : 2 * KEPT] + both[:, 2 * KEPT :] + rest
        scale = factor_ref[first : first + some][:, None]
        for comp in range(2):
            part = total[:, comp * KEPT : (comp + 1) * KEPT].reshape(some, slots, inputs, KEPT)
            part = jnp.clip(part * scale, -127.0, 127.0)
            store(comp, slice(first, first + some), part.reshape(some, slots * inputs, KEPT))


def split_frames(frames, near, far):
    middle = range(far[0], far[0] + near[0] + near[1])
    return list(middle), [f for f in range(frames) if f not in middle]


def window_of(frames, near, far, refs):
    counts = (far[0], near[0], near[1], frames - near[0] - near[1], near[0], near[1], far[1])
    window = [(ref, u) for ref, count in zip(refs, counts) for u in range(count)]
    return window, far[0] + near[0] + frames


def given(window):
    return [v for v, (ref, _) in enumerate(window) if ref is not None]


def own_kernel(
    frames, near, far, rescale, early_ref, between_ref, late_ref, taps_ref, keep_ref, scales_ref, order_ref, twist_ref,
    middle_ref, outer_ref, factor_ref, wide_taps_ref, same_twist_ref, early_far_ref, late_far_ref,
):
    inputs = scales_ref.shape[0]
    blocks = scales_ref.shape[1] // LANES
    part = LANES // blocks
    values = scales_ref[...].astype(jnp.float32) * rescale
    stacked = jnp.concatenate([values[:, b * LANES : (b + 1) * LANES] for b in range(blocks)], axis=0)
    stacked = jnp.dot(stacked.astype(jnp.bfloat16), order_ref[...], preferred_element_type=jnp.float32)
    held = [stacked[b * inputs : (b + 1) * inputs] for b in range(blocks)]
    lane = lax.broadcasted_iota(jnp.int32, (inputs, LANES), 1)
    bit = 1
    while bit < blocks:
        shift = bit * part
        left = (lane // shift) % 2 == 0
        for b in range(blocks):
            if not b & bit:
                x, y = held[b], held[b | bit]
                held[b] = jnp.where(left, x, pltpu.roll(y, shift, 1))
                held[b | bit] = jnp.where(left, pltpu.roll(x, LANES - shift, 1), y)
        bit *= 2
    for k1 in range(blocks):
        factor_ref[k1] = held[k1]
    wide_taps_ref[...] = taps_ref[...].astype(jnp.float32)
    same_twist_ref[...] = twist_ref[...]
    cut = early_far_ref.shape[2]
    early_far_ref[...] = between_ref[:, :, :cut]
    late_far_ref[...] = between_ref[:, :, cut:]

    own = (early_ref, between_ref, late_ref)
    sources = window_of(frames, near, far, (None, None, *own, None, None))
    for plan, out_ref in zip(split_frames(frames, near, far), (middle_ref, outer_ref)):
        filter_blocks(plan, given(sources[0]), sources, wide_taps_ref, keep_ref, out_ref)


def middle_kernel(
    frames, near, far, before_ref, after_ref, taps_ref, keep_ref, twist_ref, table_ref, factor_ref, begun_ref,
    outer_begun_ref, out_ref, edge_ref, outer_ref, filt, rows,
):
    sources = window_of(frames, near, far, (None, before_ref) + (None,) * 3 + (after_ref, None))
    middle, outer = split_frames(frames, near, far)
    fresh = given(sources[0])
    inputs = factor_ref.shape[1]

    def store(comp, some, part):
        out_ref[comp, some] = part[:, : 8 * inputs]
        edge_ref[comp, some] = part[:, 8 * inputs :]

    filter_blocks(middle, fresh, sources, taps_ref, keep_ref, filt, begun_ref)
    transform(len(middle), len(middle), twist_ref, table_ref, factor_ref, filt, rows, store)
    filter_blocks(outer, fresh, sources, taps_ref, keep_ref, outer_ref, outer_begun_ref)


def outer_kernel(
    frames, near, far, before_ref, after_ref, taps_ref, keep_ref, twist_ref, table_ref, factor_ref, middle_ref,
    edge_ref, begun_ref, out_ref, filt, rows, edge, first_words, second_words,
):
    sources = window_of(frames, near, far, (before_ref,) + (None,) * 5 + (after_ref,))
    middle, plan = split_frames(frames, near, far)
    inputs = factor_ref.shape[1]
    taken = (len(middle) - 8) * inputs
    edge[:, :, :taken] = edge_ref[...]

    def store(comp, some, part):
        edge[comp, some, taken:] = part
        if comp == 1:
            arrange(some.start // 8, (first_words, second_words)[some.start // 8])

    def arrange(pair, words):
        for high in range(2):
            for i in range(inputs):
                parts = []
                for comp in range(2):
                    for channel in range(4):
                        k1 = (pair * 2 + high) * 4 + channel
                        for half in (middle_ref, edge):
                            parts.append(half[comp, k1, pl.ds(i, 8, stride=inputs), :])
                turned = jnp.concatenate(parts, axis=0).T
                words[pl.ds(high * inputs + i, KEPT, stride=2 * inputs), :] = turned
        narrow = words[...].reshape(KEPT, 2 * inputs, LANES).astype(jnp.bfloat16)
        out_ref[:, pair * 2 * inputs : (pair + 1) * 2 * inputs, :] = narrow

    filter_blocks(plan, given(sources[0]), sources, taps_ref, keep_ref, filt, begun_ref)
    transform(len(plan), SLOT - len(middle), twist_ref, table_ref, factor_ref, filt, rows, store)


def split_table():
    table = second_table()
    high = table.astype(jnp.bfloat16)
    low = (table - high.astype(np.float64)).astype(jnp.bfloat16)
    return jnp.concatenate([high, low], axis=1)


def scratch(inputs, slots):
    return [
        pltpu.VMEM((2, RADIX * FINE // LANES, slots, inputs, LANES), jnp.float32),
        pltpu.VMEM((4, RADIX * slots * inputs, LANES), jnp.float32),
    ]


VMEM = pl.BlockSpec(memory_space=pltpu.VMEM)


def sums_shape(count, chunks, inputs):
    return jax.ShapeDtypeStruct((2, chunks, count, inputs, LANES), jnp.float32)


def lane_order():
    part = LANES // RADIX
    order = np.zeros((LANES, LANES))
    for m in range(part):
        for k1 in range(RADIX):
            order[m * RADIX + k1, k1 * part + m] = 1.0
    return order.astype(jnp.bfloat16)


def own_blocks_call(pieces, taps, keep, scales, rescale, frames, near, far):
    inputs = pieces[0].shape[1]
    chunks = taps.shape[1] // LANES
    twist = twist_table()
    middle, outer = split_frames(frames, near, far)
    return pl.pallas_call(
        functools.partial(own_kernel, frames, near, far, rescale),
        out_shape=(
            sums_shape(len(middle), chunks, inputs),
            sums_shape(len(outer), chunks, inputs),
            jax.ShapeDtypeStruct((RADIX, inputs, KEPT), jnp.float32),
            jax.ShapeDtypeStruct(taps.shape, jnp.float32),
            jax.ShapeDtypeStruct(twist.shape, jnp.float32),
            jax.ShapeDtypeStruct((2, inputs, far[1] * taps.shape[1]), pieces[0].dtype),
            jax.ShapeDtypeStruct((2, inputs, far[0] * taps.shape[1]), pieces[0].dtype),
        ),
        in_specs=[VMEM] * 8,
        out_specs=(VMEM,) * 7,
        compiler_params=pltpu.CompilerParams(vmem_limit_bytes=VMEM_LIMIT),
        cost_estimate=pl.CostEstimate(flops=3 * 10**9, bytes_accessed=6 * 2**20, transcendentals=0),
        name="own_blocks",
    )(*pieces, taps, keep, scales, lane_order(), twist)


def middle_frames_call(near_blocks, taps, keep, twist, table, factor, begun, outer_begun, frames, near, far):
    inputs = near_blocks[0].shape[1]
    count = near[0] + near[1]
    return pl.pallas_call(
        functools.partial(middle_kernel, frames, near, far),
        out_shape=(
            jax.ShapeDtypeStruct((2, RADIX, 8 * inputs, KEPT), jnp.float32),
            jax.ShapeDtypeStruct((2, RADIX, (count - 8) * inputs, KEPT), jnp.float32),
            jax.ShapeDtypeStruct(outer_begun.shape, jnp.float32),
        ),
        in_specs=[VMEM] * 9,
        out_specs=(VMEM,) * 3,
        scratch_shapes=scratch(inputs, count),
        compiler_params=pltpu.CompilerParams(vmem_limit_bytes=VMEM_LIMIT),
        cost_estimate=pl.CostEstimate(flops=3 * 10**9, bytes_accessed=5 * 2**20, transcendentals=0),
        name="middle_frames",
    )(*near_blocks, taps, keep, twist, table, factor, begun, outer_begun)


def outer_frames_call(far_blocks, taps, keep, twist, table, factor, middle, edge, begun, frames, near, far):
    inputs = far_blocks[0].shape[1]
    return pl.pallas_call(
        functools.partial(outer_kernel, frames, near, far),
        out_shape=jax.ShapeDtypeStruct((KEPT, 4 * inputs, LANES), jnp.bfloat16),
        in_specs=[VMEM] * 10,
        out_specs=VMEM,
        scratch_shapes=scratch(inputs, SLOT - near[0] - near[1])
        + [pltpu.VMEM((2, RADIX, 8 * inputs, KEPT), jnp.float32)]
        + [pltpu.VMEM((KEPT * 2 * inputs, LANES), jnp.float32)] * 2,
        compiler_params=pltpu.CompilerParams(vmem_limit_bytes=VMEM_LIMIT),
        name="outer_frames",
    )(*far_blocks, taps, keep, twist, table, factor, middle, edge, begun)


def correlate_kernel(normalizer, words_ref, out_ref, joined, swapped, result, sems):
    stations, times, inputs, _ = words_ref.shape
    size = stations * inputs
    half = size // 2

    lane = lax.broadcasted_iota(jnp.int32, (size, LANES), 1)
    sign = jnp.where(lane < LANES // 2, 1.0, -1.0).astype(jnp.bfloat16)

    for q in range(times // 4):
        held = [words_ref[:, 4 * q + r].astype(jnp.float32).reshape(size, LANES).astype(jnp.bfloat16) for r in range(4)]
        for bit in (1, 2):
            shift = bit * SLOT
            left = (lane // shift) % 2 == 0
            for r in range(4):
                if not r & bit:
                    x, y = held[r], held[r | bit]
                    held[r] = jnp.where(left, x, pltpu.roll(y, shift, 1))
                    held[r | bit] = jnp.where(left, pltpu.roll(x, LANES - shift, 1), y)
        for c in range(4):
            lanes = slice(q * LANES, (q + 1) * LANES)
            joined[c, :, lanes] = held[c]
            swapped[c, :, lanes] = pltpu.roll(held[c], LANES // 2, 1) * sign

    def product(left, right):
        return lax.dot_general(
            left, right, (((1,), (1,)), ((), ())), preferred_element_type=jnp.float32
        )

    def finish(values):
        return (values * normalizer).astype(jnp.bfloat16)

    lower = lax.broadcasted_iota(jnp.int32, (half, half), 0) >= lax.broadcasted_iota(
        jnp.int32, (half, half), 1
    )
    copies = []
    for channel in range(4):
        first, second = joined[channel, :half], joined[channel, half:]
        first_other, second_other = swapped[channel, :half], swapped[channel, half:]
        result[channel, :half, :half] = finish(jnp.where(lower, product(first, first), product(first_other, first)))
        result[channel, half:, :half] = finish(product(second, first))
        result[channel, :half, half:] = finish(product(first_other, second))
        result[channel, half:, half:] = finish(
            jnp.where(lower, product(second, second), product(second_other, second))
        )
        copies.append(pltpu.make_async_copy(result.at[channel], out_ref.at[channel], sems.at[channel]))
        copies[-1].start()
    for copy in copies:
        copy.wait()


def correlate(words, normalizer):
    stations, times, inputs, _ = words.shape
    size = stations * inputs
    return pl.pallas_call(
        functools.partial(correlate_kernel, normalizer),
        out_shape=jax.ShapeDtypeStruct((4, size, size), jnp.bfloat16),
        in_specs=[VMEM],
        out_specs=pl.BlockSpec(memory_space=pltpu.HBM),
        scratch_shapes=[pltpu.VMEM((4, size, times * 2 * SLOT), jnp.bfloat16)] * 2
        + [pltpu.VMEM((4, size, size), jnp.bfloat16), pltpu.SemaphoreType.DMA((4,))],
        compiler_params=pltpu.CompilerParams(vmem_limit_bytes=VMEM_LIMIT),
        name="correlate",
    )(words)


def body(samples, taps, scales):
    length = taps.shape[1]
    inputs = samples.shape[1]
    frames = samples.shape[2] // length
    stations, times = lax.axis_size("stn"), lax.axis_size("tm")
    near, far = (5, 5), (2, 3)
    onward = [(i, i + 1) for i in range(times - 1)]
    backward = [(i, (i - 1) % times) for i in range(times)]

    def third(whole, which):
        span = frames // 3 * length
        return lax.slice_in_dim(whole, which * span, (which + 1) * span, axis=2)

    late = third(samples, 2)
    before = lax.ppermute(late, "tm", onward)
    later, late = lax.optimization_barrier((samples, late))
    early = third(later, 0)
    after = lax.ppermute(early, "tm", backward)
    latest, early = lax.optimization_barrier((later, early))
    pieces = (early, third(latest, 1), late)
    keep = jnp.where(lax.axis_index("tm") == times - 1, 0.0, 1.0)
    keep = jnp.broadcast_to(keep.astype(jnp.float32), (inputs, LANES))
    table = split_table()
    rescale = 16.0 / math.sqrt(length)
    begun, outer_begun, factor, wide_taps, twist, early_far, late_far = own_blocks_call(
        pieces, taps, keep, scales, rescale, frames, near, far
    )
    far_after = lax.ppermute(early_far, "tm", backward)
    far_before = lax.ppermute(late_far, "tm", onward)
    middle, edge, outer_begun = middle_frames_call(
        (before, after), wide_taps, keep, twist, table, factor, begun, outer_begun, frames, near, far
    )
    words = outer_frames_call(
        (far_before, far_after), wide_taps, keep, twist, table, factor, middle, edge, outer_begun, frames, near, far
    )
    words = words.reshape(stations * times, inputs, LANES)
    words = lax.all_to_all(words, ("stn", "tm"), split_axis=0, concat_axis=0, tiled=True)
    words = words.reshape(stations, times, inputs, LANES)
    return correlate(words, 1.0 / (2.0 * frames * times * length))


def solution(mesh):
    placed = (P(None, "stn", "tm"), P(), P("stn", None))
    return jax.shard_map(
        body, mesh=mesh, in_specs=placed, out_specs=P(("stn", "tm"), None, None), check_vma=False
    )
```

```python
import functools
import math

import jax
import jax.numpy as jnp
import numpy as np
from jax import lax
from jax.experimental import pallas as pl
from jax.experimental.pallas import tpu as pltpu
from jax.sharding import PartitionSpec as P

LANES = 128
RADIX = 16
FINE = 256
KEPT = 128
SLOT = 16
VMEM_LIMIT = 28 * 2**20


def second_table():
    fine = np.arange(FINE)
    outputs = np.arange(KEPT) + (FINE - KEPT) // 2
    angle = 2.0 * np.pi * ((outputs[:, None] * fine[None, :]) % FINE) / FINE
    cosine, sine = np.cos(angle), np.sin(angle)
    return np.block([[cosine, sine], [-sine, cosine]]).T


def twist_table():
    angle = 2.0 * np.pi * (np.arange(RADIX)[:, None] * np.arange(FINE)[None, :]) / (RADIX * FINE)
    return np.stack([np.cos(angle), -np.sin(angle)]).astype(np.float32)


def add(a, b):
    return (a[0] + b[0], a[1] + b[1])


def sub(a, b):
    return (a[0] - b[0], a[1] - b[1])


def turn(a):
    return (a[1], -a[0])


def four(a, b, c, d):
    even, odd = add(a, c), sub(a, c)
    both, rest = add(b, d), turn(sub(b, d))
    return (add(even, both), add(odd, rest), sub(even, both), sub(odd, rest))


def times_root(a, power):
    if power == 0:
        return a
    if power == 4:
        return turn(a)
    half = math.sqrt(0.5)
    if power == 2:
        return ((a[0] + a[1]) * half, (a[1] - a[0]) * half)
    if power == 6:
        return ((a[1] - a[0]) * half, -(a[0] + a[1]) * half)
    cosine, sine = math.cos(2 * math.pi * power / 16), math.sin(2 * math.pi * power / 16)
    return (a[0] * cosine + a[1] * sine, a[1] * cosine - a[0] * sine)


def sixteen(points):
    columns = [four(points[b], points[4 + b], points[8 + b], points[12 + b]) for b in range(4)]
    out = [None] * 16
    for low in range(4):
        mixed = four(*[times_root(columns[b][low], b * low) for b in range(4)])
        for high in range(4):
            out[low + 4 * high] = mixed[high]
    return out


def filter_blocks(plan, fresh, sources, taps_ref, keep_ref, out_ref, begun_ref=None):
    tap_count, length = taps_ref.shape
    inputs = keep_ref.shape[0]
    window, first_later = sources

    def filter_chunk(chunk, _):
        lanes = pl.ds(pl.multiple_of(chunk * LANES, LANES), LANES)
        weights = taps_ref[:, lanes]
        taps = [jnp.broadcast_to(weights[p : p + 1], (inputs, LANES)) for p in range(tap_count)]
        keep = keep_ref[...]
        for comp in range(2):
            sums = {f: [None, None] for f in plan}
            if begun_ref is not None:
                sums = {f: [None, begun_ref[comp, chunk, slot]] for slot, f in enumerate(plan)}
            for v in fresh:
                users = [f for f in plan if f <= v < f + tap_count]
                if not users:
                    continue
                ref, u = window[v]
                at = pl.multiple_of(u * length + chunk * LANES, LANES)
                block = ref[comp, :, pl.ds(at, LANES)].astype(jnp.float32)
                for f in users:
                    later = int(begun_ref is not None or v >= first_later or f < first_later - tap_count + 1)
                    term = taps[v - f] * block
                    held = sums[f][later]
                    sums[f][later] = term if held is None else held + term
            for slot, f in enumerate(plan):
                early, late = sums[f]
                if early is not None:
                    early = early * keep
                    late = early if late is None else late + early
                out_ref[comp, chunk, slot] = late
        return 0

    lax.fori_loop(0, length // LANES, filter_chunk, 0, unroll=4)


def transform(used, slots, twist_ref, table_ref, factor_ref, filt, rows, store):
    inputs = factor_ref.shape[1]

    def first_transform(slot, _):
        for half in range(2):
            points = [(filt[0, 2 * n + half, slot], filt[1, 2 * n + half, slot]) for n in range(RADIX)]
            mixed = sixteen(points)
            for k1 in range(RADIX):
                real, imag = mixed[k1]
                if k1:
                    cosine = twist_ref[0, pl.ds(k1, 1), pl.ds(half * LANES, LANES)]
                    sine = twist_ref[1, pl.ds(k1, 1), pl.ds(half * LANES, LANES)]
                    real, imag = real * cosine - imag * sine, imag * cosine + real * sine
                at = pl.ds(pl.multiple_of((k1 * slots + slot) * inputs, inputs), inputs)
                rows[half, at, :] = real
                rows[2 + half, at, :] = imag
        return 0

    lax.fori_loop(0, used, first_transform, 0, unroll=True)
    for slot in range(used, slots):
        for q in range(4):
            for k1 in range(RADIX):
                at = (k1 * slots + slot) * inputs
                rows[q, at : at + inputs, :] = jnp.zeros((inputs, LANES), jnp.float32)

    some = 8
    count = some * slots * inputs
    for first in range(0, RADIX, some):
        span = slice(first * slots * inputs, first * slots * inputs + count)
        block = jnp.concatenate([rows[q, span, :] for q in range(4)], axis=1)
        high = block.astype(jnp.bfloat16)
        low = (block - high.astype(jnp.float32)).astype(jnp.bfloat16)
        both = jnp.dot(high, table_ref[...], preferred_element_type=jnp.float32)
        rest = jnp.dot(low, table_ref[:, : 2 * KEPT], preferred_element_type=jnp.float32)
        total = both[:, : 2 * KEPT] + both[:, 2 * KEPT :] + rest
        scale = factor_ref[first : first + some][:, None]
        for comp in range(2):
            part = total[:, comp * KEPT : (comp + 1) * KEPT].reshape(some, slots, inputs, KEPT)
            part = jnp.clip(part * scale, -127.0, 127.0)
            store(comp, slice(first, first + some), part.reshape(some, slots * inputs, KEPT))


def split_frames(frames, near, far):
    middle = range(far[0], far[0] + near[0] + near[1])
    return list(middle), [f for f in range(frames) if f not in middle]


def window_of(frames, near, far, refs):
    counts = (far[0], near[0], near[1], frames - near[0] - near[1], near[0], near[1], far[1])
    window = [(ref, u) for ref, count in zip(refs, counts) for u in range(count)]
    return window, far[0] + near[0] + frames


def given(window):
    return [v for v, (ref, _) in enumerate(window) if ref is not None]


def own_kernel(
    frames, near, far, rescale, early_ref, between_ref, late_ref, taps_ref, keep_ref, scales_ref, order_ref, twist_ref,
    middle_ref, outer_ref, factor_ref, wide_taps_ref, same_twist_ref, early_far_ref, late_far_ref,
):
    inputs = scales_ref.shape[0]
    blocks = scales_ref.shape[1] // LANES
    part = LANES // blocks
    values = scales_ref[...].astype(jnp.float32) * rescale
    stacked = jnp.concatenate([values[:, b * LANES : (b + 1) * LANES] for b in range(blocks)], axis=0)
    stacked = jnp.dot(stacked.astype(jnp.bfloat16), order_ref[...], preferred_element_type=jnp.float32)
    held = [stacked[b * inputs : (b + 1) * inputs] for b in range(blocks)]
    lane = lax.broadcasted_iota(jnp.int32, (inputs, LANES), 1)
    bit = 1
    while bit < blocks:
        shift = bit * part
        left = (lane // shift) % 2 == 0
        for b in range(blocks):
            if not b & bit:
                x, y = held[b], held[b | bit]
                held[b] = jnp.where(left, x, pltpu.roll(y, shift, 1))
                held[b | bit] = jnp.where(left, pltpu.roll(x, LANES - shift, 1), y)
        bit *= 2
    for k1 in range(blocks):
        factor_ref[k1] = held[k1]
    wide_taps_ref[...] = taps_ref[...].astype(jnp.float32)
    same_twist_ref[...] = twist_ref[...]
    cut = early_far_ref.shape[2]
    early_far_ref[...] = between_ref[:, :, :cut]
    late_far_ref[...] = between_ref[:, :, cut:]

    own = (early_ref, between_ref, late_ref)
    sources = window_of(frames, near, far, (None, None, *own, None, None))
    for plan, out_ref in zip(split_frames(frames, near, far), (middle_ref, outer_ref)):
        filter_blocks(plan, given(sources[0]), sources, wide_taps_ref, keep_ref, out_ref)


def middle_kernel(
    frames, near, far, after_ref, before_ref, taps_ref, keep_ref, twist_ref, table_ref, factor_ref, begun_ref,
    outer_begun_ref, out_ref, edge_ref, outer_ref, filt, rows,
):
    sources = window_of(frames, near, far, (None, before_ref) + (None,) * 3 + (after_ref, None))
    middle, outer = split_frames(frames, near, far)
    fresh = given(sources[0])
    inputs = factor_ref.shape[1]

    def store(comp, some, part):
        out_ref[comp, some] = part[:, : 8 * inputs]
        edge_ref[comp, some] = part[:, 8 * inputs :]

    filter_blocks(middle, fresh, sources, taps_ref, keep_ref, filt, begun_ref)
    transform(len(middle), len(middle), twist_ref, table_ref, factor_ref, filt, rows, store)
    filter_blocks(outer, fresh, sources, taps_ref, keep_ref, outer_ref, outer_begun_ref)


def outer_kernel(
    frames, near, far, after_ref, before_ref, taps_ref, keep_ref, twist_ref, table_ref, factor_ref, middle_ref,
    edge_ref, begun_ref, out_ref, filt, rows, edge, first_words, second_words,
):
    sources = window_of(frames, near, far, (before_ref,) + (None,) * 5 + (after_ref,))
    middle, plan = split_frames(frames, near, far)
    inputs = factor_ref.shape[1]
    taken = (len(middle) - 8) * inputs
    edge[:, :, :taken] = edge_ref[...]

    def store(comp, some, part):
        edge[comp, some, taken:] = part
        if comp == 1:
            arrange(some.start // 8, (first_words, second_words)[some.start // 8])

    def arrange(pair, words):
        for high in range(2):
            for i in range(inputs):
                parts = []
                for comp in range(2):
                    for channel in range(4):
                        k1 = (pair * 2 + high) * 4 + channel
                        for half in (middle_ref, edge):
                            parts.append(half[comp, k1, pl.ds(i, 8, stride=inputs), :])
                turned = jnp.concatenate(parts, axis=0).T
                words[pl.ds(high * inputs + i, KEPT, stride=2 * inputs), :] = turned
        narrow = words[...].reshape(KEPT, 2 * inputs, LANES).astype(jnp.bfloat16)
        out_ref[:, pair * 2 * inputs : (pair + 1) * 2 * inputs, :] = narrow

    filter_blocks(plan, given(sources[0]), sources, taps_ref, keep_ref, filt, begun_ref)
    transform(len(plan), SLOT - len(middle), twist_ref, table_ref, factor_ref, filt, rows, store)


def split_table():
    table = second_table()
    high = table.astype(jnp.bfloat16)
    low = (table - high.astype(np.float64)).astype(jnp.bfloat16)
    return jnp.concatenate([high, low], axis=1)


def scratch(inputs, slots):
    return [
        pltpu.VMEM((2, RADIX * FINE // LANES, slots, inputs, LANES), jnp.float32),
        pltpu.VMEM((4, RADIX * slots * inputs, LANES), jnp.float32),
    ]


VMEM = pl.BlockSpec(memory_space=pltpu.VMEM)


def sums_shape(count, chunks, inputs):
    return jax.ShapeDtypeStruct((2, chunks, count, inputs, LANES), jnp.float32)


def lane_order():
    part = LANES // RADIX
    order = np.zeros((LANES, LANES))
    for m in range(part):
        for k1 in range(RADIX):
            order[m * RADIX + k1, k1 * part + m] = 1.0
    return order.astype(jnp.bfloat16)


def own_blocks_call(pieces, taps, keep, scales, rescale, frames, near, far):
    inputs = pieces[0].shape[1]
    chunks = taps.shape[1] // LANES
    twist = twist_table()
    middle, outer = split_frames(frames, near, far)
    return pl.pallas_call(
        functools.partial(own_kernel, frames, near, far, rescale),
        out_shape=(
            sums_shape(len(middle), chunks, inputs),
            sums_shape(len(outer), chunks, inputs),
            jax.ShapeDtypeStruct((RADIX, inputs, KEPT), jnp.float32),
            jax.ShapeDtypeStruct(taps.shape, jnp.float32),
            jax.ShapeDtypeStruct(twist.shape, jnp.float32),
            jax.ShapeDtypeStruct((2, inputs, far[1] * taps.shape[1]), pieces[0].dtype),
            jax.ShapeDtypeStruct((2, inputs, far[0] * taps.shape[1]), pieces[0].dtype),
        ),
        in_specs=[VMEM] * 8,
        out_specs=(VMEM,) * 7,
        compiler_params=pltpu.CompilerParams(vmem_limit_bytes=VMEM_LIMIT),
        cost_estimate=pl.CostEstimate(flops=3 * 10**9, bytes_accessed=6 * 2**20, transcendentals=0),
        name="own_blocks",
    )(*pieces, taps, keep, scales, lane_order(), twist)


def middle_frames_call(near_blocks, taps, keep, twist, table, factor, begun, outer_begun, frames, near, far):
    inputs = near_blocks[0].shape[1]
    count = near[0] + near[1]
    return pl.pallas_call(
        functools.partial(middle_kernel, frames, near, far),
        out_shape=(
            jax.ShapeDtypeStruct((2, RADIX, 8 * inputs, KEPT), jnp.float32),
            jax.ShapeDtypeStruct((2, RADIX, (count - 8) * inputs, KEPT), jnp.float32),
            jax.ShapeDtypeStruct(outer_begun.shape, jnp.float32),
        ),
        in_specs=[VMEM] * 9,
        out_specs=(VMEM,) * 3,
        scratch_shapes=scratch(inputs, count),
        compiler_params=pltpu.CompilerParams(vmem_limit_bytes=VMEM_LIMIT),
        cost_estimate=pl.CostEstimate(flops=3 * 10**9, bytes_accessed=5 * 2**20, transcendentals=0),
        name="middle_frames",
    )(*near_blocks, taps, keep, twist, table, factor, begun, outer_begun)


def outer_frames_call(far_blocks, taps, keep, twist, table, factor, middle, edge, begun, frames, near, far):
    inputs = far_blocks[0].shape[1]
    return pl.pallas_call(
        functools.partial(outer_kernel, frames, near, far),
        out_shape=jax.ShapeDtypeStruct((KEPT, 4 * inputs, LANES), jnp.bfloat16),
        in_specs=[VMEM] * 10,
        out_specs=VMEM,
        scratch_shapes=scratch(inputs, SLOT - near[0] - near[1])
        + [pltpu.VMEM((2, RADIX, 8 * inputs, KEPT), jnp.float32)]
        + [pltpu.VMEM((KEPT * 2 * inputs, LANES), jnp.float32)] * 2,
        compiler_params=pltpu.CompilerParams(vmem_limit_bytes=VMEM_LIMIT),
        name="outer_frames",
    )(*far_blocks, taps, keep, twist, table, factor, middle, edge, begun)


def correlate_kernel(normalizer, words_ref, out_ref, joined, swapped, result, sems):
    stations, times, inputs, _ = words_ref.shape
    size = stations * inputs
    half = size // 2

    lane = lax.broadcasted_iota(jnp.int32, (size, LANES), 1)
    sign = jnp.where(lane < LANES // 2, 1.0, -1.0).astype(jnp.bfloat16)

    for q in range(times // 4):
        held = [words_ref[:, 4 * q + r].astype(jnp.float32).reshape(size, LANES).astype(jnp.bfloat16) for r in range(4)]
        for bit in (1, 2):
            shift = bit * SLOT
            left = (lane // shift) % 2 == 0
            for r in range(4):
                if not r & bit:
                    x, y = held[r], held[r | bit]
                    held[r] = jnp.where(left, x, pltpu.roll(y, shift, 1))
                    held[r | bit] = jnp.where(left, pltpu.roll(x, LANES - shift, 1), y)
        for c in range(4):
            lanes = slice(q * LANES, (q + 1) * LANES)
            joined[c, :, lanes] = held[c]
            swapped[c, :, lanes] = pltpu.roll(held[c], LANES // 2, 1) * sign

    def product(left, right):
        return lax.dot_general(
            left, right, (((1,), (1,)), ((), ())), preferred_element_type=jnp.float32
        )

    def finish(values):
        return (values * normalizer).astype(jnp.bfloat16)

    lower = lax.broadcasted_iota(jnp.int32, (half, half), 0) >= lax.broadcasted_iota(
        jnp.int32, (half, half), 1
    )
    copies = []
    for channel in range(4):
        first, second = joined[channel, :half], joined[channel, half:]
        first_other, second_other = swapped[channel, :half], swapped[channel, half:]
        result[channel, :half, :half] = finish(jnp.where(lower, product(first, first), product(first_other, first)))
        result[channel, half:, :half] = finish(product(second, first))
        result[channel, :half, half:] = finish(product(first_other, second))
        result[channel, half:, half:] = finish(
            jnp.where(lower, product(second, second), product(second_other, second))
        )
        copies.append(pltpu.make_async_copy(result.at[channel], out_ref.at[channel], sems.at[channel]))
        copies[-1].start()
    for copy in copies:
        copy.wait()


def correlate(words, normalizer):
    stations, times, inputs, _ = words.shape
    size = stations * inputs
    return pl.pallas_call(
        functools.partial(correlate_kernel, normalizer),
        out_shape=jax.ShapeDtypeStruct((4, size, size), jnp.bfloat16),
        in_specs=[VMEM],
        out_specs=pl.BlockSpec(memory_space=pltpu.HBM),
        scratch_shapes=[pltpu.VMEM((4, size, times * 2 * SLOT), jnp.bfloat16)] * 2
        + [pltpu.VMEM((4, size, size), jnp.bfloat16), pltpu.SemaphoreType.DMA((4,))],
        compiler_params=pltpu.CompilerParams(vmem_limit_bytes=VMEM_LIMIT),
        name="correlate",
    )(words)


def body(samples, taps, scales):
    length = taps.shape[1]
    inputs = samples.shape[1]
    frames = samples.shape[2] // length
    stations, times = lax.axis_size("stn"), lax.axis_size("tm")
    near, far = (5, 5), (3, 2)
    onward = [(i, i + 1) for i in range(times - 1)]
    backward = [(i, (i - 1) % times) for i in range(times)]

    def third(whole, which):
        span = frames // 3 * length
        return lax.slice_in_dim(whole, which * span, (which + 1) * span, axis=2)

    early = third(samples, 0)
    after = lax.ppermute(early, "tm", backward)
    later, early = lax.optimization_barrier((samples, early))
    late = third(later, 2)
    before = lax.ppermute(late, "tm", onward)
    latest, late = lax.optimization_barrier((later, late))
    pieces = (early, third(latest, 1), late)
    keep = jnp.where(lax.axis_index("tm") == times - 1, 0.0, 1.0)
    keep = jnp.broadcast_to(keep.astype(jnp.float32), (inputs, LANES))
    table = split_table()
    rescale = 16.0 / math.sqrt(length)
    begun, outer_begun, factor, wide_taps, twist, early_far, late_far = own_blocks_call(
        pieces, taps, keep, scales, rescale, frames, near, far
    )
    far_after = lax.ppermute(early_far, "tm", backward)
    far_before = lax.ppermute(late_far, "tm", onward)
    middle, edge, outer_begun = middle_frames_call(
        (after, before), wide_taps, keep, twist, table, factor, begun, outer_begun, frames, near, far
    )
    words = outer_frames_call(
        (far_after, far_before), wide_taps, keep, twist, table, factor, middle, edge, outer_begun, frames, near, far
    )
    words = words.reshape(stations * times, inputs, LANES)
    words = lax.all_to_all(words, ("stn", "tm"), split_axis=0, concat_axis=0, tiled=True)
    words = words.reshape(stations, times, inputs, LANES)
    return correlate(words, 1.0 / (2.0 * frames * times * length))


def solution(mesh):
    placed = (P(None, "stn", "tm"), P(), P("stn", None))
    return jax.shard_map(
        body, mesh=mesh, in_specs=placed, out_specs=P(("stn", "tm"), None, None), check_vma=False
    )
```

```python
import functools
import math

import jax
import jax.numpy as jnp
import numpy as np
from jax import lax
from jax.experimental import pallas as pl
from jax.experimental.pallas import tpu as pltpu
from jax.sharding import PartitionSpec as P

LANES = 128
RADIX = 16
FINE = 256
KEPT = 128
SLOT = 16
VMEM_LIMIT = 28 * 2**20


def second_table():
    fine = np.arange(FINE)
    outputs = np.arange(KEPT) + (FINE - KEPT) // 2
    angle = 2.0 * np.pi * ((outputs[:, None] * fine[None, :]) % FINE) / FINE
    cosine, sine = np.cos(angle), np.sin(angle)
    return np.block([[cosine, sine], [-sine, cosine]]).T


def twist_table():
    angle = 2.0 * np.pi * (np.arange(RADIX)[:, None] * np.arange(FINE)[None, :]) / (RADIX * FINE)
    return np.stack([np.cos(angle), -np.sin(angle)]).astype(np.float32)


def add(a, b):
    return (a[0] + b[0], a[1] + b[1])


def sub(a, b):
    return (a[0] - b[0], a[1] - b[1])


def turn(a):
    return (a[1], -a[0])


def four(a, b, c, d):
    even, odd = add(a, c), sub(a, c)
    both, rest = add(b, d), turn(sub(b, d))
    return (add(even, both), add(odd, rest), sub(even, both), sub(odd, rest))


def times_root(a, power):
    if power == 0:
        return a
    if power == 4:
        return turn(a)
    half = math.sqrt(0.5)
    if power == 2:
        return ((a[0] + a[1]) * half, (a[1] - a[0]) * half)
    if power == 6:
        return ((a[1] - a[0]) * half, -(a[0] + a[1]) * half)
    cosine, sine = math.cos(2 * math.pi * power / 16), math.sin(2 * math.pi * power / 16)
    return (a[0] * cosine + a[1] * sine, a[1] * cosine - a[0] * sine)


def sixteen(points):
    columns = [four(points[b], points[4 + b], points[8 + b], points[12 + b]) for b in range(4)]
    out = [None] * 16
    for low in range(4):
        mixed = four(*[times_root(columns[b][low], b * low) for b in range(4)])
        for high in range(4):
            out[low + 4 * high] = mixed[high]
    return out


def filter_blocks(plan, fresh, sources, taps_ref, keep_ref, out_ref, begun_ref=None):
    tap_count, length = taps_ref.shape
    inputs = keep_ref.shape[0]
    window, first_later = sources

    def filter_chunk(chunk, _):
        lanes = pl.ds(pl.multiple_of(chunk * LANES, LANES), LANES)
        weights = taps_ref[:, lanes]
        taps = [jnp.broadcast_to(weights[p : p + 1], (inputs, LANES)) for p in range(tap_count)]
        keep = keep_ref[...]
        for comp in range(2):
            sums = {f: [None, None] for f in plan}
            if begun_ref is not None:
                sums = {f: [None, begun_ref[comp, chunk, slot]] for slot, f in enumerate(plan)}
            for v in fresh:
                users = [f for f in plan if f <= v < f + tap_count]
                if not users:
                    continue
                ref, u = window[v]
                at = pl.multiple_of(u * length + chunk * LANES, LANES)
                block = ref[comp, :, pl.ds(at, LANES)].astype(jnp.float32)
                for f in users:
                    later = int(begun_ref is not None or v >= first_later or f < first_later - tap_count + 1)
                    term = taps[v - f] * block
                    held = sums[f][later]
                    sums[f][later] = term if held is None else held + term
            for slot, f in enumerate(plan):
                early, late = sums[f]
                if early is not None:
                    early = early * keep
                    late = early if late is None else late + early
                out_ref[comp, chunk, slot] = late
        return 0

    lax.fori_loop(0, length // LANES, filter_chunk, 0, unroll=4)


def transform(used, slots, twist_ref, table_ref, factor_ref, filt, rows, store):
    inputs = factor_ref.shape[1]

    def first_transform(slot, _):
        for half in range(2):
            points = [(filt[0, 2 * n + half, slot], filt[1, 2 * n + half, slot]) for n in range(RADIX)]
            mixed = sixteen(points)
            for k1 in range(RADIX):
                real, imag = mixed[k1]
                if k1:
                    cosine = twist_ref[0, pl.ds(k1, 1), pl.ds(half * LANES, LANES)]
                    sine = twist_ref[1, pl.ds(k1, 1), pl.ds(half * LANES, LANES)]
                    real, imag = real * cosine - imag * sine, imag * cosine + real * sine
                at = pl.ds(pl.multiple_of((k1 * slots + slot) * inputs, inputs), inputs)
                rows[half, at, :] = real
                rows[2 + half, at, :] = imag
        return 0

    lax.fori_loop(0, used, first_transform, 0, unroll=True)
    for slot in range(used, slots):
        for q in range(4):
            for k1 in range(RADIX):
                at = (k1 * slots + slot) * inputs
                rows[q, at : at + inputs, :] = jnp.zeros((inputs, LANES), jnp.float32)

    some = 8
    count = some * slots * inputs
    for first in range(0, RADIX, some):
        span = slice(first * slots * inputs, first * slots * inputs + count)
        block = jnp.concatenate([rows[q, span, :] for q in range(4)], axis=1)
        high = block.astype(jnp.bfloat16)
        low = (block - high.astype(jnp.float32)).astype(jnp.bfloat16)
        both = jnp.dot(high, table_ref[...], preferred_element_type=jnp.float32)
        rest = jnp.dot(low, table_ref[:, : 2 * KEPT], preferred_element_type=jnp.float32)
        total = both[:, : 2 * KEPT] + both[:, 2 * KEPT :] + rest
        scale = factor_ref[first : first + some][:, None]
        for comp in range(2):
            part = total[:, comp * KEPT : (comp + 1) * KEPT].reshape(some, slots, inputs, KEPT)
            part = jnp.clip(part * scale, -127.0, 127.0)
            store(comp, slice(first, first + some), part.reshape(some, slots * inputs, KEPT))


def split_frames(frames, near, far):
    middle = range(far[0], far[0] + near[0] + near[1])
    return list(middle), [f for f in range(frames) if f not in middle]


def window_of(frames, near, far, refs):
    counts = (far[0], near[0], near[1], frames - near[0] - near[1], near[0], near[1], far[1])
    window = [(ref, u) for ref, count in zip(refs, counts) for u in range(count)]
    return window, far[0] + near[0] + frames


def given(window):
    return [v for v, (ref, _) in enumerate(window) if ref is not None]


def own_kernel(
    frames, near, far, rescale, early_ref, between_ref, late_ref, taps_ref, keep_ref, scales_ref, order_ref, twist_ref,
    middle_ref, outer_ref, factor_ref, wide_taps_ref, same_twist_ref, early_far_ref, late_far_ref,
):
    inputs = scales_ref.shape[0]
    blocks = scales_ref.shape[1] // LANES
    part = LANES // blocks
    values = scales_ref[...].astype(jnp.float32) * rescale
    stacked = jnp.concatenate([values[:, b * LANES : (b + 1) * LANES] for b in range(blocks)], axis=0)
    stacked = jnp.dot(stacked.astype(jnp.bfloat16), order_ref[...], preferred_element_type=jnp.float32)
    held = [stacked[b * inputs : (b + 1) * inputs] for b in range(blocks)]
    lane = lax.broadcasted_iota(jnp.int32, (inputs, LANES), 1)
    bit = 1
    while bit < blocks:
        shift = bit * part
        left = (lane // shift) % 2 == 0
        for b in range(blocks):
            if not b & bit:
                x, y = held[b], held[b | bit]
                held[b] = jnp.where(left, x, pltpu.roll(y, shift, 1))
                held[b | bit] = jnp.where(left, pltpu.roll(x, LANES - shift, 1), y)
        bit *= 2
    for k1 in range(blocks):
        factor_ref[k1] = held[k1]
    wide_taps_ref[...] = taps_ref[...].astype(jnp.float32)
    same_twist_ref[...] = twist_ref[...]
    cut = early_far_ref.shape[2]
    early_far_ref[...] = between_ref[:, :, :cut]
    late_far_ref[...] = between_ref[:, :, cut:]

    own = (early_ref, between_ref, late_ref)
    sources = window_of(frames, near, far, (None, None, *own, None, None))
    for plan, out_ref in zip(split_frames(frames, near, far), (middle_ref, outer_ref)):
        filter_blocks(plan, given(sources[0]), sources, wide_taps_ref, keep_ref, out_ref)


def middle_kernel(
    frames, near, far, before_ref, after_ref, taps_ref, keep_ref, twist_ref, table_ref, factor_ref, begun_ref,
    outer_begun_ref, out_ref, edge_ref, outer_ref, filt, rows,
):
    sources = window_of(frames, near, far, (None, before_ref) + (None,) * 3 + (after_ref, None))
    middle, outer = split_frames(frames, near, far)
    fresh = given(sources[0])
    inputs = factor_ref.shape[1]

    def store(comp, some, part):
        out_ref[comp, some] = part[:, : 8 * inputs]
        edge_ref[comp, some] = part[:, 8 * inputs :]

    filter_blocks(middle, fresh, sources, taps_ref, keep_ref, filt, begun_ref)
    transform(len(middle), len(middle), twist_ref, table_ref, factor_ref, filt, rows, store)
    filter_blocks(outer, fresh, sources, taps_ref, keep_ref, outer_ref, outer_begun_ref)


def outer_kernel(
    frames, near, far, after_ref, before_ref, taps_ref, keep_ref, twist_ref, table_ref, factor_ref, middle_ref,
    edge_ref, begun_ref, out_ref, filt, rows, edge, first_words, second_words,
):
    sources = window_of(frames, near, far, (before_ref,) + (None,) * 5 + (after_ref,))
    middle, plan = split_frames(frames, near, far)
    inputs = factor_ref.shape[1]
    taken = (len(middle) - 8) * inputs
    edge[:, :, :taken] = edge_ref[...]

    def store(comp, some, part):
        edge[comp, some, taken:] = part
        if comp == 1:
            arrange(some.start // 8, (first_words, second_words)[some.start // 8])

    def arrange(pair, words):
        for high in range(2):
            for i in range(inputs):
                parts = []
                for comp in range(2):
                    for channel in range(4):
                        k1 = (pair * 2 + high) * 4 + channel
                        for half in (middle_ref, edge):
                            parts.append(half[comp, k1, pl.ds(i, 8, stride=inputs), :])
                turned = jnp.concatenate(parts, axis=0).T
                words[pl.ds(high * inputs + i, KEPT, stride=2 * inputs), :] = turned
        narrow = words[...].reshape(KEPT, 2 * inputs, LANES).astype(jnp.bfloat16)
        out_ref[:, pair * 2 * inputs : (pair + 1) * 2 * inputs, :] = narrow

    filter_blocks(plan, given(sources[0]), sources, taps_ref, keep_ref, filt, begun_ref)
    transform(len(plan), SLOT - len(middle), twist_ref, table_ref, factor_ref, filt, rows, store)


def split_table():
    table = second_table()
    high = table.astype(jnp.bfloat16)
    low = (table - high.astype(np.float64)).astype(jnp.bfloat16)
    return jnp.concatenate([high, low], axis=1)


def scratch(inputs, slots):
    return [
        pltpu.VMEM((2, RADIX * FINE // LANES, slots, inputs, LANES), jnp.float32),
        pltpu.VMEM((4, RADIX * slots * inputs, LANES), jnp.float32),
    ]


VMEM = pl.BlockSpec(memory_space=pltpu.VMEM)


def sums_shape(count, chunks, inputs):
    return jax.ShapeDtypeStruct((2, chunks, count, inputs, LANES), jnp.float32)


def lane_order():
    part = LANES // RADIX
    order = np.zeros((LANES, LANES))
    for m in range(part):
        for k1 in range(RADIX):
            order[m * RADIX + k1, k1 * part + m] = 1.0
    return order.astype(jnp.bfloat16)


def own_blocks_call(pieces, taps, keep, scales, rescale, frames, near, far):
    inputs = pieces[0].shape[1]
    chunks = taps.shape[1] // LANES
    twist = twist_table()
    middle, outer = split_frames(frames, near, far)
    return pl.pallas_call(
        functools.partial(own_kernel, frames, near, far, rescale),
        out_shape=(
            sums_shape(len(middle), chunks, inputs),
            sums_shape(len(outer), chunks, inputs),
            jax.ShapeDtypeStruct((RADIX, inputs, KEPT), jnp.float32),
            jax.ShapeDtypeStruct(taps.shape, jnp.float32),
            jax.ShapeDtypeStruct(twist.shape, jnp.float32),
            jax.ShapeDtypeStruct((2, inputs, far[1] * taps.shape[1]), pieces[0].dtype),
            jax.ShapeDtypeStruct((2, inputs, far[0] * taps.shape[1]), pieces[0].dtype),
        ),
        in_specs=[VMEM] * 8,
        out_specs=(VMEM,) * 7,
        compiler_params=pltpu.CompilerParams(vmem_limit_bytes=VMEM_LIMIT),
        cost_estimate=pl.CostEstimate(flops=3 * 10**9, bytes_accessed=6 * 2**20, transcendentals=0),
        name="own_blocks",
    )(*pieces, taps, keep, scales, lane_order(), twist)


def middle_frames_call(near_blocks, taps, keep, twist, table, factor, begun, outer_begun, frames, near, far):
    inputs = near_blocks[0].shape[1]
    count = near[0] + near[1]
    return pl.pallas_call(
        functools.partial(middle_kernel, frames, near, far),
        out_shape=(
            jax.ShapeDtypeStruct((2, RADIX, 8 * inputs, KEPT), jnp.float32),
            jax.ShapeDtypeStruct((2, RADIX, (count - 8) * inputs, KEPT), jnp.float32),
            jax.ShapeDtypeStruct(outer_begun.shape, jnp.float32),
        ),
        in_specs=[VMEM] * 9,
        out_specs=(VMEM,) * 3,
        scratch_shapes=scratch(inputs, count),
        compiler_params=pltpu.CompilerParams(vmem_limit_bytes=VMEM_LIMIT),
        cost_estimate=pl.CostEstimate(flops=3 * 10**9, bytes_accessed=5 * 2**20, transcendentals=0),
        name="middle_frames",
    )(*near_blocks, taps, keep, twist, table, factor, begun, outer_begun)


def outer_frames_call(far_blocks, taps, keep, twist, table, factor, middle, edge, begun, frames, near, far):
    inputs = far_blocks[0].shape[1]
    return pl.pallas_call(
        functools.partial(outer_kernel, frames, near, far),
        out_shape=jax.ShapeDtypeStruct((KEPT, 4 * inputs, LANES), jnp.bfloat16),
        in_specs=[VMEM] * 10,
        out_specs=VMEM,
        scratch_shapes=scratch(inputs, SLOT - near[0] - near[1])
        + [pltpu.VMEM((2, RADIX, 8 * inputs, KEPT), jnp.float32)]
        + [pltpu.VMEM((KEPT * 2 * inputs, LANES), jnp.float32)] * 2,
        compiler_params=pltpu.CompilerParams(vmem_limit_bytes=VMEM_LIMIT),
        name="outer_frames",
    )(*far_blocks, taps, keep, twist, table, factor, middle, edge, begun)


def cut_kernel(spans, in_ref, *refs):
    outs, sems = refs[:-1], refs[-1]
    copies = [
        pltpu.make_async_copy(in_ref.at[:, :, start:stop], out, sems.at[i])
        for i, ((start, stop), out) in enumerate(zip(spans, outs))
    ]
    for copy in copies:
        copy.start()
    for copy in copies:
        copy.wait()


def cut_pieces(samples, near, frames, length):
    spans = [(0, near[1] * length), ((frames - near[0]) * length, frames * length)]
    early, late = pl.pallas_call(
        functools.partial(cut_kernel, spans),
        out_shape=[jax.ShapeDtypeStruct(samples.shape[:2] + (b - a,), samples.dtype) for a, b in spans],
        in_specs=[pl.BlockSpec(memory_space=pltpu.HBM)],
        out_specs=[VMEM] * 2,
        scratch_shapes=[pltpu.SemaphoreType.DMA((2,))],
        compiler_params=pltpu.CompilerParams(vmem_limit_bytes=VMEM_LIMIT),
        name="cut",
    )(pltpu.with_memory_space_constraint(samples, pltpu.HBM))
    return late, early, lax.slice_in_dim(samples, spans[0][1], spans[1][0], axis=2)


def correlate_kernel(normalizer, words_ref, out_ref, joined, swapped, result, sems):
    stations, times, inputs, _ = words_ref.shape
    size = stations * inputs
    half = size // 2

    lane = lax.broadcasted_iota(jnp.int32, (size, LANES), 1)
    sign = jnp.where(lane < LANES // 2, 1.0, -1.0).astype(jnp.bfloat16)

    for q in range(times // 4):
        held = [words_ref[:, 4 * q + r].astype(jnp.float32).reshape(size, LANES).astype(jnp.bfloat16) for r in range(4)]
        for bit in (1, 2):
            shift = bit * SLOT
            left = (lane // shift) % 2 == 0
            for r in range(4):
                if not r & bit:
                    x, y = held[r], held[r | bit]
                    held[r] = jnp.where(left, x, pltpu.roll(y, shift, 1))
                    held[r | bit] = jnp.where(left, pltpu.roll(x, LANES - shift, 1), y)
        for c in range(4):
            lanes = slice(q * LANES, (q + 1) * LANES)
            joined[c, :, lanes] = held[c]
            swapped[c, :, lanes] = pltpu.roll(held[c], LANES // 2, 1) * sign

    def product(left, right):
        return lax.dot_general(
            left, right, (((1,), (1,)), ((), ())), preferred_element_type=jnp.float32
        )

    def finish(values):
        return (values * normalizer).astype(jnp.bfloat16)

    lower = lax.broadcasted_iota(jnp.int32, (half, half), 0) >= lax.broadcasted_iota(
        jnp.int32, (half, half), 1
    )
    copies = []
    for channel in range(4):
        first, second = joined[channel, :half], joined[channel, half:]
        first_other, second_other = swapped[channel, :half], swapped[channel, half:]
        result[channel, :half, :half] = finish(jnp.where(lower, product(first, first), product(first_other, first)))
        result[channel, half:, :half] = finish(product(second, first))
        result[channel, :half, half:] = finish(product(first_other, second))
        result[channel, half:, half:] = finish(
            jnp.where(lower, product(second, second), product(second_other, second))
        )
        copies.append(pltpu.make_async_copy(result.at[channel], out_ref.at[channel], sems.at[channel]))
        copies[-1].start()
    for copy in copies:
        copy.wait()


def correlate(words, normalizer):
    stations, times, inputs, _ = words.shape
    size = stations * inputs
    return pl.pallas_call(
        functools.partial(correlate_kernel, normalizer),
        out_shape=jax.ShapeDtypeStruct((4, size, size), jnp.bfloat16),
        in_specs=[VMEM],
        out_specs=pl.BlockSpec(memory_space=pltpu.HBM),
        scratch_shapes=[pltpu.VMEM((4, size, times * 2 * SLOT), jnp.bfloat16)] * 2
        + [pltpu.VMEM((4, size, size), jnp.bfloat16), pltpu.SemaphoreType.DMA((4,))],
        compiler_params=pltpu.CompilerParams(vmem_limit_bytes=VMEM_LIMIT),
        name="correlate",
    )(words)


def body(samples, taps, scales):
    length = taps.shape[1]
    inputs = samples.shape[1]
    frames = samples.shape[2] // length
    stations, times = lax.axis_size("stn"), lax.axis_size("tm")
    near, far = (5, 5), (3, 2)
    onward = [(i, i + 1) for i in range(times - 1)]
    backward = [(i, (i - 1) % times) for i in range(times)]

    late, early, between = cut_pieces(samples, near, frames, length)
    before = lax.ppermute(late, "tm", onward)
    after = lax.ppermute(early, "tm", backward)
    pieces = (early, between, late)
    keep = jnp.where(lax.axis_index("tm") == times - 1, 0.0, 1.0)
    keep = jnp.broadcast_to(keep.astype(jnp.float32), (inputs, LANES))
    table = split_table()
    rescale = 16.0 / math.sqrt(length)
    begun, outer_begun, factor, wide_taps, twist, early_far, late_far = own_blocks_call(
        pieces, taps, keep, scales, rescale, frames, near, far
    )
    far_after = lax.ppermute(early_far, "tm", backward)
    far_before = lax.ppermute(late_far, "tm", onward)
    middle, edge, outer_begun = middle_frames_call(
        (before, after), wide_taps, keep, twist, table, factor, begun, outer_begun, frames, near, far
    )
    words = outer_frames_call(
        (far_after, far_before), wide_taps, keep, twist, table, factor, middle, edge, outer_begun, frames, near, far
    )
    words = words.reshape(stations * times, inputs, LANES)
    words = lax.all_to_all(words, ("stn", "tm"), split_axis=0, concat_axis=0, tiled=True)
    words = words.reshape(stations, times, inputs, LANES)
    return correlate(words, 1.0 / (2.0 * frames * times * length))


def solution(mesh):
    placed = (P(None, "stn", "tm"), P(), P("stn", None))
    return jax.shard_map(
        body, mesh=mesh, in_specs=placed, out_specs=P(("stn", "tm"), None, None), check_vma=False
    )
```

```python
import functools
import math

import jax
import jax.numpy as jnp
import numpy as np
from jax import lax
from jax.experimental import pallas as pl
from jax.experimental.pallas import tpu as pltpu
from jax.sharding import PartitionSpec as P

LANES = 128
RADIX = 16
FINE = 256
KEPT = 128
SLOT = 16
VMEM_LIMIT = 28 * 2**20


def second_table():
    fine = np.arange(FINE)
    outputs = np.arange(KEPT) + (FINE - KEPT) // 2
    angle = 2.0 * np.pi * ((outputs[:, None] * fine[None, :]) % FINE) / FINE
    cosine, sine = np.cos(angle), np.sin(angle)
    return np.block([[cosine, sine], [-sine, cosine]]).T


def twist_table():
    angle = 2.0 * np.pi * (np.arange(RADIX)[:, None] * np.arange(FINE)[None, :]) / (RADIX * FINE)
    return np.stack([np.cos(angle), -np.sin(angle)]).astype(np.float32)


def add(a, b):
    return (a[0] + b[0], a[1] + b[1])


def sub(a, b):
    return (a[0] - b[0], a[1] - b[1])


def turn(a):
    return (a[1], -a[0])


def four(a, b, c, d):
    even, odd = add(a, c), sub(a, c)
    both, rest = add(b, d), turn(sub(b, d))
    return (add(even, both), add(odd, rest), sub(even, both), sub(odd, rest))


def times_root(a, power):
    if power == 0:
        return a
    if power == 4:
        return turn(a)
    half = math.sqrt(0.5)
    if power == 2:
        return ((a[0] + a[1]) * half, (a[1] - a[0]) * half)
    if power == 6:
        return ((a[1] - a[0]) * half, -(a[0] + a[1]) * half)
    cosine, sine = math.cos(2 * math.pi * power / 16), math.sin(2 * math.pi * power / 16)
    return (a[0] * cosine + a[1] * sine, a[1] * cosine - a[0] * sine)


def sixteen(points):
    columns = [four(points[b], points[4 + b], points[8 + b], points[12 + b]) for b in range(4)]
    out = [None] * 16
    for low in range(4):
        mixed = four(*[times_root(columns[b][low], b * low) for b in range(4)])
        for high in range(4):
            out[low + 4 * high] = mixed[high]
    return out


def filter_blocks(plan, fresh, sources, taps_ref, keep_ref, out_ref, begun_ref=None):
    tap_count, length = taps_ref.shape
    inputs = keep_ref.shape[0]
    window, first_later = sources

    def filter_chunk(chunk, _):
        lanes = pl.ds(pl.multiple_of(chunk * LANES, LANES), LANES)
        weights = taps_ref[:, lanes]
        taps = [jnp.broadcast_to(weights[p : p + 1], (inputs, LANES)) for p in range(tap_count)]
        keep = keep_ref[...]
        for comp in range(2):
            sums = {f: [None, None] for f in plan}
            if begun_ref is not None:
                sums = {f: [None, begun_ref[comp, chunk, slot]] for slot, f in enumerate(plan)}
            for v in fresh:
                users = [f for f in plan if f <= v < f + tap_count]
                if not users:
                    continue
                ref, u = window[v]
                at = pl.multiple_of(u * length + chunk * LANES, LANES)
                block = ref[comp, :, pl.ds(at, LANES)].astype(jnp.float32)
                for f in users:
                    later = int(begun_ref is not None or v >= first_later or f < first_later - tap_count + 1)
                    term = taps[v - f] * block
                    held = sums[f][later]
                    sums[f][later] = term if held is None else held + term
            for slot, f in enumerate(plan):
                early, late = sums[f]
                if early is not None:
                    early = early * keep
                    late = early if late is None else late + early
                out_ref[comp, chunk, slot] = late
        return 0

    lax.fori_loop(0, length // LANES, filter_chunk, 0, unroll=4)


def transform(used, slots, twist_ref, table_ref, factor_ref, filt, rows, store):
    inputs = factor_ref.shape[1]

    def first_transform(slot, _):
        for half in range(2):
            points = [(filt[0, 2 * n + half, slot], filt[1, 2 * n + half, slot]) for n in range(RADIX)]
            mixed = sixteen(points)
            for k1 in range(RADIX):
                real, imag = mixed[k1]
                if k1:
                    cosine = twist_ref[0, pl.ds(k1, 1), pl.ds(half * LANES, LANES)]
                    sine = twist_ref[1, pl.ds(k1, 1), pl.ds(half * LANES, LANES)]
                    real, imag = real * cosine - imag * sine, imag * cosine + real * sine
                at = pl.ds(pl.multiple_of((k1 * slots + slot) * inputs, inputs), inputs)
                rows[half, at, :] = real
                rows[2 + half, at, :] = imag
        return 0

    lax.fori_loop(0, used, first_transform, 0, unroll=True)
    for slot in range(used, slots):
        for q in range(4):
            for k1 in range(RADIX):
                at = (k1 * slots + slot) * inputs
                rows[q, at : at + inputs, :] = jnp.zeros((inputs, LANES), jnp.float32)

    some = 8
    count = some * slots * inputs
    for first in range(0, RADIX, some):
        span = slice(first * slots * inputs, first * slots * inputs + count)
        block = jnp.concatenate([rows[q, span, :] for q in range(4)], axis=1)
        high = block.astype(jnp.bfloat16)
        low = (block - high.astype(jnp.float32)).astype(jnp.bfloat16)
        both = jnp.dot(high, table_ref[...], preferred_element_type=jnp.float32)
        rest = jnp.dot(low, table_ref[:, : 2 * KEPT], preferred_element_type=jnp.float32)
        total = both[:, : 2 * KEPT] + both[:, 2 * KEPT :] + rest
        scale = factor_ref[first : first + some][:, None]
        for comp in range(2):
            part = total[:, comp * KEPT : (comp + 1) * KEPT].reshape(some, slots, inputs, KEPT)
            part = jnp.clip(part * scale, -127.0, 127.0)
            store(comp, slice(first, first + some), part.reshape(some, slots * inputs, KEPT))


def split_frames(frames, near, far):
    middle = range(far[0], far[0] + near[0] + near[1])
    return list(middle), [f for f in range(frames) if f not in middle]


def window_of(frames, near, far, refs):
    counts = (far[0], near[0], near[1], frames - near[0] - near[1], near[0], near[1], far[1])
    window = [(ref, u) for ref, count in zip(refs, counts) for u in range(count)]
    return window, far[0] + near[0] + frames


def given(window):
    return [v for v, (ref, _) in enumerate(window) if ref is not None]


def own_kernel(
    frames, near, far, rescale, late_ref, between_ref, early_ref, taps_ref, keep_ref, scales_ref, order_ref, twist_ref,
    middle_ref, outer_ref, factor_ref, wide_taps_ref, same_twist_ref, early_far_ref, late_far_ref,
):
    inputs = scales_ref.shape[0]
    blocks = scales_ref.shape[1] // LANES
    part = LANES // blocks
    values = scales_ref[...].astype(jnp.float32) * rescale
    stacked = jnp.concatenate([values[:, b * LANES : (b + 1) * LANES] for b in range(blocks)], axis=0)
    stacked = jnp.dot(stacked.astype(jnp.bfloat16), order_ref[...], preferred_element_type=jnp.float32)
    held = [stacked[b * inputs : (b + 1) * inputs] for b in range(blocks)]
    lane = lax.broadcasted_iota(jnp.int32, (inputs, LANES), 1)
    bit = 1
    while bit < blocks:
        shift = bit * part
        left = (lane // shift) % 2 == 0
        for b in range(blocks):
            if not b & bit:
                x, y = held[b], held[b | bit]
                held[b] = jnp.where(left, x, pltpu.roll(y, shift, 1))
                held[b | bit] = jnp.where(left, pltpu.roll(x, LANES - shift, 1), y)
        bit *= 2
    for k1 in range(blocks):
        factor_ref[k1] = held[k1]
    wide_taps_ref[...] = taps_ref[...].astype(jnp.float32)
    same_twist_ref[...] = twist_ref[...]
    cut = early_far_ref.shape[2]
    early_far_ref[...] = between_ref[:, :, :cut]
    late_far_ref[...] = between_ref[:, :, cut:]

    own = (early_ref, between_ref, late_ref)
    sources = window_of(frames, near, far, (None, None, *own, None, None))
    for plan, out_ref in zip(split_frames(frames, near, far), (middle_ref, outer_ref)):
        filter_blocks(plan, given(sources[0]), sources, wide_taps_ref, keep_ref, out_ref)


def middle_kernel(
    frames, near, far, before_ref, after_ref, taps_ref, keep_ref, twist_ref, table_ref, factor_ref, begun_ref,
    outer_begun_ref, out_ref, edge_ref, outer_ref, filt, rows,
):
    sources = window_of(frames, near, far, (None, before_ref) + (None,) * 3 + (after_ref, None))
    middle, outer = split_frames(frames, near, far)
    fresh = given(sources[0])
    inputs = factor_ref.shape[1]

    def store(comp, some, part):
        out_ref[comp, some] = part[:, : 8 * inputs]
        edge_ref[comp, some] = part[:, 8 * inputs :]

    filter_blocks(middle, fresh, sources, taps_ref, keep_ref, filt, begun_ref)
    transform(len(middle), len(middle), twist_ref, table_ref, factor_ref, filt, rows, store)
    filter_blocks(outer, fresh, sources, taps_ref, keep_ref, outer_ref, outer_begun_ref)


def outer_kernel(
    frames, near, far, after_ref, before_ref, taps_ref, keep_ref, twist_ref, table_ref, factor_ref, middle_ref,
    edge_ref, begun_ref, out_ref, filt, rows, edge, first_words, second_words,
):
    sources = window_of(frames, near, far, (before_ref,) + (None,) * 5 + (after_ref,))
    middle, plan = split_frames(frames, near, far)
    inputs = factor_ref.shape[1]
    taken = (len(middle) - 8) * inputs
    edge[:, :, :taken] = edge_ref[...]

    def store(comp, some, part):
        edge[comp, some, taken:] = part
        if comp == 1:
            arrange(some.start // 8, (first_words, second_words)[some.start // 8])

    def arrange(pair, words):
        for high in range(2):
            for i in range(inputs):
                parts = []
                for comp in range(2):
                    for channel in range(4):
                        k1 = (pair * 2 + high) * 4 + channel
                        for half in (middle_ref, edge):
                            parts.append(half[comp, k1, pl.ds(i, 8, stride=inputs), :])
                turned = jnp.concatenate(parts, axis=0).T
                words[pl.ds(high * inputs + i, KEPT, stride=2 * inputs), :] = turned
        narrow = words[...].reshape(KEPT, 2 * inputs, LANES).astype(jnp.bfloat16)
        out_ref[:, pair * 2 * inputs : (pair + 1) * 2 * inputs, :] = narrow

    filter_blocks(plan, given(sources[0]), sources, taps_ref, keep_ref, filt, begun_ref)
    transform(len(plan), SLOT - len(middle), twist_ref, table_ref, factor_ref, filt, rows, store)


def split_table():
    table = second_table()
    high = table.astype(jnp.bfloat16)
    low = (table - high.astype(np.float64)).astype(jnp.bfloat16)
    return jnp.concatenate([high, low], axis=1)


def scratch(inputs, slots):
    return [
        pltpu.VMEM((2, RADIX * FINE // LANES, slots, inputs, LANES), jnp.float32),
        pltpu.VMEM((4, RADIX * slots * inputs, LANES), jnp.float32),
    ]


VMEM = pl.BlockSpec(memory_space=pltpu.VMEM)


def sums_shape(count, chunks, inputs):
    return jax.ShapeDtypeStruct((2, chunks, count, inputs, LANES), jnp.float32)


def lane_order():
    part = LANES // RADIX
    order = np.zeros((LANES, LANES))
    for m in range(part):
        for k1 in range(RADIX):
            order[m * RADIX + k1, k1 * part + m] = 1.0
    return order.astype(jnp.bfloat16)


def own_blocks_call(pieces, taps, keep, scales, rescale, frames, near, far):
    inputs = pieces[0].shape[1]
    chunks = taps.shape[1] // LANES
    twist = twist_table()
    middle, outer = split_frames(frames, near, far)
    return pl.pallas_call(
        functools.partial(own_kernel, frames, near, far, rescale),
        out_shape=(
            sums_shape(len(middle), chunks, inputs),
            sums_shape(len(outer), chunks, inputs),
            jax.ShapeDtypeStruct((RADIX, inputs, KEPT), jnp.float32),
            jax.ShapeDtypeStruct(taps.shape, jnp.float32),
            jax.ShapeDtypeStruct(twist.shape, jnp.float32),
            jax.ShapeDtypeStruct((2, inputs, far[1] * taps.shape[1]), pieces[0].dtype),
            jax.ShapeDtypeStruct((2, inputs, far[0] * taps.shape[1]), pieces[0].dtype),
        ),
        in_specs=[VMEM] * 8,
        out_specs=(VMEM,) * 7,
        compiler_params=pltpu.CompilerParams(vmem_limit_bytes=VMEM_LIMIT),
        cost_estimate=pl.CostEstimate(flops=3 * 10**9, bytes_accessed=6 * 2**20, transcendentals=0),
        name="own_blocks",
    )(*pieces, taps, keep, scales, lane_order(), twist)


def middle_frames_call(near_blocks, taps, keep, twist, table, factor, begun, outer_begun, frames, near, far):
    inputs = near_blocks[0].shape[1]
    count = near[0] + near[1]
    return pl.pallas_call(
        functools.partial(middle_kernel, frames, near, far),
        out_shape=(
            jax.ShapeDtypeStruct((2, RADIX, 8 * inputs, KEPT), jnp.float32),
            jax.ShapeDtypeStruct((2, RADIX, (count - 8) * inputs, KEPT), jnp.float32),
            jax.ShapeDtypeStruct(outer_begun.shape, jnp.float32),
        ),
        in_specs=[VMEM] * 9,
        out_specs=(VMEM,) * 3,
        scratch_shapes=scratch(inputs, count),
        compiler_params=pltpu.CompilerParams(vmem_limit_bytes=VMEM_LIMIT),
        cost_estimate=pl.CostEstimate(flops=3 * 10**9, bytes_accessed=5 * 2**20, transcendentals=0),
        name="middle_frames",
    )(*near_blocks, taps, keep, twist, table, factor, begun, outer_begun)


def outer_frames_call(far_blocks, taps, keep, twist, table, factor, middle, edge, begun, frames, near, far):
    inputs = far_blocks[0].shape[1]
    return pl.pallas_call(
        functools.partial(outer_kernel, frames, near, far),
        out_shape=jax.ShapeDtypeStruct((KEPT, 4 * inputs, LANES), jnp.bfloat16),
        in_specs=[VMEM] * 10,
        out_specs=VMEM,
        scratch_shapes=scratch(inputs, SLOT - near[0] - near[1])
        + [pltpu.VMEM((2, RADIX, 8 * inputs, KEPT), jnp.float32)]
        + [pltpu.VMEM((KEPT * 2 * inputs, LANES), jnp.float32)] * 2,
        compiler_params=pltpu.CompilerParams(vmem_limit_bytes=VMEM_LIMIT),
        name="outer_frames",
    )(*far_blocks, taps, keep, twist, table, factor, middle, edge, begun)


def cut_kernel(spans, in_ref, *refs):
    outs, sems = refs[:-1], refs[-1]
    copies = [
        pltpu.make_async_copy(in_ref.at[:, :, start:stop], out, sems.at[i])
        for i, ((start, stop), out) in enumerate(zip(spans, outs))
    ]
    for copy in copies:
        copy.start()
    for copy in copies:
        copy.wait()


def cut_pieces(samples, near, frames, length):
    spans = [((frames - near[0]) * length, frames * length), (0, near[1] * length)]
    late, early = pl.pallas_call(
        functools.partial(cut_kernel, spans),
        out_shape=[jax.ShapeDtypeStruct(samples.shape[:2] + (b - a,), samples.dtype) for a, b in spans],
        in_specs=[pl.BlockSpec(memory_space=pltpu.HBM)],
        out_specs=[VMEM] * 2,
        scratch_shapes=[pltpu.SemaphoreType.DMA((2,))],
        compiler_params=pltpu.CompilerParams(vmem_limit_bytes=VMEM_LIMIT),
        name="cut",
    )(pltpu.with_memory_space_constraint(samples, pltpu.HBM))
    return late, early, lax.slice_in_dim(samples, spans[1][1], spans[0][0], axis=2)


def correlate_kernel(normalizer, words_ref, out_ref, joined, swapped, result, sems):
    stations, times, inputs, _ = words_ref.shape
    size = stations * inputs
    half = size // 2

    lane = lax.broadcasted_iota(jnp.int32, (size, LANES), 1)
    sign = jnp.where(lane < LANES // 2, 1.0, -1.0).astype(jnp.bfloat16)

    for q in range(times // 4):
        held = [words_ref[:, 4 * q + r].astype(jnp.float32).reshape(size, LANES).astype(jnp.bfloat16) for r in range(4)]
        for bit in (1, 2):
            shift = bit * SLOT
            left = (lane // shift) % 2 == 0
            for r in range(4):
                if not r & bit:
                    x, y = held[r], held[r | bit]
                    held[r] = jnp.where(left, x, pltpu.roll(y, shift, 1))
                    held[r | bit] = jnp.where(left, pltpu.roll(x, LANES - shift, 1), y)
        for c in range(4):
            lanes = slice(q * LANES, (q + 1) * LANES)
            joined[c, :, lanes] = held[c]
            swapped[c, :, lanes] = pltpu.roll(held[c], LANES // 2, 1) * sign

    def product(left, right):
        return lax.dot_general(
            left, right, (((1,), (1,)), ((), ())), preferred_element_type=jnp.float32
        )

    def finish(values):
        return (values * normalizer).astype(jnp.bfloat16)

    lower = lax.broadcasted_iota(jnp.int32, (half, half), 0) >= lax.broadcasted_iota(
        jnp.int32, (half, half), 1
    )
    copies = []
    for channel in range(4):
        first, second = joined[channel, :half], joined[channel, half:]
        first_other, second_other = swapped[channel, :half], swapped[channel, half:]
        result[channel, :half, :half] = finish(jnp.where(lower, product(first, first), product(first_other, first)))
        result[channel, half:, :half] = finish(product(second, first))
        result[channel, :half, half:] = finish(product(first_other, second))
        result[channel, half:, half:] = finish(
            jnp.where(lower, product(second, second), product(second_other, second))
        )
        copies.append(pltpu.make_async_copy(result.at[channel], out_ref.at[channel], sems.at[channel]))
        copies[-1].start()
    for copy in copies:
        copy.wait()


def correlate(words, normalizer):
    stations, times, inputs, _ = words.shape
    size = stations * inputs
    return pl.pallas_call(
        functools.partial(correlate_kernel, normalizer),
        out_shape=jax.ShapeDtypeStruct((4, size, size), jnp.bfloat16),
        in_specs=[VMEM],
        out_specs=pl.BlockSpec(memory_space=pltpu.HBM),
        scratch_shapes=[pltpu.VMEM((4, size, times * 2 * SLOT), jnp.bfloat16)] * 2
        + [pltpu.VMEM((4, size, size), jnp.bfloat16), pltpu.SemaphoreType.DMA((4,))],
        compiler_params=pltpu.CompilerParams(vmem_limit_bytes=VMEM_LIMIT),
        name="correlate",
    )(words)


def body(samples, taps, scales):
    length = taps.shape[1]
    inputs = samples.shape[1]
    frames = samples.shape[2] // length
    stations, times = lax.axis_size("stn"), lax.axis_size("tm")
    near, far = (5, 5), (3, 2)
    onward = [(i, i + 1) for i in range(times - 1)]
    backward = [(i, (i - 1) % times) for i in range(times)]

    late, early, between = cut_pieces(samples, near, frames, length)
    before = lax.ppermute(late, "tm", onward)
    after = lax.ppermute(early, "tm", backward)
    pieces = (late, between, early)
    keep = jnp.where(lax.axis_index("tm") == times - 1, 0.0, 1.0)
    keep = jnp.broadcast_to(keep.astype(jnp.float32), (inputs, LANES))
    table = split_table()
    rescale = 16.0 / math.sqrt(length)
    begun, outer_begun, factor, wide_taps, twist, early_far, late_far = own_blocks_call(
        pieces, taps, keep, scales, rescale, frames, near, far
    )
    far_after = lax.ppermute(early_far, "tm", backward)
    far_before = lax.ppermute(late_far, "tm", onward)
    middle, edge, outer_begun = middle_frames_call(
        (before, after), wide_taps, keep, twist, table, factor, begun, outer_begun, frames, near, far
    )
    words = outer_frames_call(
        (far_after, far_before), wide_taps, keep, twist, table, factor, middle, edge, outer_begun, frames, near, far
    )
    words = words.reshape(stations * times, inputs, LANES)
    words = lax.all_to_all(words, ("stn", "tm"), split_axis=0, concat_axis=0, tiled=True)
    words = words.reshape(stations, times, inputs, LANES)
    return correlate(words, 1.0 / (2.0 * frames * times * length))


def solution(mesh):
    placed = (P(None, "stn", "tm"), P(), P("stn", None))
    return jax.shard_map(
        body, mesh=mesh, in_specs=placed, out_specs=P(("stn", "tm"), None, None), check_vma=False
    )
```

```python
import functools
import math

import jax
import jax.numpy as jnp
import numpy as np
from jax import lax
from jax.experimental import pallas as pl
from jax.experimental.pallas import tpu as pltpu
from jax.sharding import PartitionSpec as P

LANES = 128
RADIX = 16
FINE = 256
KEPT = 128
SLOT = 16
VMEM_LIMIT = 28 * 2**20


def second_table():
    fine = np.arange(FINE)
    outputs = np.arange(KEPT) + (FINE - KEPT) // 2
    angle = 2.0 * np.pi * ((outputs[:, None] * fine[None, :]) % FINE) / FINE
    cosine, sine = np.cos(angle), np.sin(angle)
    return np.block([[cosine, sine], [-sine, cosine]]).T


def twist_table():
    angle = 2.0 * np.pi * (np.arange(RADIX)[:, None] * np.arange(FINE)[None, :]) / (RADIX * FINE)
    return np.stack([np.cos(angle), -np.sin(angle)]).astype(np.float32)


def add(a, b):
    return (a[0] + b[0], a[1] + b[1])


def sub(a, b):
    return (a[0] - b[0], a[1] - b[1])


def turn(a):
    return (a[1], -a[0])


def four(a, b, c, d):
    even, odd = add(a, c), sub(a, c)
    both, rest = add(b, d), turn(sub(b, d))
    return (add(even, both), add(odd, rest), sub(even, both), sub(odd, rest))


def times_root(a, power):
    if power == 0:
        return a
    if power == 4:
        return turn(a)
    half = math.sqrt(0.5)
    if power == 2:
        return ((a[0] + a[1]) * half, (a[1] - a[0]) * half)
    if power == 6:
        return ((a[1] - a[0]) * half, -(a[0] + a[1]) * half)
    cosine, sine = math.cos(2 * math.pi * power / 16), math.sin(2 * math.pi * power / 16)
    return (a[0] * cosine + a[1] * sine, a[1] * cosine - a[0] * sine)


def sixteen(points):
    columns = [four(points[b], points[4 + b], points[8 + b], points[12 + b]) for b in range(4)]
    out = [None] * 16
    for low in range(4):
        mixed = four(*[times_root(columns[b][low], b * low) for b in range(4)])
        for high in range(4):
            out[low + 4 * high] = mixed[high]
    return out


def filter_blocks(plan, fresh, sources, taps_ref, keep_ref, out_ref, begun_ref=None):
    tap_count, length = taps_ref.shape
    inputs = keep_ref.shape[0]
    window, first_later = sources

    def filter_chunk(chunk, _):
        lanes = pl.ds(pl.multiple_of(chunk * LANES, LANES), LANES)
        weights = taps_ref[:, lanes]
        taps = [jnp.broadcast_to(weights[p : p + 1], (inputs, LANES)) for p in range(tap_count)]
        keep = keep_ref[...]
        for comp in range(2):
            sums = {f: [None, None] for f in plan}
            if begun_ref is not None:
                sums = {f: [None, begun_ref[comp, chunk, slot]] for slot, f in enumerate(plan)}
            for v in fresh:
                users = [f for f in plan if f <= v < f + tap_count]
                if not users:
                    continue
                ref, u = window[v]
                at = pl.multiple_of(u * length + chunk * LANES, LANES)
                block = ref[comp, :, pl.ds(at, LANES)].astype(jnp.float32)
                for f in users:
                    later = int(begun_ref is not None or v >= first_later or f < first_later - tap_count + 1)
                    term = taps[v - f] * block
                    held = sums[f][later]
                    sums[f][later] = term if held is None else held + term
            for slot, f in enumerate(plan):
                early, late = sums[f]
                if early is not None:
                    early = early * keep
                    late = early if late is None else late + early
                out_ref[comp, chunk, slot] = late
        return 0

    lax.fori_loop(0, length // LANES, filter_chunk, 0, unroll=4)


def transform(used, slots, twist_ref, table_ref, factor_ref, filt, rows, store):
    inputs = factor_ref.shape[1]

    def first_transform(slot, _):
        for half in range(2):
            points = [(filt[0, 2 * n + half, slot], filt[1, 2 * n + half, slot]) for n in range(RADIX)]
            mixed = sixteen(points)
            for k1 in range(RADIX):
                real, imag = mixed[k1]
                if k1:
                    cosine = twist_ref[0, pl.ds(k1, 1), pl.ds(half * LANES, LANES)]
                    sine = twist_ref[1, pl.ds(k1, 1), pl.ds(half * LANES, LANES)]
                    real, imag = real * cosine - imag * sine, imag * cosine + real * sine
                at = pl.ds(pl.multiple_of((k1 * slots + slot) * inputs, inputs), inputs)
                rows[half, at, :] = real
                rows[2 + half, at, :] = imag
        return 0

    lax.fori_loop(0, used, first_transform, 0, unroll=True)
    for slot in range(used, slots):
        for q in range(4):
            for k1 in range(RADIX):
                at = (k1 * slots + slot) * inputs
                rows[q, at : at + inputs, :] = jnp.zeros((inputs, LANES), jnp.float32)

    some = 8
    count = some * slots * inputs
    for first in range(0, RADIX, some):
        span = slice(first * slots * inputs, first * slots * inputs + count)
        block = jnp.concatenate([rows[q, span, :] for q in range(4)], axis=1)
        high = block.astype(jnp.bfloat16)
        low = (block - high.astype(jnp.float32)).astype(jnp.bfloat16)
        both = jnp.dot(high, table_ref[...], preferred_element_type=jnp.float32)
        rest = jnp.dot(low, table_ref[:, : 2 * KEPT], preferred_element_type=jnp.float32)
        total = both[:, : 2 * KEPT] + both[:, 2 * KEPT :] + rest
        scale = factor_ref[first : first + some][:, None]
        for comp in range(2):
            part = total[:, comp * KEPT : (comp + 1) * KEPT].reshape(some, slots, inputs, KEPT)
            part = jnp.clip(part * scale, -127.0, 127.0)
            store(comp, slice(first, first + some), part.reshape(some, slots * inputs, KEPT))


def split_frames(frames, near, far):
    middle = range(far[0], far[0] + near[0] + near[1])
    return list(middle), [f for f in range(frames) if f not in middle]


def window_of(frames, near, far, refs):
    counts = (far[0], near[0], near[1], frames - near[0] - near[1], near[0], near[1], far[1])
    window = [(ref, u) for ref, count in zip(refs, counts) for u in range(count)]
    return window, far[0] + near[0] + frames


def given(window):
    return [v for v, (ref, _) in enumerate(window) if ref is not None]


def own_kernel(
    frames, near, far, rescale, late_ref, between_ref, early_ref, taps_ref, keep_ref, scales_ref, order_ref, twist_ref,
    middle_ref, outer_ref, factor_ref, wide_taps_ref, same_twist_ref, early_far_ref, late_far_ref,
):
    inputs = scales_ref.shape[0]
    blocks = scales_ref.shape[1] // LANES
    part = LANES // blocks
    values = scales_ref[...].astype(jnp.float32) * rescale
    stacked = jnp.concatenate([values[:, b * LANES : (b + 1) * LANES] for b in range(blocks)], axis=0)
    stacked = jnp.dot(stacked.astype(jnp.bfloat16), order_ref[...], preferred_element_type=jnp.float32)
    held = [stacked[b * inputs : (b + 1) * inputs] for b in range(blocks)]
    lane = lax.broadcasted_iota(jnp.int32, (inputs, LANES), 1)
    bit = 1
    while bit < blocks:
        shift = bit * part
        left = (lane // shift) % 2 == 0
        for b in range(blocks):
            if not b & bit:
                x, y = held[b], held[b | bit]
                held[b] = jnp.where(left, x, pltpu.roll(y, shift, 1))
                held[b | bit] = jnp.where(left, pltpu.roll(x, LANES - shift, 1), y)
        bit *= 2
    for k1 in range(blocks):
        factor_ref[k1] = held[k1]
    wide_taps_ref[...] = taps_ref[...].astype(jnp.float32)
    same_twist_ref[...] = twist_ref[...]
    cut = early_far_ref.shape[2]
    early_far_ref[...] = between_ref[:, :, :cut]
    late_far_ref[...] = between_ref[:, :, cut:]

    own = (early_ref, between_ref, late_ref)
    sources = window_of(frames, near, far, (None, None, *own, None, None))
    for plan, out_ref in zip(split_frames(frames, near, far), (middle_ref, outer_ref)):
        filter_blocks(plan, given(sources[0]), sources, wide_taps_ref, keep_ref, out_ref)


def middle_kernel(
    frames, near, far, before_ref, after_ref, taps_ref, keep_ref, twist_ref, table_ref, factor_ref, begun_ref,
    outer_begun_ref, out_ref, edge_ref, outer_ref, filt, rows,
):
    sources = window_of(frames, near, far, (None, before_ref) + (None,) * 3 + (after_ref, None))
    middle, outer = split_frames(frames, near, far)
    fresh = given(sources[0])
    inputs = factor_ref.shape[1]

    def store(comp, some, part):
        out_ref[comp, some] = part[:, : 8 * inputs]
        edge_ref[comp, some] = part[:, 8 * inputs :]

    filter_blocks(middle, fresh, sources, taps_ref, keep_ref, filt, begun_ref)
    transform(len(middle), len(middle), twist_ref, table_ref, factor_ref, filt, rows, store)
    filter_blocks(outer, fresh, sources, taps_ref, keep_ref, outer_ref, outer_begun_ref)


def outer_kernel(
    frames, near, far, after_ref, before_ref, taps_ref, keep_ref, twist_ref, table_ref, factor_ref, middle_ref,
    edge_ref, begun_ref, out_ref, filt, rows, edge, first_words, second_words,
):
    sources = window_of(frames, near, far, (before_ref,) + (None,) * 5 + (after_ref,))
    middle, plan = split_frames(frames, near, far)
    inputs = factor_ref.shape[1]
    taken = (len(middle) - 8) * inputs
    edge[:, :, :taken] = edge_ref[...]

    def store(comp, some, part):
        edge[comp, some, taken:] = part
        if comp == 1:
            arrange(some.start // 8, (first_words, second_words)[some.start // 8])

    def arrange(pair, words):
        for high in range(2):
            for i in range(inputs):
                parts = []
                for comp in range(2):
                    for channel in range(4):
                        k1 = (pair * 2 + high) * 4 + channel
                        for half in (middle_ref, edge):
                            parts.append(half[comp, k1, pl.ds(i, 8, stride=inputs), :])
                turned = jnp.concatenate(parts, axis=0).T
                words[pl.ds(high * inputs + i, KEPT, stride=2 * inputs), :] = turned
        narrow = words[...].reshape(KEPT, 2 * inputs, LANES).astype(jnp.bfloat16)
        out_ref[:, pair * 2 * inputs : (pair + 1) * 2 * inputs, :] = narrow

    filter_blocks(plan, given(sources[0]), sources, taps_ref, keep_ref, filt, begun_ref)
    transform(len(plan), SLOT - len(middle), twist_ref, table_ref, factor_ref, filt, rows, store)


def split_table():
    table = second_table()
    high = table.astype(jnp.bfloat16)
    low = (table - high.astype(np.float64)).astype(jnp.bfloat16)
    return jnp.concatenate([high, low], axis=1)


def scratch(inputs, slots):
    return [
        pltpu.VMEM((2, RADIX * FINE // LANES, slots, inputs, LANES), jnp.float32),
        pltpu.VMEM((4, RADIX * slots * inputs, LANES), jnp.float32),
    ]


VMEM = pl.BlockSpec(memory_space=pltpu.VMEM)


def sums_shape(count, chunks, inputs):
    return jax.ShapeDtypeStruct((2, chunks, count, inputs, LANES), jnp.float32)


def lane_order():
    part = LANES // RADIX
    order = np.zeros((LANES, LANES))
    for m in range(part):
        for k1 in range(RADIX):
            order[m * RADIX + k1, k1 * part + m] = 1.0
    return order.astype(jnp.bfloat16)


def own_blocks_call(pieces, taps, keep, scales, rescale, frames, near, far):
    inputs = pieces[0].shape[1]
    chunks = taps.shape[1] // LANES
    twist = twist_table()
    middle, outer = split_frames(frames, near, far)
    return pl.pallas_call(
        functools.partial(own_kernel, frames, near, far, rescale),
        out_shape=(
            sums_shape(len(middle), chunks, inputs),
            sums_shape(len(outer), chunks, inputs),
            jax.ShapeDtypeStruct((RADIX, inputs, KEPT), jnp.float32),
            jax.ShapeDtypeStruct(taps.shape, jnp.float32),
            jax.ShapeDtypeStruct(twist.shape, jnp.float32),
            jax.ShapeDtypeStruct((2, inputs, far[1] * taps.shape[1]), pieces[0].dtype),
            jax.ShapeDtypeStruct((2, inputs, far[0] * taps.shape[1]), pieces[0].dtype),
        ),
        in_specs=[VMEM] * 8,
        out_specs=(VMEM,) * 7,
        compiler_params=pltpu.CompilerParams(vmem_limit_bytes=VMEM_LIMIT),
        cost_estimate=pl.CostEstimate(flops=3 * 10**9, bytes_accessed=6 * 2**20, transcendentals=0),
        name="own_blocks",
    )(*pieces, taps, keep, scales, lane_order(), twist)


def middle_frames_call(near_blocks, taps, keep, twist, table, factor, begun, outer_begun, frames, near, far):
    inputs = near_blocks[0].shape[1]
    count = near[0] + near[1]
    return pl.pallas_call(
        functools.partial(middle_kernel, frames, near, far),
        out_shape=(
            jax.ShapeDtypeStruct((2, RADIX, 8 * inputs, KEPT), jnp.float32),
            jax.ShapeDtypeStruct((2, RADIX, (count - 8) * inputs, KEPT), jnp.float32),
            jax.ShapeDtypeStruct(outer_begun.shape, jnp.float32),
        ),
        in_specs=[VMEM] * 9,
        out_specs=(VMEM,) * 3,
        scratch_shapes=scratch(inputs, count),
        compiler_params=pltpu.CompilerParams(vmem_limit_bytes=VMEM_LIMIT),
        cost_estimate=pl.CostEstimate(flops=3 * 10**9, bytes_accessed=5 * 2**20, transcendentals=0),
        name="middle_frames",
    )(*near_blocks, taps, keep, twist, table, factor, begun, outer_begun)


def outer_frames_call(far_blocks, taps, keep, twist, table, factor, middle, edge, begun, frames, near, far):
    inputs = far_blocks[0].shape[1]
    return pl.pallas_call(
        functools.partial(outer_kernel, frames, near, far),
        out_shape=jax.ShapeDtypeStruct((KEPT, 4 * inputs, LANES), jnp.bfloat16),
        in_specs=[VMEM] * 10,
        out_specs=VMEM,
        scratch_shapes=scratch(inputs, SLOT - near[0] - near[1])
        + [pltpu.VMEM((2, RADIX, 8 * inputs, KEPT), jnp.float32)]
        + [pltpu.VMEM((KEPT * 2 * inputs, LANES), jnp.float32)] * 2,
        compiler_params=pltpu.CompilerParams(vmem_limit_bytes=VMEM_LIMIT),
        name="outer_frames",
    )(*far_blocks, taps, keep, twist, table, factor, middle, edge, begun)


def cut_kernel(spans, in_ref, *refs):
    outs, sems = refs[:-1], refs[-1]
    copies = [
        pltpu.make_async_copy(in_ref.at[:, :, start:stop], out, sems.at[i])
        for i, ((start, stop), out) in enumerate(zip(spans, outs))
    ]
    for copy in copies:
        copy.start()
    for copy in copies:
        copy.wait()


def cut_pieces(samples, near, frames, length):
    spans = [((frames - near[0]) * length, frames * length), (0, near[1] * length)]
    late, early = pl.pallas_call(
        functools.partial(cut_kernel, spans),
        out_shape=[jax.ShapeDtypeStruct(samples.shape[:2] + (b - a,), samples.dtype) for a, b in spans],
        in_specs=[pl.BlockSpec(memory_space=pltpu.HBM)],
        out_specs=[VMEM] * 2,
        scratch_shapes=[pltpu.SemaphoreType.DMA((2,))],
        compiler_params=pltpu.CompilerParams(vmem_limit_bytes=VMEM_LIMIT),
        name="cut",
    )(pltpu.with_memory_space_constraint(samples, pltpu.HBM))
    return late, early, lax.slice_in_dim(samples, spans[1][1], spans[0][0], axis=2)


def correlate_kernel(normalizer, words_ref, out_ref, joined, swapped, result, sems):
    stations, times, inputs, _ = words_ref.shape
    size = stations * inputs
    half = size // 2

    lane = lax.broadcasted_iota(jnp.int32, (size, LANES), 1)
    sign = jnp.where(lane < LANES // 2, 1.0, -1.0).astype(jnp.bfloat16)

    for q in range(times // 4):
        held = [words_ref[:, 4 * q + r].astype(jnp.float32).reshape(size, LANES).astype(jnp.bfloat16) for r in range(4)]
        for bit in (1, 2):
            shift = bit * SLOT
            left = (lane // shift) % 2 == 0
            for r in range(4):
                if not r & bit:
                    x, y = held[r], held[r | bit]
                    held[r] = jnp.where(left, x, pltpu.roll(y, shift, 1))
                    held[r | bit] = jnp.where(left, pltpu.roll(x, LANES - shift, 1), y)
        for c in range(4):
            lanes = slice(q * LANES, (q + 1) * LANES)
            joined[c, :, lanes] = held[c]
            swapped[c, :, lanes] = pltpu.roll(held[c], LANES // 2, 1) * sign

    def product(left, right):
        return lax.dot_general(
            left, right, (((1,), (1,)), ((), ())), preferred_element_type=jnp.float32
        )

    def finish(values):
        return (values * normalizer).astype(jnp.bfloat16)

    lower = lax.broadcasted_iota(jnp.int32, (half, half), 0) >= lax.broadcasted_iota(
        jnp.int32, (half, half), 1
    )
    copies = []
    for channel in range(4):
        first, second = joined[channel, :half], joined[channel, half:]
        first_other, second_other = swapped[channel, :half], swapped[channel, half:]
        result[channel, :half, :half] = finish(jnp.where(lower, product(first, first), product(first_other, first)))
        result[channel, half:, :half] = finish(product(second, first))
        result[channel, :half, half:] = finish(product(first_other, second))
        result[channel, half:, half:] = finish(
            jnp.where(lower, product(second, second), product(second_other, second))
        )
        copies.append(pltpu.make_async_copy(result.at[channel], out_ref.at[channel], sems.at[channel]))
        copies[-1].start()
    for copy in copies:
        copy.wait()


def correlate(words, normalizer):
    stations, times, inputs, _ = words.shape
    size = stations * inputs
    return pl.pallas_call(
        functools.partial(correlate_kernel, normalizer),
        out_shape=jax.ShapeDtypeStruct((4, size, size), jnp.bfloat16),
        in_specs=[VMEM],
        out_specs=pl.BlockSpec(memory_space=pltpu.HBM),
        scratch_shapes=[pltpu.VMEM((4, size, times * 2 * SLOT), jnp.bfloat16)] * 2
        + [pltpu.VMEM((4, size, size), jnp.bfloat16), pltpu.SemaphoreType.DMA((4,))],
        compiler_params=pltpu.CompilerParams(vmem_limit_bytes=VMEM_LIMIT),
        name="correlate",
    )(words)


def body(samples, taps, scales):
    length = taps.shape[1]
    inputs = samples.shape[1]
    frames = samples.shape[2] // length
    stations, times = lax.axis_size("stn"), lax.axis_size("tm")
    near, far = (6, 5), (2, 2)
    onward = [(i, i + 1) for i in range(times - 1)]
    backward = [(i, (i - 1) % times) for i in range(times)]

    late, early, between = cut_pieces(samples, near, frames, length)
    before = lax.ppermute(late, "tm", onward)
    after = lax.ppermute(early, "tm", backward)
    pieces = (late, between, early)
    keep = jnp.where(lax.axis_index("tm") == times - 1, 0.0, 1.0)
    keep = jnp.broadcast_to(keep.astype(jnp.float32), (inputs, LANES))
    table = split_table()
    rescale = 16.0 / math.sqrt(length)
    begun, outer_begun, factor, wide_taps, twist, early_far, late_far = own_blocks_call(
        pieces, taps, keep, scales, rescale, frames, near, far
    )
    far_after = lax.ppermute(early_far, "tm", backward)
    far_before = lax.ppermute(late_far, "tm", onward)
    middle, edge, outer_begun = middle_frames_call(
        (before, after), wide_taps, keep, twist, table, factor, begun, outer_begun, frames, near, far
    )
    words = outer_frames_call(
        (far_after, far_before), wide_taps, keep, twist, table, factor, middle, edge, outer_begun, frames, near, far
    )
    words = words.reshape(stations * times, inputs, LANES)
    words = lax.all_to_all(words, ("stn", "tm"), split_axis=0, concat_axis=0, tiled=True)
    words = words.reshape(stations, times, inputs, LANES)
    return correlate(words, 1.0 / (2.0 * frames * times * length))


def solution(mesh):
    placed = (P(None, "stn", "tm"), P(), P("stn", None))
    return jax.shard_map(
        body, mesh=mesh, in_specs=placed, out_specs=P(("stn", "tm"), None, None), check_vma=False
    )
```
